256 devices in a mesh: dp: 128 (over x, y, z_hi, core), tp: 2 (over z_lo).
Axes of the slice: x: 4, y: 4, z: 8 (z_hi: 4, z_lo: 2; z = z_hi * 2 + z_lo), core: 2. Of those that a mesh axis runs over, the one named last changes fastest.
Arguments:
- tokens: bfloat16 [256, 512, 768], P('dp', 'tp'), may hold values from -6 to 6
- eval_tokens: bfloat16 [256, 512, 768], P('dp', 'tp'), may hold values from -6 to 6
- cotangent: bfloat16 [256, 512, 768], P('dp', 'tp'), may hold values from -6 to 6
- lengths: int32 [256], P('dp'), may hold values from 1 to 512, as said below
- w_query: bfloat16 [768, 768], P(('dp', 'tp')), may hold values from -0.21875 to 0.21875
- w_key: bfloat16 [768, 768], P(('dp', 'tp')), may hold values from -0.21875 to 0.21875
- w_value: bfloat16 [768, 768], P(('dp', 'tp')), may hold values from -0.21875 to 0.21875
- w_out: bfloat16 [768, 768], P(('dp', 'tp')), may hold values from -3.5 to 3.5
- w_up: bfloat16 [768, 3072], P('dp', 'tp'), may hold values from -0.21875 to 0.21875
- w_down: bfloat16 [3072, 768], P('tp', 'dp'), may hold values from -0.109375 to 0.109375
- a_query: bfloat16 [768, 8], P(('dp', 'tp')), may hold values from -0.21875 to 0.21875
- a_value: bfloat16 [768, 8], P(('dp', 'tp')), may hold values from -0.21875 to 0.21875
- query_up_weight: bfloat16 [8, 768], replicated, may hold values from -0.59765625 to 0.59765625
- value_up_weight: bfloat16 [8, 768], replicated, may hold values from -0.59765625 to 0.59765625
- query_bias_vector: bfloat16 [768], replicated, may hold values from -1.796875 to 1.796875
- value_bias_vector: bfloat16 [768], replicated, may hold values from -0.29882812 to 0.29882812
- bias_out: bfloat16 [768], replicated, may hold values from -1.796875 to 1.796875
- bias_up: bfloat16 [3072], replicated, may hold values from -1.796875 to 1.796875
- bias_down: bfloat16 [768], replicated, may hold values from -1.796875 to 1.796875
- gain_one: bfloat16 [768], replicated, may hold values from 0.5 to 1.5
- shift_one: bfloat16 [768], replicated, may hold values from -1.796875 to 1.796875
- gain_two: bfloat16 [768], replicated, may hold values from 0.5 to 1.5
- shift_two: bfloat16 [768], replicated, may hold values from -1.796875 to 1.796875
Outputs:
- activations: bfloat16 [256, 512, 768], P('dp', 'tp')
- input_grad: float32 [256, 512, 768], P('dp', 'tp')
- grad_b_query: float32 [8, 768], replicated
- grad_b_value: float32 [8, 768], replicated
- eval_output: bfloat16 [256, 512, 768], P('dp', 'tp')
The draws below stay inside these ranges and needn't reach their ends.
Inputs may be any that keep to these rules, and one draw needn't show every extreme that they name: `lengths`: of the 2 items of each index of dp (items k * 2 to k * 2 + 1), at least one has length 512; the others are drawn evenly.
All inputs are finite; a program needn't handle non-finite values.
Results may differ from the reference program's by a relative error of at most 0.015.
Values may be sent and summed in bfloat16 or wider, within the bound.
A program may use at most 128 MiB of HBM per device.

```python
import math
import jax
import jax.numpy as jnp
from jax import lax

D = 768
HEADS = 12
FF = 3072
RANK = 8
SEQ = 512
ITEMS = 2
ITEMS_ALL = 256


def draw_lengths(key, part):
    key = jax.random.fold_in(key, 11)
    key_lengths, key_pick = jax.random.split(key)
    drawn = jax.random.randint(key_lengths, (ITEMS_ALL,), 1, SEQ + 1)
    picked = jax.random.randint(key_pick, (ITEMS_ALL // ITEMS,), 0, ITEMS)
    slot_index = jnp.arange(ITEMS_ALL, dtype=jnp.int32) % ITEMS
    longest = slot_index == jnp.repeat(picked, ITEMS, total_repeat_length=ITEMS_ALL)
    return jnp.where(longest, SEQ, drawn).astype(jnp.int32)


def steps_of(rng, extent, shards, low, largest):
    def one(position, shards_of):
        heights = jax.random.uniform(jax.random.fold_in(jax.random.fold_in(rng, 6), position), (shards_of,), jnp.float32, low / len(shards), largest / len(shards))
        return jnp.repeat(jnp.exp(heights), extent[position] // shards_of).reshape((-1,) + (1,) * (len(extent) - position - 1))

    gain = one(*shards[0])
    for cut in shards[1:]:
        gain = gain * one(*cut)
    return gain


def scatter_about(own_key, shape, scale, reach, cuts=(), held_as=jnp.bfloat16):
    factor_of = steps_of(own_key, shape, cuts, -0.22, 0.18) if cuts else 1.0
    array = jax.random.normal(own_key, shape, jnp.float32) * scale * factor_of
    return jnp.minimum(jnp.maximum(array, -reach), reach).astype(held_as)


def setup_inputs(seed: int = 0) -> dict:
    keys = jax.random.split(jax.random.key(seed), 24)
    return {
        "tokens": scatter_about(keys[0], (ITEMS_ALL, SEQ, D), 1.0, 6.0, ((0, 128), (1, 2))),
        "eval_tokens": scatter_about(keys[1], (ITEMS_ALL, SEQ, D), 1.0, 6.0, ((0, 128), (1, 2))),
        "cotangent": scatter_about(keys[2], (ITEMS_ALL, SEQ, D), 1.0, 6.0, ((0, 128), (1, 2))),
        "lengths": draw_lengths(jax.random.fold_in(keys[23], 71), 0),
        "w_query": scatter_about(keys[4], (D, D), D ** -0.5, 0.21875, ((0, 256),)),
        "w_key": scatter_about(keys[5], (D, D), D ** -0.5, 0.21875, ((0, 256),)),
        "w_value": scatter_about(keys[6], (D, D), D ** -0.5, 0.21875, ((0, 256),)),
        "w_out": scatter_about(keys[7], (D, D), (2 * D // SEQ) ** -0.5, 3.5, ((0, 256),)),
        "w_up": scatter_about(keys[8], (D, FF), D ** -0.5, 0.21875, ((0, 128), (1, 2))),
        "w_down": scatter_about(keys[9], (FF, D), FF ** -0.5, 0.109375, ((0, 2), (1, 128))),
        "a_query": scatter_about(keys[10], (D, RANK), D ** -0.5, 0.21875, ((0, 256),)),
        "a_value": scatter_about(keys[11], (D, RANK), D ** -0.5, 0.21875, ((0, 256),)),
        "query_up_weight": scatter_about(keys[12], (RANK, D), 0.1, 0.59765625),
        "value_up_weight": scatter_about(keys[13], (RANK, D), 0.1, 0.59765625),
        "query_bias_vector": scatter_about(keys[14], (D,), 0.3, 1.796875),
        "value_bias_vector": scatter_about(keys[15], (D,), 0.05, 0.29882812),
        "bias_out": scatter_about(keys[16], (D,), 0.3, 1.796875),
        "bias_up": scatter_about(keys[17], (FF,), 0.3, 1.796875),
        "bias_down": scatter_about(keys[18], (D,), 0.3, 1.796875),
        "gain_one": jnp.clip(1.0 + 0.1 * jax.random.normal(keys[19], (D,), jnp.float32), 0.5, 1.5).astype(jnp.bfloat16),
        "shift_one": scatter_about(keys[20], (D,), 0.3, 1.796875),
        "gain_two": jnp.clip(1.0 + 0.1 * jax.random.normal(keys[21], (D,), jnp.float32), 0.5, 1.5).astype(jnp.bfloat16),
        "shift_two": scatter_about(keys[22], (D,), 0.3, 1.796875),
    }


EPSILON = 1e-05
HIGHEST = lax.Precision.HIGHEST

@jax.custom_vjp
def low_rank_part(v):
    return lax.optimization_barrier(v.astype(jnp.bfloat16)).astype(jnp.float32)

@jax.custom_vjp
def low_back(v):
    return v

def low_keep(v):
    return (low_rank_part(v), None)

def low_pass(kept, grad):
    return (grad,)

def back_keep(v):
    return (v, None)

def back_low(kept, grad):
    return (low_rank_part(grad),)
low_rank_part.defvjp(low_keep, low_pass)
low_back.defvjp(back_keep, back_low)

def matrix_product(left, right):
    return jnp.dot(left, right, precision=HIGHEST)

def norm_rows(matrix_rows, gain_vec, shift_vec):
    row_mean = lax.optimization_barrier(jnp.mean(matrix_rows, axis=-1, keepdims=True))
    centred = matrix_rows - row_mean
    spread = lax.optimization_barrier(jnp.mean(centred * centred, axis=-1, keepdims=True))
    return centred * lax.rsqrt(spread + EPSILON) * gain_vec + shift_vec

def attend(query_low, key_low, value_low, key_mask_valid):
    lead_count, seq_len, model_width = query_low.shape
    head_size = model_width // HEADS
    query_heads = query_low.reshape(lead_count, seq_len, HEADS, head_size)
    key_heads = key_low.reshape(lead_count, seq_len, HEADS, head_size)
    value_heads = value_low.reshape(lead_count, seq_len, HEADS, head_size)
    raw_scores = jnp.einsum('nqhe,nkhe->nhqk', query_heads, key_heads, precision=HIGHEST) * (1.0 / math.sqrt(head_size))
    raw_scores = low_back(raw_scores)
    masked = jnp.where(key_mask_valid[:, None, None, :], raw_scores, -1e+30)
    row_max = lax.optimization_barrier(jnp.max(masked, axis=-1, keepdims=True))
    exp_scores = jnp.exp(masked - row_max)
    attn_prob = exp_scores / lax.optimization_barrier(jnp.sum(exp_scores, axis=-1, keepdims=True))
    attn_mix = jnp.einsum('nhqk,nkhe->nqhe', low_rank_part(attn_prob), value_heads, precision=HIGHEST)
    return attn_mix.reshape(lead_count, seq_len, model_width)
attend_saved = jax.checkpoint(attend)

def forward_pass(input_rows, query_adapter_term, value_adapter_term, frozen_params, key_mask_valid):
    query_weight_matrix, key_mat, value_weight_matrix, out_mat, up_mat, down_mat, query_down_weight, value_down_weight, query_bias_vector, value_bias_vector, bias_out, bias_up, bias_down, gain_one, shift_one, gain_two, shift_two = frozen_params
    query_preactivation = matrix_product(input_rows, query_weight_matrix) + query_bias_vector + 2.0 * matrix_product(low_rank_part(matrix_product(input_rows, query_down_weight)), query_adapter_term)
    value_preactivation = matrix_product(input_rows, value_weight_matrix) + value_bias_vector + 2.0 * matrix_product(low_rank_part(matrix_product(input_rows, value_down_weight)), value_adapter_term)
    query_low = low_rank_part(low_back(query_preactivation))
    key_low = low_rank_part(low_back(matrix_product(input_rows, key_mat)))
    value_low = low_rank_part(low_back(value_preactivation))
    attn_mix = low_rank_part(low_back(attend_saved(query_low, key_low, value_low, key_mask_valid)))
    first_sum = input_rows + low_back(matrix_product(attn_mix, out_mat) + bias_out)
    normed = norm_rows(first_sum, gain_one, shift_one)
    hidden_pre = low_back(matrix_product(low_rank_part(normed), up_mat) + bias_up)
    hidden_act = low_rank_part(jax.nn.gelu(hidden_pre, approximate=False))
    second_sum = normed + low_back(matrix_product(hidden_act, down_mat) + bias_down)
    return norm_rows(second_sum, gain_two, shift_two)

def reference(tokens, eval_tokens, cotangent, lengths, w_query, w_key, w_value, w_out, w_up, w_down, a_query, a_value, query_up_weight, value_up_weight, query_bias_vector, value_bias_vector, bias_out, bias_up, bias_down, gain_one, shift_one, gain_two, shift_two):
    frozen_params = tuple((member.astype(jnp.float32) for member in (w_query, w_key, w_value, w_out, w_up, w_down, a_query, a_value, query_bias_vector, value_bias_vector, bias_out, bias_up, bias_down, gain_one, shift_one, gain_two, shift_two)))
    query_adapter_term = query_up_weight.astype(jnp.float32)
    value_adapter_term = value_up_weight.astype(jnp.float32)
    merged_weights = (low_rank_part(frozen_params[0] + 2.0 * matrix_product(frozen_params[6], query_adapter_term)), frozen_params[1], low_rank_part(frozen_params[2] + 2.0 * matrix_product(frozen_params[7], value_adapter_term))) + frozen_params[3:]
    zero_adapter_weights = jnp.zeros_like(query_adapter_term)
    block_items = math.gcd(ITEMS_ALL, 8)
    block_count = ITEMS_ALL // block_items
    positions = jnp.arange(SEQ, dtype=jnp.int32)

    def one_block(carry, pieces):
        block_input, evaluate_block, block_cot, block_len = pieces
        key_mask_valid = positions[None, :] < block_len[:, None]

        def apply_encoder_layer(adapter_query_delta, adapter_value_delta, input_rows):
            return forward_pass(input_rows, adapter_query_delta, adapter_value_delta, frozen_params, key_mask_valid)
        layer_result, pullback_function = jax.vjp(apply_encoder_layer, query_adapter_term, value_adapter_term, block_input.astype(jnp.float32))
        grad_cot = block_cot.astype(jnp.float32) * key_mask_valid[:, :, None].astype(jnp.float32)
        grad_query, grad_value, grad_input = pullback_function(grad_cot)
        evaluate_output = forward_pass(evaluate_block.astype(jnp.float32), zero_adapter_weights, zero_adapter_weights, merged_weights, key_mask_valid)
        return ((carry[0] + grad_query, carry[1] + grad_value), (layer_result.astype(jnp.bfloat16), grad_input, evaluate_output.astype(jnp.bfloat16)))
    shape_blocks = (block_count, block_items, SEQ, D)
    start = (jnp.zeros((RANK, D), jnp.float32), jnp.zeros((RANK, D), jnp.float32))
    sums, stacked = lax.scan(one_block, start, (tokens.reshape(shape_blocks), eval_tokens.reshape(shape_blocks), cotangent.reshape(shape_blocks), lengths.reshape(block_count, block_items)))
    layer_result, grad_input, evaluate_output = stacked
    whole = (ITEMS_ALL, SEQ, D)
    return (layer_result.reshape(whole), grad_input.reshape(whole), sums[0], sums[1], evaluate_output.reshape(whole))
```

```python
import functools
import math

import jax
import jax.numpy as jnp
from jax import lax
from jax.experimental import pallas as pl
from jax.experimental.pallas import tpu as pltpu
from jax.sharding import PartitionSpec as P

HEADS = 12
EPSILON = 1e-05
D = 768
FF = 3072
SEQ = 512
HALF = 256
BLOCK = 48
QKV = 2560
QKV_HALF = QKV // 2
OUT_HALF = D // 2
FEED_HALF = FF
STAGED = QKV_HALF + OUT_HALF + FEED_HALF
HOPS = (1, 3, 2)
MESH = pl.DeviceIdType.MESH
BF16 = jnp.bfloat16
F32 = jnp.float32


def place():
    dp, tp = lax.axis_index("dp"), lax.axis_index("tp")
    core = lax.rem(dp, 2)
    z = lax.rem(lax.div(dp, 2), 4) * 2 + tp
    y = lax.rem(lax.div(dp, 8), 4)
    x = lax.div(dp, 32)
    return x, y, z, core


def device(x, y, z, core):
    return (((x * 4 + y) * 4 + lax.div(z, 2)) * 2 + core, lax.rem(z, 2))


def slot_of(z, core):
    return (lax.div(z, 2) * 2 + core) * 2 + lax.rem(z, 2)


def remote(src, dst, send, recv, target):
    return pltpu.make_async_remote_copy(
        src_ref=src, dst_ref=dst, send_sem=send, recv_sem=recv, device_id=target, device_id_type=MESH
    )


def gather_kernel(
    staged, tokens, eval_tokens, cotangent,
    w_qkv, w_out, w_feed, rows, eval_rows, cots,
    arrived, packed, z_send, z_recv, xy_send, xy_recv, sib_send, sib_recv, pair_send, pair_recv, local_sem,
):
    x, y, z, core = place()
    tp = lax.rem(z, 2)
    sibling = device(x, y, z, 1 - core)
    partner = device(x, y, z + 1 - 2 * tp, core)
    first = core == 0
    u = jnp.where(first, x, y)
    v = jnp.where(first, y, x)

    def at(uu, vv):
        uu, vv = lax.rem(uu, 4), lax.rem(vv, 4)
        return device(jnp.where(first, uu, vv), jnp.where(first, vv, uu), z, core)

    def block(uu, vv):
        uu, vv = lax.rem(uu, 4), lax.rem(vv, 4)
        return jnp.where(first, uu * 4 + vv, vv * 4 + uu)

    column = [(dz, dc) for dz in range(8) for dc in range(2) if (dz, dc) != (0, 0)]
    greet = [device(x, y, lax.rem(z + dz, 8), lax.rem(core + dc, 2)) for dz, dc in column]
    greet += [at(u + h, v) for h in HOPS] + [at(u, v + h) for h in HOPS]
    barrier = pltpu.get_barrier_semaphore()
    for other in greet:
        pl.semaphore_signal(barrier, inc=1, device_id=other, device_id_type=MESH)
    pl.semaphore_wait(barrier, len(greet))

    mine = slot_of(z, core)
    parts = ((0, QKV_HALF), (QKV_HALF, STAGED - QKV_HALF))
    waits = []

    def z_copy(part, n):
        dz, dc = column[n]
        lo, width = parts[part]
        zz, cc = lax.rem(z + dz, 8), lax.rem(core + dc, 2)
        return remote(
            staged.at[cc, :, pl.ds(lo, width)], arrived.at[mine, :, pl.ds(lo, width)],
            z_send.at[part, n], z_recv.at[part, mine], device(x, y, zz, cc),
        )

    def z_arrival(part, n):
        dz, dc = column[n]
        lo, width = parts[part]
        slot = slot_of(lax.rem(z + dz, 8), lax.rem(core + dc, 2))
        return remote(
            staged.at[core, :, pl.ds(lo, width)], arrived.at[slot, :, pl.ds(lo, width)],
            z_send.at[part, n], z_recv.at[part, slot], partner,
        )

    def send(copy):
        copy.start()
        waits.append(copy)

    for n in range(15):
        send(z_copy(0, n))
    pair = []
    t_rows = pl.ds(pl.multiple_of(tp * HALF, HALF), HALF)
    pair.append(remote(tokens.at[1 - tp], rows.at[t_rows], pair_send.at[0], pair_recv.at[0], partner))
    pair.append(remote(eval_tokens, eval_rows.at[:, t_rows], pair_send.at[1], pair_recv.at[1], partner))
    pair.append(remote(cotangent.at[1 - tp], cots.at[t_rows], pair_send.at[2], pair_recv.at[2], partner))
    own = [
        pltpu.make_async_copy(tokens.at[tp], rows.at[t_rows], local_sem.at[0]),
        pltpu.make_async_copy(eval_tokens, eval_rows.at[:, t_rows], local_sem.at[1]),
        pltpu.make_async_copy(cotangent.at[tp], cots.at[t_rows], local_sem.at[2]),
    ]
    for n in range(15):
        send(z_copy(1, n))
    for c in pair + own:
        c.start()
    arrived[pl.ds(mine, 1)] = staged[pl.ds(core, 1)]

    groups = (
        (w_qkv, pl.multiple_of(core * QKV_HALF, 128), QKV_HALF),
        (w_out, pl.multiple_of(core * OUT_HALF, 128), OUT_HALF),
        (w_feed, pl.multiple_of(core * FEED_HALF, 128), FEED_HALF),
    )

    def region(g, uu, vv, other=False):
        ref, lo, width = groups[g]
        if other:
            lo = pl.multiple_of((1 - core) * width, 128)
        return ref.at[pl.ds(pl.multiple_of(block(uu, vv) * BLOCK, BLOCK), BLOCK), pl.ds(lo, width)]

    def pieces(j, k):
        return (u + (4 - HOPS[j - 1] if j else 0), v + (4 - HOPS[k - 1] if k else 0))

    def spread_first(g):
        for k, h in enumerate(HOPS):
            r = region(g, u, v)
            send(remote(r, r, xy_send.at[g, k], xy_recv.at[g, k], at(u + h, v)))

    def spread_second(g, j):
        r = region(g, *pieces(j, 0))
        for k, h in enumerate(HOPS):
            n = 3 + 3 * j + k
            send(remote(r, r, xy_send.at[g, n], xy_recv.at[g, n], at(u, v + h)))

    def to_sibling(g, j, k):
        r = region(g, *pieces(j, k))
        send(remote(r, r, sib_send.at[g, 4 * j + k], sib_recv.at[g, 4 * j + k], sibling))

    def take(g, j, k):
        r = region(g, *pieces(j, k))
        n = 3 + 3 * j + k - 1 if k else j - 1
        remote(r, r, xy_send.at[g, n], xy_recv.at[g, n], partner).wait_recv()

    def take_sibling(g, j, k):
        r = region(g, v + (4 - HOPS[j - 1] if j else 0), u + (4 - HOPS[k - 1] if k else 0), True)
        remote(r, r, sib_send.at[g, 4 * j + k], sib_recv.at[g, 4 * j + k], partner).wait_recv()

    def spread(g):
        spread_first(g)
        spread_second(g, 0)
        to_sibling(g, 0, 0)
        for j in range(1, 4):
            take(g, j, 0)
            spread_second(g, j)
            to_sibling(g, j, 0)

    def finish(g):
        for j in range(4):
            for k in range(1, 4):
                take(g, j, k)
                to_sibling(g, j, k)
        for j in range(4):
            for k in range(4):
                take_sibling(g, j, k)

    here = pl.ds(pl.multiple_of(block(u, v) * BLOCK, BLOCK), BLOCK)
    for n in range(15):
        z_arrival(0, n).wait_recv()
    for s in range(16):
        packed[3 * s : 3 * s + 3, 0:QKV_HALF] = arrived[s, 0:3, 0:QKV_HALF].astype(F32)
    w_qkv[here, pl.ds(pl.multiple_of(core * QKV_HALF, 128), QKV_HALF)] = packed[:, 0:QKV_HALF].astype(BF16)
    spread(0)
    for n in range(15):
        z_arrival(1, n).wait_recv()
    for s in range(16):
        packed[3 * s : 3 * s + 3, 0:OUT_HALF] = arrived[s, 0:3, QKV_HALF : QKV_HALF + OUT_HALF].astype(F32)
    w_out[here, pl.ds(pl.multiple_of(core * OUT_HALF, 128), OUT_HALF)] = packed[:, 0:OUT_HALF].astype(BF16)
    lo = QKV_HALF + OUT_HALF
    for s in range(16):
        part = s % 2
        for half in range(2):
            row = (s // 2) * 6 + half * 3
            for which in range(2):
                src = lo + half * 1536 + which * D
                packed[row : row + 3, which * 1536 + part * D : which * 1536 + part * D + D] = arrived[
                    s, 0:3, src : src + D
                ].astype(F32)
    w_feed[here, pl.ds(pl.multiple_of(core * FEED_HALF, 128), FEED_HALF)] = packed[...].astype(BF16)
    spread(1)
    spread(2)
    finish(0)
    finish(1)
    finish(2)
    for c in pair:
        c.wait()
    for c in own:
        c.wait()
    for c in waits:
        c.wait_send()


def gather_all(staged, tokens, eval_tokens, cotangent):
    out = (
        jax.ShapeDtypeStruct((D, QKV), BF16),
        jax.ShapeDtypeStruct((D, D), BF16),
        jax.ShapeDtypeStruct((D, 2 * FF), BF16),
        jax.ShapeDtypeStruct((SEQ, D), BF16),
        jax.ShapeDtypeStruct((2, SEQ, D), BF16),
        jax.ShapeDtypeStruct((SEQ, D), BF16),
    )
    vmem, hbm = pl.BlockSpec(memory_space=pltpu.VMEM), pl.BlockSpec(memory_space=pl.ANY)
    dma = pltpu.SemaphoreType.DMA
    return pl.pallas_call(
        gather_kernel,
        out_shape=out,
        in_specs=[vmem, hbm, hbm, hbm],
        out_specs=[vmem, vmem, vmem, hbm, hbm, hbm],
        scratch_shapes=[
            pltpu.VMEM((16, 4, STAGED), BF16),
            pltpu.VMEM((BLOCK, FF), F32),
            dma((2, 15)), dma((2, 16)), dma((3, 15)), dma((3, 15)), dma((3, 16)), dma((3, 16)),
            dma((3,)), dma((3,)), dma((3,)),
        ],
        compiler_params=pltpu.CompilerParams(collective_id=0, has_side_effects=True, vmem_limit_bytes=56 << 20),
    )(staged, tokens, eval_tokens, cotangent)


def staged_weights(w_query, w_key, w_value, w_out, w_up, w_down, a_query, a_value):
    def halves(a, count):
        return jnp.moveaxis(a.reshape(3, 2, count), 1, 0)

    blank = functools.partial(jnp.zeros, dtype=BF16)
    qkv = jnp.concatenate([a_query, a_value, blank((3, 112)), w_query, w_key, w_value, blank((3, 128))], axis=1)
    feed = jnp.stack([w_up, w_down.T]).reshape(2, 2, 3, 2, D)
    feed = jnp.transpose(feed, (3, 2, 1, 0, 4)).reshape(2, 3, FF)
    both = jnp.concatenate([halves(qkv, QKV_HALF), halves(w_out, OUT_HALF), feed], axis=2)
    return jnp.pad(both, ((0, 0), (0, 1), (0, 0)))


def norm_rows(rows, gain, shift):
    mean = jnp.mean(rows, axis=-1, keepdims=True)
    centred = rows - mean
    spread = jnp.mean(centred * centred, axis=-1, keepdims=True)
    return centred * lax.rsqrt(spread + EPSILON) * gain + shift


def gelu(u):
    return jax.nn.gelu(u, approximate=False)


def dot(a, b):
    return jnp.dot(a, b, preferred_element_type=F32)


def split_heads(a):
    return a.reshape(*a.shape[:-1], HEADS, D // HEADS)


def attend(query, key, value, valid):
    q, k, v = split_heads(query), split_heads(key), split_heads(value)
    scores = jnp.einsum("nqhe,nkhe->nhqk", q, k, preferred_element_type=F32) * 0.125
    scores = jnp.where(valid[:, None, None, :], scores, -1e30)
    top = jnp.max(scores, axis=-1, keepdims=True)
    e = jnp.exp(scores - top)
    prob = e / jnp.sum(e, axis=-1, keepdims=True)
    mix = jnp.einsum("nhqk,nkhe->nqhe", prob.astype(BF16), v, preferred_element_type=F32)
    return mix.reshape(query.shape).astype(BF16), prob


def shards(
    tokens, eval_tokens, cotangent, lengths, w_query, w_key, w_value, w_out, w_up, w_down, a_query, a_value,
    query_up, value_up, query_bias, value_bias, bias_out, bias_up, bias_down, gain_one, shift_one, gain_two, shift_two,
):
    tp = lax.axis_index("tp")
    staged = staged_weights(w_query, w_key, w_value, w_out, w_up, w_down, a_query, a_value)
    qkv, out_mat, feed, rows, eval_rows, cots = gather_all(staged, tokens, eval_tokens, cotangent)
    up = jnp.concatenate([feed[:, 0:1536], feed[:, FF : FF + 1536]], axis=1)
    down = jnp.concatenate([feed[:, 1536:FF], feed[:, FF + 1536 :]], axis=1)
    b_up = jnp.transpose(bias_up.reshape(2, 2, D), (1, 0, 2)).reshape(FF)
    aq, av = qkv[:, 0:8], qkv[:, 8:16]
    wq, wk, wv = (qkv[:, 128 + n * D : 128 + n * D + D] for n in range(3))
    g1, s1, g2, s2, bo, bu, bd, bq, bv = (
        a.astype(F32) for a in (gain_one, shift_one, gain_two, shift_two, bias_out, b_up, bias_down, query_bias, value_bias)
    )
    merged_q = (wq.astype(F32) + 2.0 * dot(aq, query_up)).astype(BF16)
    merged_v = (wv.astype(F32) + 2.0 * dot(av, value_up)).astype(BF16)
    valid = jnp.arange(SEQ, dtype=jnp.int32)[None, :] < lengths[:, None]

    def after(x, mix):
        first = x.astype(F32) + dot(mix, out_mat) + bo
        normed = norm_rows(first, g1, s1)
        pre = dot(normed.astype(BF16), up) + bu
        second = normed + jnp.einsum("sf,df->sd", gelu(pre).astype(BF16), down, preferred_element_type=F32) + bd
        return first, pre, second, norm_rows(second, g2, s2)

    x = rows
    low_q, low_v = dot(x, aq).astype(BF16), dot(x, av).astype(BF16)
    q = (dot(x, wq) + bq + 2.0 * dot(low_q, query_up)).astype(BF16)
    k = dot(x, wk).astype(BF16)
    v = (dot(x, wv) + bv + 2.0 * dot(low_v, value_up)).astype(BF16)
    my_valid = lax.dynamic_slice_in_dim(valid, tp, 1)
    mix, prob = attend(q[None], k[None], v[None], my_valid)
    first, pre, second, layer = after(x, mix[0])
    cot = cots.astype(F32) * my_valid[0][:, None]
    g_second = jax.vjp(lambda r: norm_rows(r, g2, s2), second)[1](cot)[0]
    g_act = dot(g_second.astype(BF16), down)
    g_pre = jax.vjp(gelu, pre)[1](g_act)[0].astype(BF16)
    g_normed = g_second + jnp.einsum("sf,df->sd", g_pre, up, preferred_element_type=F32)
    g_first = jax.vjp(lambda r: norm_rows(r, g1, s1), first)[1](g_normed)[0]
    g_mix = jnp.einsum("sd,ed->se", g_first.astype(BF16), out_mat, preferred_element_type=F32).astype(BF16)
    gh, vh, kh, qh = split_heads(g_mix), split_heads(v), split_heads(k), split_heads(q)
    prob = prob[0]
    g_prob = jnp.einsum("qhe,khe->hqk", gh, vh, preferred_element_type=F32)
    g_score = (prob * (g_prob - jnp.sum(prob * g_prob, axis=-1, keepdims=True))).astype(BF16)
    gq = (jnp.einsum("hqk,khe->qhe", g_score, kh, preferred_element_type=F32) * 0.125).reshape(SEQ, D).astype(BF16)
    gk = (jnp.einsum("hqk,qhe->khe", g_score, qh, preferred_element_type=F32) * 0.125).reshape(SEQ, D).astype(BF16)
    gv = jnp.einsum("hqk,qhe->khe", prob.astype(BF16), gh, preferred_element_type=F32).reshape(SEQ, D).astype(BF16)

    def back(g, w):
        return jnp.einsum("sd,ed->se", g, w, preferred_element_type=F32)

    igrad = g_first + back(gq, merged_q) + back(gk, wk) + back(gv, merged_v)
    gbq = 2.0 * jnp.einsum("sr,sd->rd", low_q, gq, preferred_element_type=F32)
    gbv = 2.0 * jnp.einsum("sr,sd->rd", low_v, gv, preferred_element_type=F32)
    gbq, gbv = lax.psum((gbq, gbv), ("dp", "tp"))

    layer_low = layer.astype(BF16).reshape(2, HALF, D)
    swap = [(0, 1), (1, 0)]

    def place_rows(a):
        keep = lax.dynamic_index_in_dim(a, tp, 0, keepdims=False)
        got = lax.ppermute(lax.dynamic_index_in_dim(a, 1 - tp, 0, keepdims=False).astype(BF16), "tp", swap)
        got = got.astype(a.dtype)
        return jnp.where(tp == 0, jnp.stack([keep, got]), jnp.stack([got, keep]))

    activations = place_rows(layer_low)
    input_grad = place_rows(igrad.reshape(2, HALF, D))

    eq = dot(eval_tokens, merged_q) + bq
    ek = dot(eval_rows, wk)
    ev = dot(eval_rows, merged_v) + bv
    emix, _ = attend(eq.astype(BF16), ek.astype(BF16), ev.astype(BF16), valid)
    evaluated = after(eval_tokens.reshape(SEQ, D), emix.reshape(SEQ, D))[3].astype(BF16).reshape(2, HALF, D)
    return activations, input_grad, gbq, gbv, evaluated


def solution(mesh):
    rows, frozen, whole = P("dp", "tp", None), P(("dp", "tp"), None), P()
    in_specs = (rows, rows, rows, P("dp"), frozen, frozen, frozen, frozen, P("dp", "tp"), P("tp", "dp"), frozen, frozen)
    in_specs += (whole,) * 11
    out_specs = (rows, rows, whole, whole, rows)
    return jax.shard_map(shards, mesh=mesh, in_specs=in_specs, out_specs=out_specs, check_vma=False)
```

```python
import functools

import jax
import jax.numpy as jnp
from jax import lax
from jax.experimental import pallas as pl
from jax.experimental.pallas import tpu as pltpu
from jax.sharding import PartitionSpec as P

EPSILON = 1e-05
D = 768
FF = 3072
SEQ = 512
HALF = 256
BLOCK = 48
PAIRS = 6
SIDE = 384
WIDTHS = (640, 640, 384, 1536, 1536)
STARTS = (0, 640, 1280, 1664, 3200)
STAGED = 4736
DIRECT = (True, False, False, False, False)
Z_PARTS = ((0, 640), (640, 1024), (1664, 3072))
MESH = pl.DeviceIdType.MESH
BF16 = jnp.bfloat16
F32 = jnp.float32
COMM = True


def dot(a, b):
    return jnp.dot(a, b, preferred_element_type=F32)


def dot_nt(a, b):
    return lax.dot_general(a, b, (((1,), (1,)), ((), ())), preferred_element_type=F32)


def dot_tn(a, b):
    return lax.dot_general(a, b, (((0,), (0,)), ((), ())), preferred_element_type=F32)


def place():
    dp, tp = lax.axis_index("dp"), lax.axis_index("tp")
    core = lax.rem(dp, 2)
    z = lax.rem(lax.div(dp, 2), 4) * 2 + tp
    y = lax.rem(lax.div(dp, 8), 4)
    x = lax.div(dp, 32)
    return x, y, z, core


def device(x, y, z, core):
    return (((x * 4 + y) * 4 + lax.div(z, 2)) * 2 + core, lax.rem(z, 2))


def slot_of(z, core):
    return (lax.div(z, 2) * 2 + core) * 2 + lax.rem(z, 2)


def remote(src, dst, send, recv, target):
    return pltpu.make_async_remote_copy(
        src_ref=src, dst_ref=dst, send_sem=send, recv_sem=recv, device_id=target, device_id_type=MESH
    )


def by_rows(count, body, size=64):
    def step(i, carry):
        body(pl.ds(pl.multiple_of(i * size, size), size), i * size)
        return carry

    lax.fori_loop(0, count // size, step, 0)


def layer_kernel(
    lengths, staged, tokens, eval_tokens, cotangent, ups, vec,
    act_out, grad_out, eval_out, adapter_out,
    arrived, packed, wa0, wa1, wo, f0, f1, mkv, umat, x, xe, cot, low, kb,
    q, k, v, mix_t, expo, inv, scores, ds, gates, hidden, xh1, rs1, norm_low, acc, y_low, dqkv,
    qe, mixe_t, expo_e, inv_e, norm_e, acc_e, ig_send, ig_recv, ig_own, red, red_sib, red_x, red_y, red_z, red_sum, red_all,
    z_send, z_recv, xy_send, xy_recv, sib_send, sib_recv, pair_send, pair_recv, local_sem, red_send, red_recv,
):
    if COMM:
        px, py, z, core = place()
    else:
        px = py = z = core = jnp.int32(0)
    tp = lax.rem(z, 2)
    first = core == 0
    u = jnp.where(first, px, py)
    w = jnp.where(first, py, px)
    sibling = device(px, py, z, 1 - core)
    partner = device(px, py, z + 1 - 2 * tp, core)
    mine_rows = pl.ds(pl.multiple_of(tp * HALF, HALF), HALF)
    other_rows = pl.ds(pl.multiple_of((1 - tp) * HALF, HALF), HALF)
    waits = []

    def send(copy):
        if COMM:
            copy.start()
            waits.append(copy)

    def at(uu, ww):
        uu, ww = lax.rem(uu, 4), lax.rem(ww, 4)
        return device(jnp.where(first, uu, ww), jnp.where(first, ww, uu), z, core)

    def block_row(uu, ww):
        uu, ww = lax.rem(uu, 4), lax.rem(ww, 4)
        return pl.multiple_of(jnp.where(first, uu * 4 + ww, ww * 4 + uu) * BLOCK, BLOCK)

    column = [(dz, dc) for dz in range(8) for dc in range(2) if (dz, dc) != (0, 0)]
    if COMM:
        greet = [device(px, py, lax.rem(z + dz, 8), lax.rem(core + dc, 2)) for dz, dc in column]
        greet += [at(u + h, w) for h in (1, 2, 3)] + [at(u, w + h) for h in (1, 2, 3)]
        barrier = pltpu.get_barrier_semaphore()
        for other in greet:
            pl.semaphore_signal(barrier, inc=1, device_id=other, device_id_type=MESH)

    lane = lax.broadcasted_iota(jnp.int32, (1, 128), 1)
    left = lane < 64
    zero_u = jnp.zeros((8, SIDE), F32)
    upf = ups[...].astype(F32) * 2.0
    top = [upf[0:8, 0:SIDE], zero_u, upf[0:8, SIDE:D], zero_u]
    bottom = [zero_u, upf[8:16, 0:SIDE], zero_u, upf[8:16, SIDE:D]]
    umat[...] = jnp.concatenate(
        [jnp.concatenate(top, axis=1), jnp.concatenate(bottom, axis=1), jnp.zeros((112, 2 * D), F32)], axis=0
    ).astype(BF16)
    for item in range(2):
        position = lax.broadcasted_iota(jnp.int32, (SEQ, 128), 0)
        kb[item] = jnp.where(position < lengths[item], 0.0, -1e30).astype(BF16)

    if COMM:
        pl.semaphore_wait(barrier, len(greet))

    mine = slot_of(z, core)

    def z_copy(part, n):
        dz, dc = column[n]
        lo, width = Z_PARTS[part]
        zz, cc = lax.rem(z + dz, 8), lax.rem(core + dc, 2)
        return remote(
            staged.at[cc, :, pl.ds(lo, width)], arrived.at[mine, :, pl.ds(lo, width)],
            z_send.at[part, n], z_recv.at[part, mine], device(px, py, zz, cc),
        )

    def z_wait(part):
        if not COMM:
            return
        lo, width = Z_PARTS[part]
        for dz, dc in column:
            slot = slot_of(lax.rem(z + dz, 8), lax.rem(core + dc, 2))
            place_at = arrived.at[slot, :, pl.ds(lo, width)]
            remote(place_at, place_at, z_send.at[part, 0], z_recv.at[part, slot], partner).wait_recv()

    groups = [(ref, width, pl.multiple_of(core * width, 128)) for ref, width in zip((wa0, wa1, wo, f0, f1), WIDTHS)]

    def region(g, uu, ww, part=None, other=False):
        ref, width, lo = groups[g]
        if other:
            lo = pl.multiple_of((1 - core) * width, 128)
        cut = (width // 128 + 1) // 2 * 128
        if part == 0:
            width = cut
        elif part == 1:
            lo, width = pl.multiple_of(lo + cut, 128), width - cut
        return ref.at[pl.ds(block_row(uu, ww), BLOCK), pl.ds(lo, width)]

    steps = (0, 3, 1, 2)

    def xy(g, n, r, target):
        send(remote(r, r, xy_send.at[g, n], xy_recv.at[g, n], target))

    def take(g, n, r):
        if COMM:
            remote(r, r, xy_send.at[g, n], xy_recv.at[g, n], partner).wait_recv()

    def to_sibling(g, j, i):
        r = region(g, u + steps[j], w + steps[i])
        send(remote(r, r, sib_send.at[g, 4 * j + i], sib_recv.at[g, 4 * j + i], sibling))

    def from_sibling(g):
        if COMM:
            for j in range(4):
                for i in range(4):
                    r = region(g, w + steps[j], u + steps[i], other=True)
                    n = 4 * j + i
                    remote(r, r, sib_send.at[g, n], sib_recv.at[g, n], partner).wait_recv()

    def line_send(g, base, uu, ww, ahead):
        r = region(g, uu, ww)
        xy(g, base, r, ahead(1))
        xy(g, base + 1, r, ahead(3))
        if DIRECT[g]:
            xy(g, base + 2, r, ahead(2))

    def line_forward(g, base, behind, before, ahead):
        take(g, base, behind())
        if not DIRECT[g]:
            xy(g, base + 2, behind(0), ahead(1))
        take(g, base + 1, before())
        if not DIRECT[g]:
            xy(g, base + 3, before(1), ahead(3))

    def line_finish(g, base, far):
        if DIRECT[g]:
            take(g, base + 2, far())
        else:
            take(g, base + 2, far(0))
            take(g, base + 3, far(1))

    def along_u(h):
        return at(u + h, w)

    def along_w(h):
        return at(u, w + h)

    def first_send(g):
        line_send(g, 0, u, w, along_u)

    def first_forward(g):
        line_forward(
            g, 0, lambda part=None: region(g, u + 3, w, part), lambda part=None: region(g, u + 1, w, part), along_u
        )

    def first_finish(g):
        line_finish(g, 0, lambda part=None: region(g, u + 2, w, part))

    def second_send(g, j):
        line_send(g, 4 + 4 * j, u + steps[j], w, along_w)
        to_sibling(g, j, 0)

    def second_forward(g, j):
        uu = u + steps[j]
        line_forward(
            g, 4 + 4 * j, lambda part=None: region(g, uu, w + 3, part), lambda part=None: region(g, uu, w + 1, part),
            along_w,
        )
        to_sibling(g, j, 1)
        to_sibling(g, j, 2)

    def second_finish(g, j):
        line_finish(g, 4 + 4 * j, lambda part=None: region(g, u + steps[j], w + 2, part))
        to_sibling(g, j, 3)

    here = pl.ds(block_row(u, w), BLOCK)

    def assemble(g):
        ref, width, lo = groups[g]
        for s in range(16):
            if g < 3:
                packed[3 * s : 3 * s + 3, 0:width] = arrived[s, 0:3, STARTS[g] : STARTS[g] + width].astype(F32)
            elif s % 2 == g - 3:
                for half in range(2):
                    row, src = (s // 2) * 6 + half * 3, STARTS[3] + half * 1536
                    packed[row : row + 3, :] = arrived[s, 0:3, src : src + 1536].astype(F32)
        ref[here, pl.ds(lo, width)] = packed[:, 0:width].astype(BF16)


    def row(n):
        return vec[n : n + 1, :]

    def project(g):
        wa = (wa0, wa1)[g]
        side = slice(SIDE * g, SIDE * g + SIDE)
        for half in range(2):
            r = slice(HALF * half, HALF * half + HALF)
            got = dot(x[r, :], wa[...])
            if g == 0:
                low[r, :] = got[:, 0:128].astype(BF16)
            more = dot(low[r, :], umat[:, D * g : D * g + D])
            q[r, side] = ((got[:, 128:512] + more[:, 0:SIDE] + row(0)[:, side]) * 0.125).astype(BF16)
            k[r, side] = got[:, 512:896].astype(BF16)
            v[r, side] = (got[:, 896:1280] + more[:, SIDE:D] + row(1)[:, side]).astype(BF16)

    def merge():
        for g, wa in enumerate((wa0, wa1)):
            more = dot(wa0[:, 0:128], umat[:, D * g : D * g + D])
            side = SIDE * g
            mkv[:, side : side + SIDE] = (wa[:, 128:512].astype(F32) + more[:, 0:SIDE]).astype(BF16)
            mkv[:, D + side : D + side + SIDE] = wa[:, 512:896]
            mkv[:, 2 * D + side : 2 * D + side + SIDE] = (wa[:, 896:1280].astype(F32) + more[:, SIDE:D]).astype(BF16)

    def project_eval():
        for item in range(2):
            for half in range(2):
                r = slice(HALF * half, HALF * half + HALF)
                got = dot(xe[item, r, :], mkv[:, D : 3 * D])
                gates[r, D * item : D * item + D] = got[:, 0:D].astype(BF16)
                gates[r, D * (2 + item) : D * (3 + item)] = (got[:, D:] + row(1)).astype(BF16)
            own = dot(xe[item, mine_rows, :], mkv[:, 0:D])
            qe[HALF * item : HALF * item + HALF, :] = ((own + row(0)) * 0.125).astype(BF16)

    def heads(k2, q2, bias):
        for h in range(2):
            keep = left if h == 0 else lane >= 64
            spare = lane == (64 if h == 0 else 0)
            kh = jnp.where(keep, k2, jnp.where(spare, bias, jnp.zeros_like(bias)))
            yield h, kh, jnp.where(spare, jnp.ones_like(q2), q2)

    def softmax(h, queries, e_ref, inverse):
        for c in range(0, queries, 256):
            s = scores[h, :, c : c + 256]
            e = jnp.exp(s - jnp.max(s, axis=0, keepdims=True))
            inverse[:, c : c + 256] = 1.0 / jnp.sum(e, axis=0, keepdims=True)
            e_ref[:, c : c + 256] = e.astype(BF16)

    def attend(lo, hi):
        def pair(p, carry):
            s = pl.ds(pl.multiple_of(p * 128, 128), 128)
            v2t = jnp.transpose(v[:, s])
            for h, kh, qh in heads(k[:, s], q[:, s], kb[tp]):
                scores[h] = dot_nt(kh, qh)
            for h in range(2):
                n = 2 * p + h
                softmax(h, SEQ, expo.at[n], inv.at[n])
                o = dot(v2t[64 * h : 64 * h + 64, :], expo[n]) * inv[n]
                mix_t[pl.ds(pl.multiple_of(p * 128 + 64 * h, 64), 64), :] = o.astype(BF16)
            return carry

        lax.fori_loop(lo, hi, pair, 0)

    def attend_eval(item):
        own = slice(HALF * item, HALF * item + HALF)

        def pair(p, carry):
            s = pl.ds(pl.multiple_of(p * 128, 128), 128)
            ks = pl.ds(pl.multiple_of(D * item + p * 128, 128), 128)
            vs = pl.ds(pl.multiple_of(D * (2 + item) + p * 128, 128), 128)
            v2t = jnp.transpose(gates[:, vs])
            for h, kh, qh in heads(gates[:, ks], qe[own, s], kb[item]):
                scores[h, :, 0:HALF] = dot_nt(kh, qh)
            for h in range(2):
                softmax(h, HALF, expo_e.at[h], inv_e.at[h])
                o = dot(v2t[64 * h : 64 * h + 64, :], expo_e[h]) * inv_e[h]
                mixe_t[pl.ds(pl.multiple_of(p * 128 + 64 * h, 64), 64), own] = o.astype(BF16)
            return carry

        lax.fori_loop(0, PAIRS, pair, 0)

    def mean(a):
        return jnp.sum(a, axis=-1, keepdims=True) * (1.0 / D)

    def normalise(a):
        centred = a - mean(a)
        scale = lax.rsqrt(mean(centred * centred) + EPSILON)
        return centred * scale, scale

    def first_norm(mixed, base, total, low_ref, keep):
        total[...] = dot_tn(mixed[...], wo[...])

        def body(r, at_row):
            xhat, scale = normalise(total[r, :] + base(at_row).astype(F32) + row(2))
            if keep:
                xh1[r, :] = xhat
                rs1[r, :] = scale
            normed = xhat * row(4) + row(5)
            low_ref[r, :] = normed.astype(BF16)
            total[r, :] = normed + row(3)

        by_rows(SEQ, body)

    def feed(part, low_ref, total, keep):
        f = (f0, f1)[part]
        for c in range(2):
            n = 2 * part + c
            bias = row(8 + n)
            for half in range(2):
                r = slice(HALF * half, HALF * half + HALF)
                pre = dot(low_ref[r, :], f[:, 1536 * c : 1536 * c + D]) + bias
                phi = 0.5 + 0.5 * lax.erf(pre * 0.7071067811865476)
                hidden[r, :] = (pre * phi).astype(BF16)
                if keep:
                    slope = phi + pre * (0.3989422804014327 * jnp.exp(pre * pre * -0.5))
                    gates[r, D * n : D * n + D] = slope.astype(BF16)
                total[r, :] += dot_nt(hidden[r, :], f[:, 1536 * c + D : 1536 * c + 2 * D])

    def feed_back(part):
        f = (f0, f1)[part]
        for c in range(2):
            n = 2 * part + c
            for half in range(2):
                r = slice(HALF * half, HALF * half + HALF)
                g = dot(norm_low[r, :], f[:, 1536 * c + D : 1536 * c + 2 * D])
                hidden[r, :] = (g * gates[r, D * n : D * n + D].astype(F32)).astype(BF16)
                acc[r, :] += dot_nt(hidden[r, :], f[:, 1536 * c : 1536 * c + D])

    def second_norm(total, out, backward):
        def body(r, at_row):
            xhat, scale = normalise(total[r, :])
            out[r, :] = (xhat * row(6) + row(7)).astype(BF16)
            if backward:
                position = lax.broadcasted_iota(jnp.int32, (64, 1), 0) + at_row
                c = jnp.where(position < lengths[tp], cot[r, :].astype(F32), 0.0) * row(6)
                g = (c - mean(c) - xhat * mean(c * xhat)) * scale
                total[r, :] = g
                norm_low[r, :] = g.astype(BF16)

        by_rows(SEQ, body)

    def first_norm_back():
        def body(r, at_row):
            c = acc[r, :] * row(4)
            xhat = xh1[r, :]
            g = (c - mean(c) - xhat * mean(c * xhat)) * rs1[r, :]
            acc[r, :] = g
            norm_low[r, :] = g.astype(BF16)

        by_rows(SEQ, body)
        g = dot_nt(wo[...], norm_low[...])
        for n in range(12):
            mix_t[64 * n : 64 * n + 64, :] = (g[64 * n : 64 * n + 64, :] * inv[n]).astype(BF16)

    def attend_back(lo, hi):
        def pair(p, carry):
            def lanes(section):
                return pl.ds(pl.multiple_of(D * section + p * 128, 128), 128)

            s = lanes(0)
            k2, q2, v2 = k[:, s], q[:, s], v[:, s]
            k2t = jnp.transpose(k2)
            g2t = mix_t[pl.ds(pl.multiple_of(p * 128, 128), 128), :]
            for h in range(2):
                keep = left if h == 0 else lane >= 64
                scores[h] = dot(jnp.where(keep, v2, jnp.zeros_like(v2)), g2t)
            dq, dk, dv = [], [], []
            for h in range(2):
                n = 2 * p + h
                for c in range(0, SEQ, 256):
                    e = expo[n, :, c : c + 256].astype(F32)
                    g = scores[h, :, c : c + 256]
                    inner = jnp.sum(e * g, axis=0, keepdims=True) * inv[n, :, c : c + 256]
                    ds[h, :, c : c + 256] = (e * (g - inner)).astype(BF16)
                dq.append(dot(k2t[64 * h : 64 * h + 64, :], ds[h]))
                dk.append(dot(ds[h], q2))
                dv.append(dot_nt(expo[n], g2t))
            dqkv[:, s] = (jnp.transpose(jnp.concatenate(dq, axis=0)) * 0.125).astype(BF16)
            dqkv[:, lanes(1)] = jnp.where(left, dk[0], dk[1]).astype(BF16)
            dqkv[:, lanes(2)] = jnp.where(left, dv[0], dv[1]).astype(BF16)
            return carry

        lax.fori_loop(lo, hi, pair, 0)

    def adapter_grads():
        red[0:8, :] = dot_tn(low[...], dqkv[:, 0:D])[0:8, :] * 2.0
        red[8:16, :] = dot_tn(low[...], dqkv[:, 2 * D :])[8:16, :] * 2.0

    def input_grads(r):
        return acc[r, :] + dot_nt(dqkv[r, :], mkv[...])


    half_row = pl.ds(pl.multiple_of(core * 8, 8), 8)

    def exchange(n, src, dst, target):
        c = remote(src, dst, red_send.at[n], red_recv.at[n], target)
        send(c)

    def expect(n, dst):
        if COMM:
            remote(dst, dst, red_send.at[n], red_recv.at[n], partner).wait_recv()

    def reduce_sibling():
        exchange(0, red.at[pl.ds(pl.multiple_of((1 - core) * 8, 8), 8)], red_sib, sibling)

    def reduce_line(base, buffer, here_at, count, target_of):
        buffer[here_at] = red_sum[...]
        for h in range(1, count):
            exchange(base + h, red_sum, buffer.at[here_at], target_of(h))

    def line_total(base, buffer, here_at, count):
        for h in range(1, count):
            src = lax.rem(here_at + count - h, count)
            expect(base + h, buffer.at[src])
        total = buffer[0]
        for h in range(1, count):
            total = total + buffer[h]
        return total


    pairs = []
    if COMM:
        for n in range(15):
            send(z_copy(0, n))
        pairs = [
            remote(tokens.at[1 - tp], x.at[mine_rows], pair_send.at[0], pair_recv.at[0], partner),
            remote(eval_tokens, xe.at[:, mine_rows], pair_send.at[1], pair_recv.at[1], partner),
            remote(cotangent.at[1 - tp], cot.at[mine_rows], pair_send.at[2], pair_recv.at[2], partner),
        ]
        pairs[0].start()
    own = [
        pltpu.make_async_copy(tokens.at[tp], x.at[mine_rows], local_sem.at[0]),
        pltpu.make_async_copy(eval_tokens, xe.at[:, mine_rows], local_sem.at[1]),
        pltpu.make_async_copy(cotangent.at[tp], cot.at[mine_rows], local_sem.at[2]),
    ]
    for c in own:
        c.start()
    if COMM:
        for part in (1, 2):
            for n in range(15):
                send(z_copy(part, n))
        pairs[1].start()
        pairs[2].start()
    arrived[pl.ds(mine, 1)] = staged[pl.ds(core, 1)]

    z_wait(0)
    assemble(0)
    first_send(0)
    second_send(0, 0)
    z_wait(1)
    assemble(1)
    assemble(2)
    first_forward(0)
    second_send(0, 1)
    second_send(0, 2)
    first_finish(0)
    second_send(0, 3)
    first_send(1)
    first_send(2)
    for j in range(4):
        second_forward(0, j)
    second_send(1, 0)
    second_send(2, 0)
    for j in range(4):
        second_finish(0, j)
    first_forward(1)
    second_send(1, 1)
    second_send(1, 2)
    first_forward(2)
    second_send(2, 1)
    second_send(2, 2)
    first_finish(1)
    second_send(1, 3)
    first_finish(2)
    second_send(2, 3)
    from_sibling(0)
    if COMM:
        pairs[0].wait_recv()
    own[0].wait()
    project(0)
    z_wait(2)
    assemble(3)
    first_send(3)
    for j in range(4):
        second_forward(1, j)
    assemble(4)
    second_send(3, 0)
    attend(0, 1)
    for j in range(4):
        second_finish(1, j)
        second_forward(2, j)
    first_forward(3)
    second_send(3, 1)
    second_send(3, 2)
    attend(1, 2)
    first_finish(3)
    second_send(3, 3)
    for j in range(4):
        second_finish(2, j)
    first_send(4)
    attend(2, 3)
    from_sibling(1)
    project(1)
    second_forward(3, 0)
    first_forward(4)
    attend(3, 4)
    second_send(4, 0)
    second_forward(3, 1)
    second_finish(3, 0)
    attend(4, 5)
    second_send(4, 1)
    first_finish(4)
    second_forward(3, 2)
    second_finish(3, 1)
    attend(5, 6)
    second_send(4, 2)
    second_send(4, 3)
    second_forward(3, 3)
    second_finish(3, 2)
    merge()
    if COMM:
        pairs[1].wait_recv()
    own[1].wait()
    second_finish(3, 3)
    project_eval()
    second_forward(4, 0)
    second_forward(4, 1)
    attend_eval(0)
    second_finish(4, 0)
    second_forward(4, 2)
    second_finish(4, 1)
    second_forward(4, 3)
    attend_eval(1)
    second_finish(4, 2)
    from_sibling(2)
    first_norm(mix_t, lambda at_row: x[pl.ds(pl.multiple_of(at_row, 64), 64), :], acc, norm_low, True)
    second_finish(4, 3)
    from_sibling(3)
    feed(0, norm_low, acc, True)
    from_sibling(4)
    feed(1, norm_low, acc, True)
    if COMM:
        pairs[2].wait_recv()
    own[2].wait()
    second_norm(acc, y_low, True)
    act_own = pltpu.make_async_copy(y_low.at[mine_rows], act_out.at[tp], local_sem.at[3])
    act_own.start()
    if COMM:
        act_far = remote(y_low.at[other_rows], act_out.at[tp], pair_send.at[3], pair_recv.at[3], partner)
        act_far.start()
    feed_back(0)
    feed_back(1)
    first_norm_back()
    attend_back(0, PAIRS)
    adapter_grads()
    reduce_sibling()
    ig_send[...] = input_grads(other_rows).astype(BF16)
    if COMM:
        ig_far = remote(ig_send, ig_recv, pair_send.at[4], pair_recv.at[4], partner)
        ig_far.start()
    expect(0, red_sib)
    red_sum[0] = red[half_row, :] + red_sib[...]
    if COMM:
        red_x[px] = red_sum[0]
        for h in (1, 2, 3):
            exchange(h, red_sum.at[0], red_x.at[px], device(lax.rem(px + h, 4), py, z, core))
    ig_own[...] = input_grads(mine_rows)
    grad_own = pltpu.make_async_copy(ig_own, grad_out.at[tp], local_sem.at[4])
    grad_own.start()

    def eval_rows(at_row):
        item = lax.div(at_row, HALF)
        start = pl.multiple_of(lax.rem(at_row, HALF) + tp * HALF, 64)
        return xe[item, pl.ds(start, 64), :]

    first_norm(mixe_t, eval_rows, acc_e, norm_e, False)
    if COMM:
        red_sum[1] = line_total(0, red_x, px, 4)
        red_y[py] = red_sum[1]
        for h in (1, 2, 3):
            exchange(3 + h, red_sum.at[1], red_y.at[py], device(px, lax.rem(py + h, 4), z, core))
    feed(0, norm_e, acc_e, False)
    if COMM:
        red_sum[2] = line_total(3, red_y, py, 4)
        red_z[z] = red_sum[2]
        for h in range(1, 8):
            exchange(6 + h, red_sum.at[2], red_z.at[z], device(px, py, lax.rem(z + h, 8), core))
    feed(1, norm_e, acc_e, False)
    second_norm(acc_e, qe, False)
    eval_own = pltpu.make_async_copy(qe.at[0:HALF], eval_out.at[0], local_sem.at[5])
    eval_own.start()
    eval_more = pltpu.make_async_copy(qe.at[HALF:SEQ], eval_out.at[1], local_sem.at[6])
    eval_more.start()
    if COMM:
        red_all[half_row, :] = line_total(6, red_z, z, 8)
        exchange(14, red_all.at[half_row], red_all.at[half_row], sibling)
        ig_far.wait_recv()
    ig_own2 = acc_e
    ig_own2[0:HALF, :] = ig_recv[...].astype(F32)
    if COMM:
        grad_far = pltpu.make_async_copy(ig_own2.at[0:HALF], grad_out.at[1 - tp], local_sem.at[7])
        grad_far.start()
        expect(14, red_all.at[pl.ds(pl.multiple_of((1 - core) * 8, 8), 8)])
    adapter_out[...] = red_all[...]
    for c in (act_own, grad_own, eval_own, eval_more):
        c.wait()
    if COMM:
        grad_far.wait()
        act_far.wait()
        ig_far.wait_send()
        for c in pairs:
            c.wait_send()
        for c in waits:
            c.wait_send()


def scratches():
    vm, dma = pltpu.VMEM, pltpu.SemaphoreType.DMA
    return [
        vm((16, 4, STAGED), BF16), vm((BLOCK, 1536), F32),
        vm((D, 1280), BF16), vm((D, 1280), BF16), vm((D, D), BF16), vm((D, FF), BF16), vm((D, FF), BF16),
        vm((D, 3 * D), BF16), vm((128, 2 * D), BF16),
        vm((SEQ, D), BF16), vm((2, SEQ, D), BF16), vm((SEQ, D), BF16), vm((SEQ, 128), BF16), vm((2, SEQ, 128), BF16),
        vm((SEQ, D), BF16), vm((SEQ, D), BF16), vm((SEQ, D), BF16), vm((D, SEQ), BF16),
        vm((12, SEQ, SEQ), BF16), vm((12, 1, SEQ), F32), vm((2, SEQ, SEQ), F32), vm((2, SEQ, SEQ), BF16),
        vm((SEQ, FF), BF16), vm((SEQ, D), BF16), vm((SEQ, D), F32), vm((SEQ, 1), F32),
        vm((SEQ, D), BF16), vm((SEQ, D), F32), vm((SEQ, D), BF16), vm((SEQ, 3 * D), BF16),
        vm((SEQ, D), BF16), vm((D, SEQ), BF16), vm((2, SEQ, HALF), BF16), vm((2, 1, HALF), F32),
        vm((SEQ, D), BF16), vm((SEQ, D), F32), vm((HALF, D), BF16), vm((HALF, D), BF16), vm((HALF, D), F32),
        vm((16, D), F32), vm((8, D), F32), vm((4, 8, D), F32), vm((4, 8, D), F32), vm((8, 8, D), F32),
        vm((3, 8, D), F32), vm((16, D), F32),
        dma((3, 15)), dma((3, 16)), dma((5, 20)), dma((5, 20)), dma((5, 16)), dma((5, 16)),
        dma((5,)), dma((5,)), dma((8,)), dma((15,)), dma((15,)),
    ]


def layer(lengths, staged, tokens, eval_tokens, cotangent, ups, vec):
    out = (
        jax.ShapeDtypeStruct((2, HALF, D), BF16),
        jax.ShapeDtypeStruct((2, HALF, D), F32),
        jax.ShapeDtypeStruct((2, HALF, D), BF16),
        jax.ShapeDtypeStruct((16, D), F32),
    )
    vmem, hbm = pl.BlockSpec(memory_space=pltpu.VMEM), pl.BlockSpec(memory_space=pl.ANY)
    params = dict(collective_id=0) if COMM else {}
    return pl.pallas_call(
        layer_kernel,
        out_shape=out,
        in_specs=[pl.BlockSpec(memory_space=pltpu.SMEM), vmem, hbm, hbm, hbm, vmem, vmem],
        out_specs=[hbm, hbm, hbm, vmem],
        scratch_shapes=scratches(),
        compiler_params=pltpu.CompilerParams(has_side_effects=True, vmem_limit_bytes=64 << 20, **params),
    )(lengths, staged, tokens, eval_tokens, cotangent, ups, vec)


def staged_weights(w_query, w_key, w_value, w_out, w_up, w_down, a_query, a_value):
    blank = functools.partial(jnp.zeros, dtype=BF16)
    sides = []
    for g, a in enumerate((jnp.concatenate([a_query, a_value, blank((3, 112))], axis=1), blank((3, 128)))):
        s = slice(SIDE * g, SIDE * g + SIDE)
        sides.append(jnp.concatenate([a, w_query[:, s], w_key[:, s], w_value[:, s]], axis=1))
    feed = jnp.stack([w_up, w_down.T]).reshape(2, 2, 3, 2, D)
    feed = jnp.transpose(feed, (3, 2, 1, 0, 4)).reshape(2, 3, FF)
    halves = [jnp.moveaxis(a.reshape(3, 2, -1), 1, 0) for a in (*sides, w_out)]
    return jnp.pad(jnp.concatenate([*halves, feed], axis=2), ((0, 0), (0, 1), (0, 0)))


def shards(
    tokens, eval_tokens, cotangent, lengths, w_query, w_key, w_value, w_out, w_up, w_down, a_query, a_value,
    query_up, value_up, query_bias, value_bias, bias_out, bias_up, bias_down, gain_one, shift_one, gain_two, shift_two,
):
    staged = staged_weights(w_query, w_key, w_value, w_out, w_up, w_down, a_query, a_value)
    ups = jnp.concatenate([query_up, value_up], axis=0)
    vec = jnp.concatenate(
        [query_bias, value_bias, bias_out, bias_down, gain_one, shift_one, gain_two, shift_two, bias_up]
    ).reshape(12, D).astype(F32)
    activations, input_grad, evaluated, adapter = layer(lengths, staged, tokens, eval_tokens, cotangent, ups, vec)
    return activations, input_grad, adapter[0:8], adapter[8:16], evaluated


def solution(mesh):
    rows, frozen, whole = P("dp", "tp", None), P(("dp", "tp"), None), P()
    in_specs = (rows, rows, rows, P("dp"), frozen, frozen, frozen, frozen, P("dp", "tp"), P("tp", "dp"), frozen, frozen)
    in_specs += (whole,) * 11
    out_specs = (rows, rows, whole, whole, rows)
    return jax.shard_map(shards, mesh=mesh, in_specs=in_specs, out_specs=out_specs, check_vma=False)
```

```python
import functools

import jax
import jax.numpy as jnp
from jax import lax
from jax.experimental import pallas as pl
from jax.experimental.pallas import tpu as pltpu
from jax.sharding import PartitionSpec as P

EPSILON = 1e-05
D = 768
FF = 3072
SEQ = 512
HALF = 256
BLOCK = 48
PAIRS = 6
ROWS = 256
SIDE = 384
WIDTHS = (640, 640, 384, 1536, 1536)
STARTS = (0, 640, 1280, 1664, 3200)
STAGED = 1664
DIRECT = (True, False, False, False, False)
SMALL = ((3, D),) * 4 + ((6, 1536), (1536, 6), (3, 8), (3, 8), (8, D), (8, D)) + ((D,),) * 8 + ((FF,),)
Z_PARTS = ((0, 640), (640, 1024))
MESH = pl.DeviceIdType.MESH
BF16 = jnp.bfloat16
F32 = jnp.float32
COMM = True


def dot(a, b):
    return jnp.dot(a, b, preferred_element_type=F32)


def dot_nt(a, b):
    return lax.dot_general(a, b, (((1,), (1,)), ((), ())), preferred_element_type=F32)


def dot_tn(a, b):
    return lax.dot_general(a, b, (((0,), (0,)), ((), ())), preferred_element_type=F32)


def place():
    dp, tp = lax.axis_index("dp"), lax.axis_index("tp")
    core = lax.rem(dp, 2)
    z = lax.rem(lax.div(dp, 2), 4) * 2 + tp
    y = lax.rem(lax.div(dp, 8), 4)
    x = lax.div(dp, 32)
    return x, y, z, core


def slot_of(z, core):
    return (lax.div(z, 2) * 2 + core) * 2 + lax.rem(z, 2)


def remote(src, dst, send, recv, target):
    return pltpu.make_async_remote_copy(
        src_ref=src, dst_ref=dst, send_sem=send, recv_sem=recv, device_id=target, device_id_type=MESH
    )


def by_rows(count, body, size=ROWS):
    def step(i, carry):
        body(pl.ds(pl.multiple_of(i * size, size), size), i * size)
        return carry

    lax.fori_loop(0, count // size, step, 0)


def layer_kernel(lengths, *refs):
    sources, small = refs[0:19], refs[27:46]
    tokens, eval_tokens, cotangent, act_out, grad_out, eval_out, adapter_q, adapter_v = refs[19:27]
    w_query, w_key, w_value, w_out, w_up, w_down, a_query, a_value, query_up, value_up = small[0:10]
    vec_q, vec_v, vec_o, vec_down, gain_a, shift_a, gain_b, shift_b, vec_up = small[10:19]
    (
        staged, staged_f, vec, arrived, arrived_f, packed, wa0, wa1, wo, f0, f1, mkv, umat, x, xe, cot, low, kb,
        q, k, v, mix_t, expo, inv, scores, ds, gates, hidden, xh1, rs1, norm_low, acc, y_low, dqkv,
        kv, qe, mixe_t, expo_e, inv_e, norm_e, acc_e, ig_send, ig_recv, ig_own, red, red_sib, red_x, red_y, red_z, red_sum, red_all,
        z_send, z_recv, f_send, f_recv, small_sem, xy_send, xy_recv, sib_send, sib_recv, pair_send, pair_recv, local_sem, red_send, red_recv,
    ) = refs[46:]
    fetches = [pltpu.make_async_copy(a, b, small_sem.at[n]) for n, (a, b) in enumerate(zip(sources, small))]
    for c in fetches:
        c.start()
    if COMM:
        px, py, z, core = place()
    else:
        px = py = z = core = jnp.minimum(lengths[0], 0)
    tp = lax.rem(z, 2)
    first = core == 0
    u = jnp.where(first, px, py)
    w = jnp.where(first, py, px)
    mine_rows = pl.ds(pl.multiple_of(tp * HALF, HALF), HALF)
    other_rows = pl.ds(pl.multiple_of((1 - tp) * HALF, HALF), HALF)
    def send(copy):
        if COMM:
            copy.start()

    round_u = [lax.rem(u + h, 4) for h in range(4)]
    round_w = [lax.rem(w + h, 4) for h in range(4)]
    scale_u, scale_w = jnp.where(first, 4, 1), jnp.where(first, 1, 4)
    base_dp = lax.div(z, 2) * 2 + core
    rows_u = [a * scale_u * BLOCK for a in round_u]
    rows_w = [a * scale_w * BLOCK for a in round_w]
    towards_u = [((a * scale_u + w * scale_w) * 8 + base_dp, tp) for a in round_u]
    towards_w = [((u * scale_u + a * scale_w) * 8 + base_dp, tp) for a in round_w]
    block_rows = [[pl.multiple_of(a + b, BLOCK) for b in rows_w] for a in rows_u]
    column = [(dz, dc) for dz in (4, 3, 5, 2, 6, 1, 7, 0) for dc in range(2) if (dz, dc) != (0, 0)]
    cores = (core, 1 - core)
    plane = (px * 4 + py) * 8
    round_z = [lax.rem(z + h, 8) for h in range(8)]
    along_z = [(plane + lax.div(a, 2) * 2, lax.rem(a, 2)) for a in round_z]
    sibling, partner = (along_z[0][0] + 1 - core, tp), (along_z[0][0] + core, 1 - tp)
    column_at = {(dz, dc): (along_z[dz][0] + cores[dc], along_z[dz][1]) for dz, dc in column}

    if COMM:
        greet = [column_at[d] for d in column] + towards_u[1:] + towards_w[1:]
        barrier = pltpu.get_barrier_semaphore()
        for other in greet:
            pl.semaphore_signal(barrier, inc=1, device_id=other, device_id_type=MESH)

    staged[...] = jnp.zeros_like(staged)
    staged_f[...] = jnp.zeros_like(staged_f)
    for n in (0, 1, 2, 6, 7):
        fetches[n].wait()
    low_maps = [a_query[...].astype(F32), a_value[...].astype(F32), jnp.zeros((3, 112), F32)]
    staged[0, 0:3, 0:128] = jnp.concatenate(low_maps, axis=1).astype(BF16)
    for g in range(2):
        a, b = 640 * g, SIDE * g
        staged[0, 0:3, a + 128 : a + 512] = w_query[:, b : b + SIDE]
        staged[0, 0:3, a + 512 : a + 640] = w_key[:, b : b + 128]
        staged[1, 0:3, a : a + 256] = w_key[:, b + 128 : b + SIDE]
        staged[1, 0:3, a + 256 : a + 640] = w_value[:, b : b + SIDE]

    def stage_rest():
        for n in (3, 4, 5):
            fetches[n].wait()
        diagonal = [lax.broadcasted_iota(jnp.int32, (8, 6), n) for n in range(2)]
        up = w_up[...].astype(F32)
        down = dot_nt((diagonal[0] == diagonal[1]).astype(BF16), w_down[...])
        for c in range(2):
            staged[c, 0:3, STARTS[2] : STARTS[2] + SIDE] = w_out[:, SIDE * c : SIDE * c + SIDE]
            for half in range(2):
                for which, part in enumerate((up, down)):
                    lo = half * 1536 + which * D
                    staged_f[c, 0:3, lo : lo + D] = part[3 * half : 3 * half + 3, c * D : c * D + D].astype(BF16)

    lane = lax.broadcasted_iota(jnp.int32, (1, 128), 1)
    left = lane < 64

    def prepare():
        for n in range(8, 19):
            fetches[n].wait()
        zero_u = jnp.zeros((8, SIDE), F32)
        up_q, up_v = query_up[...].astype(F32) * 2.0, value_up[...].astype(F32) * 2.0
        top = [up_q[:, 0:SIDE], zero_u, up_q[:, SIDE:D], zero_u]
        bottom = [zero_u, up_v[:, 0:SIDE], zero_u, up_v[:, SIDE:D]]
        for n, ref in enumerate((vec_q, vec_v, vec_o, vec_down, gain_a, shift_a, gain_b, shift_b)):
            vec[n : n + 1, :] = ref[...].astype(F32).reshape(1, D)
        for n in range(4):
            vec[8 + n : 9 + n, :] = vec_up[n * D : n * D + D].astype(F32).reshape(1, D)
        umat[...] = jnp.concatenate(
            [jnp.concatenate(top, axis=1), jnp.concatenate(bottom, axis=1), jnp.zeros((112, 2 * D), F32)], axis=0
        ).astype(BF16)
        for item in range(2):
            position = lax.broadcasted_iota(jnp.int32, (SEQ, 128), 0)
            kb[item] = jnp.where(position < lengths[item], 0.0, -1e30).astype(BF16)

    if COMM:
        pl.semaphore_wait(barrier, len(greet))

    mine = slot_of(z, core)

    def z_copy(part, n):
        dz, dc = column[n]
        lo, width = Z_PARTS[part]
        return remote(
            staged.at[cores[dc], :, pl.ds(lo, width)], arrived.at[mine, :, pl.ds(lo, width)],
            z_send.at[part], z_recv.at[part], column_at[dz, dc],
        )

    def z_wait(part):
        if not COMM:
            return
        z_all(part).wait_recv()

    def z_all(part):
        lo, width = Z_PARTS[part]
        whole = arrived.at[pl.ds(0, 15), :, pl.ds(lo, width)]
        return remote(whole, whole, z_send.at[part], z_recv.at[part], partner)

    pair_at = lax.div(z, 2)
    ahead_z = (jnp.where(tp == 0, along_z[7][0], along_z[1][0]) + core, 1 - tp)
    pair_q = lax.rem(pair_at + jnp.where(tp == 0, 3, 1), 4)
    pair_p = lax.rem(pair_at + jnp.where(tp == 0, 1, 3), 4)
    pair_far = lax.rem(pair_at + 2, 4)

    def four(n):
        return arrived_f.at[pl.ds(pl.multiple_of(n * 4, 4), 4)]

    def two(zz):
        return arrived_f.at[pl.ds(pl.multiple_of(zz * 2, 2), 2)]

    def column_copy(n):
        if n == 0:
            src, dst = staged_f.at[1 - core], arrived_f.at[z * 2 + core]
        else:
            src = dst = (None, two(z), four(pair_at), four(pair_q), four(pair_p))[n]
        return remote(src, dst, f_send.at[n], f_recv.at[n], (sibling, partner, ahead_z, partner, ahead_z)[n])

    def column_send(n):
        if n == 0:
            arrived_f[pl.ds(z * 2 + core, 1)] = staged_f[pl.ds(core, 1)]
        send(column_copy(n))

    def column_take(n):
        far_z = z + 1 - 2 * tp
        dst = (arrived_f.at[z * 2 + 1 - core], two(far_z), four(pair_q), four(pair_p), four(pair_far))[n]
        if COMM:
            remote(dst, dst, f_send.at[n], f_recv.at[n], partner).wait_recv()

    def column_step(n):
        column_take(n - 1)
        column_send(n)

    groups = [(ref, width, pl.multiple_of(core * width, 128)) for ref, width in zip((wa0, wa1, wo, f0, f1), WIDTHS)]

    def region(g, uu, ww, part=None):
        ref, width, lo = groups[g]
        cut = (width // 128 + 1) // 2 * 128
        if part == 0:
            width = cut
        elif part == 1:
            lo, width = pl.multiple_of(lo + cut, 128), width - cut
        return ref.at[pl.ds(block_rows[uu][ww], BLOCK), pl.ds(lo, width)]

    steps = (0, 3, 1, 2)

    def xy(g, n, r, target):
        send(remote(r, r, xy_send.at[g], xy_recv.at[g, n], target))

    def take(g, n, r):
        if COMM:
            remote(r, r, xy_send.at[g], xy_recv.at[g, n], partner).wait_recv()

    def to_sibling(g, j, i):
        r = region(g, steps[j], steps[i])
        send(remote(r, r, sib_send.at[g], sib_recv.at[g], sibling))

    def half_of(g, rows, other=False):
        ref, width, lo = groups[g]
        if other:
            lo = pl.multiple_of((1 - core) * width, 128)
        return ref.at[pl.ds(0, rows), pl.ds(lo, width)]

    def from_sibling(g):
        if COMM:
            r = half_of(g, D, True)
            remote(r, r, sib_send.at[g], sib_recv.at[g], partner).wait_recv()

    def all_sent(g):
        if COMM:
            r = half_of(g, 15 * BLOCK)
            remote(r, r, xy_send.at[g], xy_recv.at[g, 0], partner).wait_send()
            r = half_of(g, D)
            remote(r, r, sib_send.at[g], sib_recv.at[g], partner).wait_send()

    def line_send(g, base, uu, ww, ahead):
        r = region(g, uu, ww)
        xy(g, base, r, ahead(1))
        xy(g, base + 1, r, ahead(3))
        if DIRECT[g]:
            xy(g, base + 2, r, ahead(2))

    def line_forward(g, base, behind, before, ahead):
        take(g, base, behind())
        if not DIRECT[g]:
            xy(g, base + 2, behind(0), ahead(1))
        take(g, base + 1, before())
        if not DIRECT[g]:
            xy(g, base + 3, before(1), ahead(3))

    def line_finish(g, base, far):
        if DIRECT[g]:
            take(g, base + 2, far())
        else:
            take(g, base + 2, far(0))
            take(g, base + 3, far(1))

    def along_u(h):
        return towards_u[h]

    def along_w(h):
        return towards_w[h]

    def first_send(g):
        r = region(g, 0, 0)
        for n, h in enumerate((1, 3, 2)):
            xy(g, n, r, along_u(h))

    def second_send(g, j):
        line_send(g, 4 + 4 * j, steps[j], 0, along_w)
        to_sibling(g, j, 0)

    def second_forward(g, j):
        uu = steps[j]
        line_forward(
            g, 4 + 4 * j, lambda part=None: region(g, uu, 3, part), lambda part=None: region(g, uu, 1, part),
            along_w,
        )
        to_sibling(g, j, 1)
        to_sibling(g, j, 2)

    def second_finish(g, j):
        line_finish(g, 4 + 4 * j, lambda part=None: region(g, steps[j], 2, part))
        to_sibling(g, j, 3)

    def begin(g):
        first_send(g)
        second_send(g, 0)

    def widen(g, js=(1, 2, 3)):
        for j in js:
            take(g, j - 1, region(g, steps[j], 0))
            second_send(g, j)

    def relay(g, js=(0, 1, 2, 3)):
        for j in js:
            second_forward(g, j)

    def finish(g, js=(0, 1, 2, 3)):
        for j in js:
            second_finish(g, j)

    here = pl.ds(block_rows[0][0], BLOCK)

    def assemble(g):
        ref, width, lo = groups[g]
        for s in range(16):
            if g < 3:
                packed[3 * s : 3 * s + 3, 0:width] = arrived[s, 0:3, STARTS[g] : STARTS[g] + width].astype(F32)
            elif s // 2 % 2 == g - 3:
                for half in range(2):
                    row, src = (s // 4 * 2 + s % 2) * 6 + half * 3, half * 1536
                    packed[row : row + 3, :] = arrived_f[s, 0:3, src : src + 1536].astype(F32)
        ref[here, pl.ds(lo, width)] = packed[:, 0:width].astype(BF16)


    def row(n):
        return vec[n : n + 1, :]

    def project(g):
        wa = (wa0, wa1)[g]
        side = slice(SIDE * g, SIDE * g + SIDE)
        for half in range(2):
            r = slice(HALF * half, HALF * half + HALF)
            got = dot(x[r, :], wa[...])
            if g == 0:
                low[r, :] = got[:, 0:128].astype(BF16)
            more = dot(low[r, :], umat[:, D * g : D * g + D])
            q[r, side] = ((got[:, 128:512] + more[:, 0:SIDE] + row(0)[:, side]) * 0.125).astype(BF16)
            k[r, side] = got[:, 512:896].astype(BF16)
            v[r, side] = (got[:, 896:1280] + more[:, SIDE:D] + row(1)[:, side]).astype(BF16)

    def merge():
        for g, wa in enumerate((wa0, wa1)):
            more = dot(wa0[:, 0:128], umat[:, D * g : D * g + D])
            side = SIDE * g
            mkv[:, side : side + SIDE] = (wa[:, 128:512].astype(F32) + more[:, 0:SIDE]).astype(BF16)
            mkv[:, D + side : D + side + SIDE] = wa[:, 512:896]
            mkv[:, 2 * D + side : 2 * D + side + SIDE] = (wa[:, 896:1280].astype(F32) + more[:, SIDE:D]).astype(BF16)

    def project_eval(item):
        for half in range(2):
            r = slice(HALF * half, HALF * half + HALF)
            got = dot(xe[item, r, :], mkv[:, D : 3 * D])
            kv[r, 0:D] = got[:, 0:D].astype(BF16)
            kv[r, D : 2 * D] = (got[:, D:] + row(1)).astype(BF16)
        own = dot(xe[item, mine_rows, :], mkv[:, 0:D])
        qe[HALF * item : HALF * item + HALF, :] = ((own + row(0)) * 0.125).astype(BF16)

    def heads(k2, q2, bias):
        for h in range(2):
            keep = left if h == 0 else lane >= 64
            spare = lane == (64 if h == 0 else 0)
            kh = jnp.where(keep, k2, jnp.where(spare, bias, jnp.zeros_like(bias)))
            yield h, kh, jnp.where(spare, jnp.ones_like(q2), q2)

    def softmax(s_ref, queries, e_ref, inverse):
        for c in range(0, queries, 256):
            s = s_ref[:, c : c + 256]
            e = jnp.exp(s - jnp.max(s, axis=0, keepdims=True))
            inverse[:, c : c + 256] = 1.0 / jnp.sum(e, axis=0, keepdims=True)
            e_ref[:, c : c + 256] = e.astype(BF16)

    def attend(lo, hi):
        def pair(p, carry):
            s = pl.ds(pl.multiple_of(p * 128, 128), 128)
            v2t = jnp.transpose(v[:, s])
            for h, kh, qh in heads(k[:, s], q[:, s], kb[tp]):
                scores[h] = dot_nt(kh, qh)
            for h in range(2):
                n = 2 * p + h
                softmax(scores.at[h], SEQ, expo.at[n], inv.at[n])
                o = dot(v2t[64 * h : 64 * h + 64, :], expo[n]) * inv[n]
                mix_t[pl.ds(pl.multiple_of(p * 128 + 64 * h, 64), 64), :] = o.astype(BF16)
            return carry

        lax.fori_loop(lo, hi, pair, 0)

    def attend_eval(item):
        own = slice(HALF * item, HALF * item + HALF)

        def pairs_of(step, carry):
            turned = []
            for i in range(2):
                p = 2 * step + i
                s = pl.ds(pl.multiple_of(p * 128, 128), 128)
                ks = s
                vs = pl.ds(pl.multiple_of(D + p * 128, 128), 128)
                turned.append(jnp.transpose(kv[:, vs]))
                for h, kh, qh in heads(kv[:, ks], qe[own, s], kb[item]):
                    scores[i, :, HALF * h : HALF * h + HALF] = dot_nt(kh, qh)
            for i in range(2):
                p = 2 * step + i
                for h in range(2):
                    n = 2 * i + h
                    softmax(scores.at[i, :, pl.ds(HALF * h, HALF)], HALF, expo_e.at[n], inv_e.at[n])
                    o = dot(turned[i][64 * h : 64 * h + 64, :], expo_e[n]) * inv_e[n]
                    mixe_t[pl.ds(pl.multiple_of(p * 128 + 64 * h, 64), 64), own] = o.astype(BF16)
            return carry

        lax.fori_loop(0, PAIRS // 2, pairs_of, 0)

    def mean(a):
        return jnp.sum(a, axis=-1, keepdims=True) * (1.0 / D)

    def normalise(a):
        centred = a - mean(a)
        scale = lax.rsqrt(mean(centred * centred) + EPSILON)
        return centred * scale, scale

    def first_norm(mixed, base, total, low_ref, keep):
        total[...] = dot_tn(mixed[...], wo[...])

        def body(r, at_row):
            xhat, scale = normalise(total[r, :] + base(at_row).astype(F32) + row(2))
            if keep:
                xh1[r, :] = xhat
                rs1[r, :] = scale
            normed = xhat * row(4) + row(5)
            low_ref[r, :] = normed.astype(BF16)
            total[r, :] = normed + row(3)

        by_rows(SEQ, body)

    def feed(part, low_ref, total, keep):
        f = (f0, f1)[part]
        for c in range(2):
            n = 2 * part + c
            bias = row(8 + n)
            for half in range(2):
                r = slice(HALF * half, HALF * half + HALF)
                pre = dot(low_ref[r, :], f[:, 1536 * c : 1536 * c + D]) + bias
                phi = 0.5 + 0.5 * lax.erf(pre * 0.7071067811865476)
                hidden[r, :] = (pre * phi).astype(BF16)
                if keep:
                    slope = phi + pre * (0.3989422804014327 * jnp.exp(pre * pre * -0.5))
                    gates[r, D * n : D * n + D] = slope.astype(BF16)
                total[r, :] += dot_nt(hidden[r, :], f[:, 1536 * c + D : 1536 * c + 2 * D])

    def feed_back(part):
        f = (f0, f1)[part]
        for c in range(2):
            n = 2 * part + c
            for half in range(2):
                r = slice(HALF * half, HALF * half + HALF)
                g = dot(norm_low[r, :], f[:, 1536 * c + D : 1536 * c + 2 * D])
                hidden[r, :] = (g * gates[r, D * n : D * n + D].astype(F32)).astype(BF16)
                acc[r, :] += dot_nt(hidden[r, :], f[:, 1536 * c : 1536 * c + D])

    def second_norm(total, out, backward):
        def body(r, at_row):
            xhat, scale = normalise(total[r, :])
            out[r, :] = (xhat * row(6) + row(7)).astype(BF16)
            if backward:
                position = lax.broadcasted_iota(jnp.int32, (ROWS, 1), 0) + at_row
                c = jnp.where(position < lengths[tp], cot[r, :].astype(F32), 0.0) * row(6)
                g = (c - mean(c) - xhat * mean(c * xhat)) * scale
                total[r, :] = g
                norm_low[r, :] = g.astype(BF16)

        by_rows(SEQ, body)

    def first_norm_back():
        def body(r, at_row):
            c = acc[r, :] * row(4)
            xhat = xh1[r, :]
            g = (c - mean(c) - xhat * mean(c * xhat)) * rs1[r, :]
            acc[r, :] = g
            norm_low[r, :] = g.astype(BF16)

        by_rows(SEQ, body)
        g = dot_nt(wo[...], norm_low[...])
        for n in range(12):
            mix_t[64 * n : 64 * n + 64, :] = (g[64 * n : 64 * n + 64, :] * inv[n]).astype(BF16)

    def attend_back(lo, hi):
        def pair(p, carry):
            def lanes(section):
                return pl.ds(pl.multiple_of(D * section + p * 128, 128), 128)

            s = lanes(0)
            k2, q2, v2 = k[:, s], q[:, s], v[:, s]
            k2t = jnp.transpose(k2)
            g2t = mix_t[pl.ds(pl.multiple_of(p * 128, 128), 128), :]
            for h in range(2):
                keep = left if h == 0 else lane >= 64
                scores[h] = dot(jnp.where(keep, v2, jnp.zeros_like(v2)), g2t)
            dq, dk, dv = [], [], []
            for h in range(2):
                n = 2 * p + h
                for c in range(0, SEQ, 256):
                    e = expo[n, :, c : c + 256].astype(F32)
                    g = scores[h, :, c : c + 256]
                    inner = jnp.sum(e * g, axis=0, keepdims=True) * inv[n, :, c : c + 256]
                    ds[h, :, c : c + 256] = (e * (g - inner)).astype(BF16)
                dq.append(dot(k2t[64 * h : 64 * h + 64, :], ds[h]))
                dk.append(dot(ds[h], q2))
                dv.append(dot_nt(expo[n], g2t))
            dqkv[:, s] = (jnp.transpose(jnp.concatenate(dq, axis=0)) * 0.125).astype(BF16)
            dqkv[:, lanes(1)] = jnp.where(left, dk[0], dk[1]).astype(BF16)
            dqkv[:, lanes(2)] = jnp.where(left, dv[0], dv[1]).astype(BF16)
            return carry

        lax.fori_loop(lo, hi, pair, 0)

    def adapter_grads():
        red[0:8, :] = dot_tn(low[...], dqkv[:, 0:D])[0:8, :] * 2.0
        red[8:16, :] = dot_tn(low[...], dqkv[:, 2 * D :])[8:16, :] * 2.0

    def input_grads(r):
        return acc[r, :] + dot_nt(dqkv[r, :], mkv[...])


    along_x = [(jnp.where(first, a[0], b[0]), tp) for a, b in zip(towards_u, towards_w)]
    along_y = [(jnp.where(first, b[0], a[0]), tp) for a, b in zip(towards_u, towards_w)]

    half_row = pl.ds(pl.multiple_of(core * 8, 8), 8)

    def exchange(n, src, dst, target):
        send(remote(src, dst, red_send.at[0], red_recv.at[n], target))

    def expect(n, dst):
        if COMM:
            remote(dst, dst, red_send.at[0], red_recv.at[n], partner).wait_recv()

    def line_total(n, buffer, count):
        expect(n, buffer.at[pl.ds(0, count - 1)])
        total = buffer[0]
        for h in range(1, count):
            total = total + buffer[h]
        return total


    start = pl.multiple_of(tp * HALF, HALF)
    pairs = [
        remote(tokens.at[1 - tp, 0:128], x.at[pl.ds(start, 128)], pair_send.at[0], pair_recv.at[0], partner),
        remote(eval_tokens.at[0], xe.at[0, mine_rows], pair_send.at[1], pair_recv.at[1], partner),
        remote(eval_tokens.at[1], xe.at[1, mine_rows], pair_send.at[2], pair_recv.at[2], partner),
        remote(cotangent.at[1 - tp], cot.at[mine_rows], pair_send.at[3], pair_recv.at[3], partner),
        remote(y_low.at[other_rows], act_out.at[tp], pair_send.at[4], pair_recv.at[4], partner),
        remote(ig_send, ig_recv, pair_send.at[5], pair_recv.at[5], partner),
        remote(tokens.at[1 - tp, 128:HALF], x.at[pl.ds(start + 128, 128)], pair_send.at[6], pair_recv.at[6], partner),
    ]

    def pair_start(n):
        if COMM:
            pairs[n].start()

    def pair_wait(n):
        if COMM:
            pairs[n].wait_recv()

    own = [
        pltpu.make_async_copy(tokens.at[tp], x.at[mine_rows], local_sem.at[0]),
        pltpu.make_async_copy(eval_tokens, xe.at[:, mine_rows], local_sem.at[1]),
        pltpu.make_async_copy(cotangent.at[tp], cot.at[mine_rows], local_sem.at[2]),
    ]
    for c in own:
        c.start()

    def eval_rows(at_row):
        item = lax.div(at_row, HALF)
        start = pl.multiple_of(lax.rem(at_row, HALF) + tp * HALF, ROWS)
        return xe[item, pl.ds(start, ROWS), :]

    def z_start(part):
        for n in range(15):
            send(z_copy(part, n))

    z_start(0)
    stage_rest()
    column_send(0)
    arrived[pl.ds(mine, 1)] = staged[pl.ds(core, 1)]
    z_start(1)
    prepare()
    column_step(1)
    z_wait(0)
    assemble(0)
    begin(0)
    pair_start(0)
    column_step(2)
    z_wait(1)
    assemble(1)
    assemble(2)
    widen(0)
    begin(1)
    column_step(3)
    pair_start(6)
    pair_start(1)
    pair_start(2)
    pair_start(3)
    relay(0)
    widen(1)
    finish(0)
    begin(2)
    column_step(4)
    from_sibling(0)
    pair_wait(0)
    pair_wait(6)
    own[0].wait()
    project(0)
    relay(1)
    widen(2)
    column_take(4)
    assemble(3)
    begin(3)
    attend(0, 1)
    attend(1, 2)
    finish(1)
    relay(2)
    attend(2, 3)
    widen(3)
    from_sibling(1)
    project(1)
    finish(2)
    attend(3, 4)
    relay(3, (0,))
    attend(4, 5)
    assemble(4)
    pass
    attend(5, 6)
    relay(3, (1,))
    merge()
    from_sibling(2)
    first_norm(mix_t, lambda at_row: x[pl.ds(pl.multiple_of(at_row, ROWS), ROWS), :], acc, norm_low, True)
    relay(3, (2, 3))
    begin(4)
    pair_wait(1)
    own[1].wait()
    project_eval(0)
    finish(3, (0, 1))
    attend_eval(0)
    widen(4)
    finish(3, (2, 3))
    from_sibling(3)
    feed(0, norm_low, acc, True)
    relay(4, (0, 1))
    pair_wait(2)
    project_eval(1)
    relay(4, (2, 3))
    attend_eval(1)
    finish(4, (0, 1))
    first_norm(mixe_t, eval_rows, acc_e, norm_e, False)
    finish(4, (2, 3))
    from_sibling(4)
    feed(1, norm_low, acc, True)
    pair_wait(3)
    own[2].wait()
    second_norm(acc, y_low, True)
    act_own = pltpu.make_async_copy(y_low.at[mine_rows], act_out.at[tp], local_sem.at[3])
    act_own.start()
    pair_start(4)
    feed_back(0)
    feed_back(1)
    first_norm_back()
    attend_back(0, PAIRS)
    adapter_grads()
    exchange(0, red.at[pl.ds(pl.multiple_of((1 - core) * 8, 8), 8)], red_sib, sibling)
    ig_send[...] = input_grads(other_rows).astype(BF16)
    pair_start(5)
    expect(0, red_sib)
    red_sum[0] = red[half_row, :] + red_sib[...]
    if COMM:
        red_x[px] = red_sum[0]
        for target in along_x[1:]:
            exchange(1, red_sum.at[0], red_x.at[px], target)
    ig_own[...] = input_grads(mine_rows)
    grad_own = pltpu.make_async_copy(ig_own, grad_out.at[tp], local_sem.at[4])
    grad_own.start()

    if COMM:
        red_sum[1] = line_total(1, red_x, 4)
        red_y[py] = red_sum[1]
        for target in along_y[1:]:
            exchange(2, red_sum.at[1], red_y.at[py], target)
    feed(0, norm_e, acc_e, False)
    if COMM:
        red_sum[2] = line_total(2, red_y, 4)
        red_z[z] = red_sum[2]
        for h in range(1, 8):
            exchange(3, red_sum.at[2], red_z.at[z], column_at[h, 0])
    feed(1, norm_e, acc_e, False)
    second_norm(acc_e, qe, False)
    eval_own = pltpu.make_async_copy(qe.at[0:HALF], eval_out.at[0], local_sem.at[5])
    eval_own.start()
    eval_more = pltpu.make_async_copy(qe.at[HALF:SEQ], eval_out.at[1], local_sem.at[6])
    eval_more.start()
    pair_wait(5)
    acc_e[0:HALF, :] = ig_recv[...].astype(F32)
    grad_far = pltpu.make_async_copy(acc_e.at[0:HALF], grad_out.at[1 - tp], local_sem.at[7])
    grad_far.start()
    if COMM:
        red_all[half_row, :] = line_total(3, red_z, 8)
        exchange(4, red_all.at[half_row], red_all.at[half_row], sibling)
        expect(4, red_all.at[pl.ds(pl.multiple_of((1 - core) * 8, 8), 8)])
    sums = [pltpu.make_async_copy(red_all.at[0:8], adapter_q, local_sem.at[8])]
    sums.append(pltpu.make_async_copy(red_all.at[8:16], adapter_v, local_sem.at[9]))
    for c in sums:
        c.start()
    for c in (act_own, grad_own, eval_own, eval_more, grad_far, *sums):
        c.wait()
    pair_wait(4)
    if COMM:
        for c in pairs:
            c.wait_send()
        for part in range(2):
            z_all(part).wait_send()
        for n in range(5):
            column_copy(n).wait_send()
            all_sent(n)
        everything = acc_e.at[pl.ds(0, 15 * 8)]
        remote(everything, everything, red_send.at[0], red_recv.at[0], partner).wait_send()


def scratches():
    vm, dma = pltpu.VMEM, pltpu.SemaphoreType.DMA
    return [
        *(vm(shape, BF16) for shape in SMALL),
        vm((2, 4, STAGED), BF16), vm((2, 4, FF), BF16), vm((12, D), F32),
        vm((16, 4, STAGED), BF16), vm((16, 4, FF), BF16), vm((BLOCK, 1536), F32),
        vm((D, 1280), BF16), vm((D, 1280), BF16), vm((D, D), BF16), vm((D, FF), BF16), vm((D, FF), BF16),
        vm((D, 3 * D), BF16), vm((128, 2 * D), BF16),
        vm((SEQ, D), BF16), vm((2, SEQ, D), BF16), vm((SEQ, D), BF16), vm((SEQ, 128), BF16), vm((2, SEQ, 128), BF16),
        vm((SEQ, D), BF16), vm((SEQ, D), BF16), vm((SEQ, D), BF16), vm((D, SEQ), BF16),
        vm((12, SEQ, SEQ), BF16), vm((12, 1, SEQ), F32), vm((2, SEQ, SEQ), F32), vm((2, SEQ, SEQ), BF16),
        vm((SEQ, FF), BF16), vm((SEQ, D), BF16), vm((SEQ, D), F32), vm((SEQ, 1), F32),
        vm((SEQ, D), BF16), vm((SEQ, D), F32), vm((SEQ, D), BF16), vm((SEQ, 3 * D), BF16),
        vm((SEQ, 2 * D), BF16), vm((SEQ, D), BF16), vm((D, SEQ), BF16), vm((4, SEQ, HALF), BF16), vm((4, 1, HALF), F32),
        vm((SEQ, D), BF16), vm((SEQ, D), F32), vm((HALF, D), BF16), vm((HALF, D), BF16), vm((HALF, D), F32),
        vm((16, D), F32), vm((8, D), F32), vm((4, 8, D), F32), vm((4, 8, D), F32), vm((8, 8, D), F32),
        vm((3, 8, D), F32), vm((16, D), F32),
        dma((2,)), dma((2,)), dma((5,)), dma((5,)), dma((19,)), dma((5,)), dma((5, 20)), dma((5,)), dma((5,)),
        dma((7,)), dma((7,)), dma((10,)), dma((1,)), dma((5,)),
    ]


def layer(*operands):
    out = (
        jax.ShapeDtypeStruct((2, HALF, D), BF16),
        jax.ShapeDtypeStruct((2, HALF, D), F32),
        jax.ShapeDtypeStruct((2, HALF, D), BF16),
        jax.ShapeDtypeStruct((8, D), F32),
        jax.ShapeDtypeStruct((8, D), F32),
    )
    hbm = pl.BlockSpec(memory_space=pl.ANY)
    params = dict(collective_id=0) if COMM else {}
    return pl.pallas_call(
        layer_kernel,
        out_shape=out,
        in_specs=[pl.BlockSpec(memory_space=pltpu.SMEM)] + [hbm] * 22,
        out_specs=[hbm] * 5,
        scratch_shapes=scratches(),
        compiler_params=pltpu.CompilerParams(has_side_effects=True, vmem_limit_bytes=64 << 20, **params),
    )(*operands)


def shards(tokens, eval_tokens, cotangent, lengths, *rest):
    frozen, ups, (query_bias, value_bias, bias_out, bias_up, bias_down, *norms) = rest[0:8], rest[8:10], rest[10:]
    vectors = (query_bias, value_bias, bias_out, bias_down, *norms, bias_up)
    activations, input_grad, evaluated, grad_q, grad_v = layer(
        lengths, *frozen, *ups, *vectors, tokens, eval_tokens, cotangent
    )
    return activations, input_grad, grad_q, grad_v, evaluated


def solution(mesh):
    rows, frozen, whole = P("dp", "tp", None), P(("dp", "tp"), None), P()
    in_specs = (rows, rows, rows, P("dp"), frozen, frozen, frozen, frozen, P("dp", "tp"), P("tp", "dp"), frozen, frozen)
    in_specs += (whole,) * 11
    out_specs = (rows, rows, whole, whole, rows)
    return jax.shard_map(shards, mesh=mesh, in_specs=in_specs, out_specs=out_specs, check_vma=False)
```

```python
import functools

import jax
import jax.numpy as jnp
from jax import lax
from jax.experimental import pallas as pl
from jax.experimental.pallas import tpu as pltpu
from jax.sharding import PartitionSpec as P

EPSILON = 1e-05
D = 768
FF = 3072
SEQ = 512
HALF = 256
BLOCK = 48
PAIRS = 6
LIMIT = 60
ROWS = 256
SIDE = 384
WIDTHS = (640, 640, 384, 1536, 1536)
STARTS = (0, 640, 1280, 1664, 3200)
STAGED = 1664
DIRECT = (True, False, False, False, False)
SMALL = ((3, D),) * 4 + ((6, 1536), (6, 1536), (3, 8), (3, 8), (8, D), (8, D)) + ((D,),) * 8 + ((FF,),)
Z_PARTS = ((0, 640), (640, 1024))
MESH = pl.DeviceIdType.MESH
BF16 = jnp.bfloat16
F32 = jnp.float32
COMM = True


def dot(a, b):
    return jnp.dot(a, b, preferred_element_type=F32)


def dot_nt(a, b):
    return lax.dot_general(a, b, (((1,), (1,)), ((), ())), preferred_element_type=F32)


def dot_tn(a, b):
    return lax.dot_general(a, b, (((0,), (0,)), ((), ())), preferred_element_type=F32)


def place():
    dp, tp = lax.axis_index("dp"), lax.axis_index("tp")
    core = lax.rem(dp, 2)
    z = lax.rem(lax.div(dp, 2), 4) * 2 + tp
    y = lax.rem(lax.div(dp, 8), 4)
    x = lax.div(dp, 32)
    return x, y, z, core


def slot_of(z, core):
    return (lax.div(z, 2) * 2 + core) * 2 + lax.rem(z, 2)


def remote(src, dst, send, recv, target):
    return pltpu.make_async_remote_copy(
        src_ref=src, dst_ref=dst, send_sem=send, recv_sem=recv, device_id=target, device_id_type=MESH
    )


def by_rows(count, body, size=ROWS):
    def step(i, carry):
        body(pl.ds(pl.multiple_of(i * size, size), size), i * size)
        return carry

    lax.fori_loop(0, count // size, step, 0)


def layer_kernel(lengths, *refs):
    sources, small = refs[0:19], refs[27:46]
    tokens, eval_tokens, cotangent, act_out, grad_out, eval_out, adapter_q, adapter_v = refs[19:27]
    w_query, w_key, w_value, w_out, w_up, w_down, a_query, a_value, query_up, value_up = small[0:10]
    vec_q, vec_v, vec_o, vec_down, gain_a, shift_a, gain_b, shift_b, vec_up = small[10:19]
    (
        staged, staged_f, vec, arrived, arrived_f, packed, wa0, wa1, wo, f0, f1, mkv, umat, x, xe, cot, low, kb,
        q, k, v, mix_t, expo, inv, scores, ds, gates, hidden, xh1, rs1, norm_low, acc, y_low, dqkv,
        kv, qe, mixe_t, expo_e, inv_e, norm_e, acc_e, ig_send, ig_recv, red, red_sib, red_x, red_y, red_z, red_sum, red_all,
        z_send, z_recv, f_send, f_recv, small_sem, xy_send, xy_recv, sib_send, sib_recv, pair_send, pair_recv, local_sem, red_send, red_recv,
    ) = refs[46:]
    fetches = [pltpu.make_async_copy(a, b, small_sem.at[n]) for n, (a, b) in enumerate(zip(sources, small))]
    for c in fetches:
        c.start()
    if COMM:
        px, py, z, core = place()
    else:
        px = py = z = core = jnp.minimum(lengths[0], 0)
    tp = lax.rem(z, 2)
    first = core == 0
    u = jnp.where(first, px, py)
    w = jnp.where(first, py, px)
    mine_rows = pl.ds(pl.multiple_of(tp * HALF, HALF), HALF)
    other_rows = pl.ds(pl.multiple_of((1 - tp) * HALF, HALF), HALF)
    def send(copy):
        if COMM:
            copy.start()

    round_u = [lax.rem(u + h, 4) for h in range(4)]
    round_w = [lax.rem(w + h, 4) for h in range(4)]
    scale_u, scale_w = jnp.where(first, 4, 1), jnp.where(first, 1, 4)
    base_dp = lax.div(z, 2) * 2 + core
    rows_u = [a * scale_u * BLOCK for a in round_u]
    rows_w = [a * scale_w * BLOCK for a in round_w]
    towards_u = [((a * scale_u + w * scale_w) * 8 + base_dp, tp) for a in round_u]
    towards_w = [((u * scale_u + a * scale_w) * 8 + base_dp, tp) for a in round_w]
    block_rows = [[pl.multiple_of(a + b, BLOCK) for b in rows_w] for a in rows_u]
    column = [(dz, dc) for dz in (4, 3, 5, 2, 6, 1, 7, 0) for dc in range(2) if (dz, dc) != (0, 0)]
    cores = (core, 1 - core)
    plane = (px * 4 + py) * 8
    round_z = [lax.rem(z + h, 8) for h in range(8)]
    along_z = [(plane + lax.div(a, 2) * 2, lax.rem(a, 2)) for a in round_z]
    sibling, partner = (along_z[0][0] + 1 - core, tp), (along_z[0][0] + core, 1 - tp)
    column_at = {(dz, dc): (along_z[dz][0] + cores[dc], along_z[dz][1]) for dz, dc in column}

    if COMM:
        greet = [column_at[d] for d in column] + towards_u[1:] + towards_w[1:]
        barrier = pltpu.get_barrier_semaphore()
        for other in greet:
            pl.semaphore_signal(barrier, inc=1, device_id=other, device_id_type=MESH)

    staged[...] = jnp.zeros_like(staged)
    staged_f[...] = jnp.zeros_like(staged_f)
    for n in (0, 1, 2, 6, 7):
        fetches[n].wait()
    low_maps = [a_query[...].astype(F32), a_value[...].astype(F32), jnp.zeros((3, 112), F32)]
    staged[0, 0:3, 0:128] = jnp.concatenate(low_maps, axis=1).astype(BF16)
    for g in range(2):
        a, b = 640 * g, SIDE * g
        staged[0, 0:3, a + 128 : a + 512] = w_query[:, b : b + SIDE]
        staged[0, 0:3, a + 512 : a + 640] = w_key[:, b : b + 128]
        staged[1, 0:3, a : a + 256] = w_key[:, b + 128 : b + SIDE]
        staged[1, 0:3, a + 256 : a + 640] = w_value[:, b : b + SIDE]

    def stage_rest():
        for n in (3, 4, 5):
            fetches[n].wait()
        up, down = w_up[...].astype(F32), w_down[...].astype(F32)
        for c in range(2):
            staged[c, 0:3, STARTS[2] : STARTS[2] + SIDE] = w_out[:, SIDE * c : SIDE * c + SIDE]
            for half in range(2):
                for which, part in enumerate((up, down)):
                    lo = half * 1536 + which * D
                    staged_f[c, 0:3, lo : lo + D] = part[3 * half : 3 * half + 3, c * D : c * D + D].astype(BF16)

    lane = lax.broadcasted_iota(jnp.int32, (1, 128), 1)
    left = lane < 64

    def prepare():
        for n in range(8, 19):
            fetches[n].wait()
        zero_u = jnp.zeros((8, SIDE), F32)
        up_q, up_v = query_up[...].astype(F32) * 2.0, value_up[...].astype(F32) * 2.0
        top = [up_q[:, 0:SIDE], zero_u, up_q[:, SIDE:D], zero_u]
        bottom = [zero_u, up_v[:, 0:SIDE], zero_u, up_v[:, SIDE:D]]
        for n, ref in enumerate((vec_q, vec_v, vec_o, vec_down, gain_a, shift_a, gain_b, shift_b)):
            vec[n : n + 1, :] = ref[...].astype(F32).reshape(1, D)
        for n in range(4):
            vec[8 + n : 9 + n, :] = vec_up[n * D : n * D + D].astype(F32).reshape(1, D)
        umat[...] = jnp.concatenate(
            [jnp.concatenate(top, axis=1), jnp.concatenate(bottom, axis=1), jnp.zeros((112, 2 * D), F32)], axis=0
        ).astype(BF16)
        for item in range(2):
            position = lax.broadcasted_iota(jnp.int32, (SEQ, 128), 0)
            kb[item] = jnp.where(position < lengths[item], 0.0, -1e30).astype(BF16)

    if COMM:
        pl.semaphore_wait(barrier, len(greet))

    mine = slot_of(z, core)

    def z_copy(part, n):
        dz, dc = column[n]
        lo, width = Z_PARTS[part]
        return remote(
            staged.at[cores[dc], :, pl.ds(lo, width)], arrived.at[mine, :, pl.ds(lo, width)],
            z_send.at[part], z_recv.at[part], column_at[dz, dc],
        )

    def z_wait(part):
        if not COMM:
            return
        z_all(part).wait_recv()

    def z_all(part):
        lo, width = Z_PARTS[part]
        whole = arrived.at[pl.ds(0, 15), :, pl.ds(lo, width)]
        return remote(whole, whole, z_send.at[part], z_recv.at[part], partner)

    pair_at = lax.div(z, 2)
    ahead_z = (jnp.where(tp == 0, along_z[7][0], along_z[1][0]) + core, 1 - tp)
    pair_q = lax.rem(pair_at + jnp.where(tp == 0, 3, 1), 4)
    pair_p = lax.rem(pair_at + jnp.where(tp == 0, 1, 3), 4)
    pair_far = lax.rem(pair_at + 2, 4)

    def four(n):
        return arrived_f.at[pl.ds(pl.multiple_of(n * 4, 4), 4)]

    def two(zz):
        return arrived_f.at[pl.ds(pl.multiple_of(zz * 2, 2), 2)]

    def column_copy(n):
        if n == 0:
            src, dst = staged_f.at[1 - core], arrived_f.at[z * 2 + core]
        else:
            src = dst = (None, two(z), four(pair_at), four(pair_q), four(pair_p))[n]
        return remote(src, dst, f_send.at[n], f_recv.at[n], (sibling, partner, ahead_z, partner, ahead_z)[n])

    def column_send(n):
        if n == 0:
            arrived_f[pl.ds(z * 2 + core, 1)] = staged_f[pl.ds(core, 1)]
        send(column_copy(n))

    def column_take(n):
        far_z = z + 1 - 2 * tp
        dst = (arrived_f.at[z * 2 + 1 - core], two(far_z), four(pair_q), four(pair_p), four(pair_far))[n]
        if COMM:
            remote(dst, dst, f_send.at[n], f_recv.at[n], partner).wait_recv()

    def column_step(n):
        column_take(n - 1)
        column_send(n)

    groups = [(ref, width, pl.multiple_of(core * width, 128)) for ref, width in zip((wa0, wa1, wo, f0, f1), WIDTHS)]

    def region(g, uu, ww, part=None):
        ref, width, lo = groups[g]
        cut = (width // 128 + 1) // 2 * 128
        if part == 0:
            width = cut
        elif part == 1:
            lo, width = pl.multiple_of(lo + cut, 128), width - cut
        return ref.at[pl.ds(block_rows[uu][ww], BLOCK), pl.ds(lo, width)]

    steps = (0, 3, 1, 2)

    def xy(g, n, r, target):
        sem = n if n < 4 else (n - 4) // 4 * 2 + 3 + n % 4 // 2
        send(remote(r, r, xy_send.at[g], xy_recv.at[g, sem], target))

    def take(g, sem, blocks):
        if COMM:
            r = half_of(g, blocks * BLOCK)
            remote(r, r, xy_send.at[g], xy_recv.at[g, sem], partner).wait_recv()

    def to_sibling(g, j, i):
        r = region(g, steps[j], steps[i])
        send(remote(r, r, sib_send.at[g], sib_recv.at[g], sibling))

    def half_of(g, rows, other=False):
        ref, width, lo = groups[g]
        if other:
            lo = pl.multiple_of((1 - core) * width, 128)
        return ref.at[pl.ds(0, rows), pl.ds(lo, width)]

    def from_sibling(g):
        if COMM:
            r = half_of(g, D, True)
            remote(r, r, sib_send.at[g], sib_recv.at[g], partner).wait_recv()

    def all_sent(g):
        if COMM:
            r = half_of(g, 15 * BLOCK)
            remote(r, r, xy_send.at[g], xy_recv.at[g, 0], partner).wait_send()
            r = half_of(g, D)
            remote(r, r, sib_send.at[g], sib_recv.at[g], partner).wait_send()

    def line_send(g, base, uu, ww, ahead):
        r = region(g, uu, ww)
        xy(g, base, r, ahead(1))
        xy(g, base + 1, r, ahead(3))
        if DIRECT[g]:
            xy(g, base + 2, r, ahead(2))

    def along_u(h):
        return towards_u[h]

    def along_w(h):
        return towards_w[h]

    def first_send(g):
        r = region(g, 0, 0)
        for n, h in enumerate((1, 3, 2)):
            xy(g, n, r, along_u(h))

    def second_send(g, j):
        line_send(g, 4 + 4 * j, steps[j], 0, along_w)
        to_sibling(g, j, 0)

    def second_forward(g, j):
        take(g, 2 * j + 3, 2)
        if not DIRECT[g]:
            xy(g, 6 + 4 * j, region(g, steps[j], 3, 0), along_w(1))
            xy(g, 7 + 4 * j, region(g, steps[j], 1, 1), along_w(3))
        to_sibling(g, j, 1)
        to_sibling(g, j, 2)

    def second_finish(g, j):
        take(g, 2 * j + 4, 1)
        to_sibling(g, j, 3)

    def begin(g):
        first_send(g)
        second_send(g, 0)

    def widen(g, js=(1, 2, 3)):
        for j in js:
            take(g, j - 1, 1)
            second_send(g, j)

    def relay(g, js=(0, 1, 2, 3)):
        for j in js:
            second_forward(g, j)

    def finish(g, js=(0, 1, 2, 3)):
        for j in js:
            second_finish(g, j)

    here = pl.ds(block_rows[0][0], BLOCK)

    def assemble(g):
        ref, width, lo = groups[g]
        for s in range(16):
            if g < 3:
                packed[3 * s : 3 * s + 3, 0:width] = arrived[s, 0:3, STARTS[g] : STARTS[g] + width].astype(F32)
            elif s // 2 % 2 == g - 3:
                for half in range(2):
                    row, src = (s // 4 * 2 + s % 2) * 6 + half * 3, half * 1536
                    packed[row : row + 3, :] = arrived_f[s, 0:3, src : src + 1536].astype(F32)
        ref[here, pl.ds(lo, width)] = packed[:, 0:width].astype(BF16)


    def row(n):
        return vec[n : n + 1, :]

    def project(g):
        wa = (wa0, wa1)[g]
        side = slice(SIDE * g, SIDE * g + SIDE)
        for half in range(2):
            r = slice(HALF * half, HALF * half + HALF)
            got = dot(x[r, :], wa[...])
            if g == 0:
                low[r, :] = got[:, 0:128].astype(BF16)
            more = dot(low[r, :], umat[:, D * g : D * g + D])
            q[r, side] = ((got[:, 128:512] + more[:, 0:SIDE] + row(0)[:, side]) * 0.125).astype(BF16)
            k[r, side] = got[:, 512:896].astype(BF16)
            v[r, side] = (got[:, 896:1280] + more[:, SIDE:D] + row(1)[:, side]).astype(BF16)

    def merge():
        for g, wa in enumerate((wa0, wa1)):
            more = dot(wa0[:, 0:128], umat[:, D * g : D * g + D])
            side = SIDE * g
            mkv[:, side : side + SIDE] = (wa[:, 128:512].astype(F32) + more[:, 0:SIDE]).astype(BF16)
            mkv[:, D + side : D + side + SIDE] = wa[:, 512:896]
            mkv[:, 2 * D + side : 2 * D + side + SIDE] = (wa[:, 896:1280].astype(F32) + more[:, SIDE:D]).astype(BF16)

    def project_eval(item):
        for half in range(2):
            r = slice(HALF * half, HALF * half + HALF)
            got = dot(xe[item, r, :], mkv[:, D : 3 * D])
            kv[r, 0:D] = got[:, 0:D].astype(BF16)
            kv[r, D : 2 * D] = (got[:, D:] + row(1)).astype(BF16)
        own = dot(xe[item, mine_rows, :], mkv[:, 0:D])
        qe[HALF * item : HALF * item + HALF, :] = ((own + row(0)) * 0.125).astype(BF16)

    def heads(k2, q2, bias):
        for h in range(2):
            keep = left if h == 0 else lane >= 64
            spare = lane == (64 if h == 0 else 0)
            kh = jnp.where(keep, k2, jnp.where(spare, bias, jnp.zeros_like(bias)))
            yield h, kh, jnp.where(spare, jnp.ones_like(q2), q2)

    def softmax(s_ref, queries, e_ref, inverse):
        for c in range(0, queries, 256):
            s = s_ref[:, c : c + 256]
            e = jnp.exp(s - jnp.max(s, axis=0, keepdims=True))
            inverse[:, c : c + 256] = 1.0 / jnp.sum(e, axis=0, keepdims=True)
            e_ref[:, c : c + 256] = e.astype(BF16)

    def attend(lo, hi):
        def pair(p, carry):
            s = pl.ds(pl.multiple_of(p * 128, 128), 128)
            v2t = jnp.transpose(v[:, s])
            for h, kh, qh in heads(k[:, s], q[:, s], kb[tp]):
                scores[h] = dot_nt(kh, qh)
            for h in range(2):
                n = 2 * p + h
                softmax(scores.at[h], SEQ, expo.at[n], inv.at[n])
                o = dot(v2t[64 * h : 64 * h + 64, :], expo[n]) * inv[n]
                mix_t[pl.ds(pl.multiple_of(p * 128 + 64 * h, 64), 64), :] = o.astype(BF16)
            return carry

        lax.fori_loop(lo, hi, pair, 0)

    def attend_eval(item, lo, hi):
        own = slice(HALF * item, HALF * item + HALF)

        def pairs_of(step, carry):
            turned = []
            for i in range(2):
                p = 2 * step + i
                s = pl.ds(pl.multiple_of(p * 128, 128), 128)
                ks = s
                vs = pl.ds(pl.multiple_of(D + p * 128, 128), 128)
                turned.append(jnp.transpose(kv[:, vs]))
                for h, kh, qh in heads(kv[:, ks], qe[own, s], kb[item]):
                    scores[i, :, HALF * h : HALF * h + HALF] = dot_nt(kh, qh)
            for i in range(2):
                p = 2 * step + i
                for h in range(2):
                    n = 2 * i + h
                    softmax(scores.at[i, :, pl.ds(HALF * h, HALF)], HALF, expo_e.at[n], inv_e.at[n])
                    o = dot(turned[i][64 * h : 64 * h + 64, :], expo_e[n]) * inv_e[n]
                    mixe_t[pl.ds(pl.multiple_of(p * 128 + 64 * h, 64), 64), own] = o.astype(BF16)
            return carry

        lax.fori_loop(lo, hi, pairs_of, 0)

    def mean(a):
        return jnp.sum(a, axis=-1, keepdims=True) * (1.0 / D)

    def normalise(a):
        centred = a - mean(a)
        scale = lax.rsqrt(mean(centred * centred) + EPSILON)
        return centred * scale, scale

    def first_norm(mixed, base, total, low_ref, keep):
        total[...] = dot_tn(mixed[...], wo[...])

        def body(r, at_row):
            xhat, scale = normalise(total[r, :] + base(at_row).astype(F32) + row(2))
            if keep:
                xh1[r, :] = xhat
                rs1[r, :] = scale
            normed = xhat * row(4) + row(5)
            low_ref[r, :] = normed.astype(BF16)
            total[r, :] = normed + row(3)

        by_rows(SEQ, body)

    def feed(part, low_ref, total, keep, parts=(0, 1)):
        f = (f0, f1)[part]

        def down(c, r):
            total[r, :] += dot_nt(hidden[c, r, :], f[:, 1536 * c + D : 1536 * c + 2 * D])

        ready = None
        for c in parts:
            n = 2 * part + c
            for half in range(2):
                r = slice(HALF * half, HALF * half + HALF)
                pre = dot(low_ref[r, :], f[:, 1536 * c : 1536 * c + D]) + row(8 + n)
                if ready:
                    down(*ready)
                phi = 0.5 + 0.5 * lax.erf(pre * 0.7071067811865476)
                hidden[c, r, :] = (pre * phi).astype(BF16)
                if keep:
                    slope = phi + pre * (0.3989422804014327 * jnp.exp(pre * pre * -0.5))
                    gates[r, D * n : D * n + D] = slope.astype(BF16)
                ready = (c, r)
        down(*ready)

    def feed_back():
        def up(n, r):
            f, c = (f0, f1)[n // 2], n % 2
            acc[r, :] += dot_nt(hidden[c, r, :], f[:, 1536 * c : 1536 * c + D])

        ready = None
        for n in range(4):
            f, c = (f0, f1)[n // 2], n % 2
            for half in range(2):
                r = slice(HALF * half, HALF * half + HALF)
                g = dot(norm_low[r, :], f[:, 1536 * c + D : 1536 * c + 2 * D])
                if ready:
                    up(*ready)
                hidden[c, r, :] = (g * gates[r, D * n : D * n + D].astype(F32)).astype(BF16)
                ready = (n, r)
        up(*ready)

    def second_norm(total, out, backward):
        def body(r, at_row):
            xhat, scale = normalise(total[r, :])
            out(at_row, (xhat * row(6) + row(7)).astype(BF16))
            if backward:
                position = lax.broadcasted_iota(jnp.int32, (ROWS, 1), 0) + at_row
                c = jnp.where(position < lengths[tp], cot[r, :].astype(F32), 0.0) * row(6)
                g = (c - mean(c) - xhat * mean(c * xhat)) * scale
                total[r, :] = g
                norm_low[r, :] = g.astype(BF16)

        by_rows(SEQ, body)

    def first_norm_back():
        def body(r, at_row):
            c = acc[r, :] * row(4)
            xhat = xh1[r, :]
            g = (c - mean(c) - xhat * mean(c * xhat)) * rs1[r, :]
            acc[r, :] = g
            norm_low[r, :] = g.astype(BF16)

        by_rows(SEQ, body)
        g = dot_nt(wo[...], norm_low[...])
        for n in range(12):
            mix_t[64 * n : 64 * n + 64, :] = (g[64 * n : 64 * n + 64, :] * inv[n]).astype(BF16)

    def attend_back():
        def triple(step, carry):
            jobs = [(i, h) for i in range(3) for h in range(2)]
            parts = {}

            def lanes(i, section):
                return pl.ds(pl.multiple_of(D * section + (3 * step + i) * 128, 128), 128)

            def load(i):
                if i not in parts:
                    s = lanes(i, 0)
                    g2t = mix_t[pl.ds(pl.multiple_of((3 * step + i) * 128, 128), 128), :]
                    parts[i] = (jnp.transpose(k[:, s]), q[:, s], v[:, s], g2t, [], [], [])
                return parts[i]

            def raw(m):
                i, h = jobs[m]
                v2, g2t = load(i)[2:4]
                scores[m % 2] = dot(jnp.where(left if h == 0 else lane >= 64, v2, jnp.zeros_like(v2)), g2t)

            def middle(m):
                i, h = jobs[m]
                n = 2 * (3 * step + i) + h
                load(i)[6].append(dot_nt(expo[n], load(i)[3]))
                for c in range(0, SEQ, 256):
                    e = expo[n, :, c : c + 256].astype(F32)
                    g = scores[m % 2, :, c : c + 256]
                    inner = jnp.sum(e * g, axis=0, keepdims=True) * inv[n, :, c : c + 256]
                    ds[m % 2, :, c : c + 256] = (e * (g - inner)).astype(BF16)

            def last(m):
                i, h = jobs[m]
                k2t, q2, _, _, dq, dk, dv = load(i)
                dq.append(dot(k2t[64 * h : 64 * h + 64, :], ds[m % 2]))
                dk.append(dot(ds[m % 2], q2))
                if h == 1:
                    dqkv[:, lanes(i, 0)] = (jnp.transpose(jnp.concatenate(dq, axis=0)) * 0.125).astype(BF16)
                    dqkv[:, lanes(i, 1)] = jnp.where(left, dk[0], dk[1]).astype(BF16)
                    dqkv[:, lanes(i, 2)] = jnp.where(left, dv[0], dv[1]).astype(BF16)

            raw(0)
            for m in range(6):
                if m < 5:
                    raw(m + 1)
                middle(m)
                if m:
                    last(m - 1)
            last(5)
            return carry

        lax.fori_loop(0, 2, triple, 0)

    def adapter_grads():
        red[0:8, :] = dot_tn(low[...], dqkv[:, 0:D])[0:8, :] * 2.0
        red[8:16, :] = dot_tn(low[...], dqkv[:, 2 * D :])[8:16, :] * 2.0

    def input_grads(r):
        return acc[r, :] + dot_nt(dqkv[r, :], mkv[...])


    along_x = [(jnp.where(first, a[0], b[0]), tp) for a, b in zip(towards_u, towards_w)]
    along_y = [(jnp.where(first, b[0], a[0]), tp) for a, b in zip(towards_u, towards_w)]

    half_row = pl.ds(pl.multiple_of(core * 8, 8), 8)

    def exchange(n, src, dst, target):
        send(remote(src, dst, red_send.at[0], red_recv.at[n], target))

    def expect(n, dst):
        if COMM:
            remote(dst, dst, red_send.at[0], red_recv.at[n], partner).wait_recv()

    def line_total(n, buffer, count):
        expect(n, buffer.at[pl.ds(0, count - 1)])
        total = buffer[0]
        for h in range(1, count):
            total = total + buffer[h]
        return total


    start = pl.multiple_of(tp * HALF, HALF)
    pairs = [
        remote(tokens.at[1 - tp, 0:128], x.at[pl.ds(start, 128)], pair_send.at[0], pair_recv.at[0], partner),
        remote(eval_tokens.at[0], xe.at[0, mine_rows], pair_send.at[1], pair_recv.at[1], partner),
        remote(eval_tokens.at[1], xe.at[1, mine_rows], pair_send.at[2], pair_recv.at[2], partner),
        remote(cotangent.at[1 - tp], cot.at[mine_rows], pair_send.at[3], pair_recv.at[3], partner),
        remote(y_low.at[other_rows], act_out.at[tp], pair_send.at[4], pair_recv.at[4], partner),
        remote(ig_send, ig_recv, pair_send.at[5], pair_recv.at[5], partner),
        remote(tokens.at[1 - tp, 128:HALF], x.at[pl.ds(start + 128, 128)], pair_send.at[6], pair_recv.at[6], partner),
    ]

    def pair_start(n):
        if COMM:
            pairs[n].start()

    def pair_wait(n):
        if COMM:
            pairs[n].wait_recv()

    own = [
        pltpu.make_async_copy(tokens.at[tp], x.at[mine_rows], local_sem.at[0]),
        pltpu.make_async_copy(eval_tokens, xe.at[:, mine_rows], local_sem.at[1]),
        pltpu.make_async_copy(cotangent.at[tp], cot.at[mine_rows], local_sem.at[2]),
    ]
    for c in own:
        c.start()

    def eval_rows(at_row):
        item = lax.div(at_row, HALF)
        start = pl.multiple_of(lax.rem(at_row, HALF) + tp * HALF, ROWS)
        return xe[item, pl.ds(start, ROWS), :]

    def z_start(part):
        for n in range(15):
            send(z_copy(part, n))

    z_start(0)
    stage_rest()
    column_send(0)
    arrived[pl.ds(mine, 1)] = staged[pl.ds(core, 1)]
    z_start(1)
    prepare()
    column_step(1)
    z_wait(0)
    assemble(0)
    begin(0)
    pair_start(0)
    column_step(2)
    z_wait(1)
    assemble(1)
    assemble(2)
    widen(0)
    begin(1)
    column_step(3)
    pair_start(6)
    pair_start(1)
    pair_start(2)
    pair_start(3)
    relay(0)
    widen(1)
    finish(0)
    relay(1, (0,))
    begin(2)
    column_step(4)
    from_sibling(0)
    pair_wait(0)
    pair_wait(6)
    own[0].wait()
    project(0)
    relay(1, (1, 2, 3))
    widen(2)
    column_take(4)
    assemble(3)
    begin(3)
    attend(0, 1)
    attend(1, 2)
    finish(1)
    relay(2)
    widen(3, (1, 2))
    assemble(4)
    begin(4)
    attend(2, 3)
    from_sibling(1)
    project(1)
    widen(3, (3,))
    finish(2)
    attend(3, 4)
    relay(3, (0,))
    attend(4, 5)
    widen(4, (1, 2))
    attend(5, 6)
    relay(3, (1,))
    merge()
    from_sibling(2)
    first_norm(mix_t, lambda at_row: x[pl.ds(pl.multiple_of(at_row, ROWS), ROWS), :], acc, norm_low, True)
    relay(3, (2, 3))
    widen(4, (3,))
    pair_wait(1)
    own[1].wait()
    project_eval(0)
    relay(4, (0, 1))
    finish(3, (0, 1))
    attend_eval(0, 0, 2)
    relay(4, (2,))
    finish(3, (2, 3))
    attend_eval(0, 2, 3)
    relay(4, (3,))
    from_sibling(3)
    feed(0, norm_low, acc, True)
    finish(4)
    pair_wait(2)
    from_sibling(4)
    feed(1, norm_low, acc, True)
    pair_wait(3)
    own[2].wait()
    second_norm(acc, lambda at_row, value: y_low.__setitem__((pl.ds(at_row, ROWS), slice(None)), value), True)
    pair_start(4)
    act_out[pl.ds(tp, 1)] = y_low[mine_rows, :][None]
    feed_back()
    first_norm_back()
    attend_back()
    adapter_grads()
    exchange(0, red.at[pl.ds(pl.multiple_of((1 - core) * 8, 8), 8)], red_sib, sibling)
    ig_send[...] = input_grads(other_rows).astype(BF16)
    pair_start(5)
    expect(0, red_sib)
    red_sum[0] = red[half_row, :] + red_sib[...]
    if COMM:
        red_x[px] = red_sum[0]
        for target in along_x[1:]:
            exchange(1, red_sum.at[0], red_x.at[px], target)
    grad_out[pl.ds(tp, 1)] = input_grads(mine_rows)[None]

    project_eval(1)
    if COMM:
        red_sum[1] = line_total(1, red_x, 4)
        red_y[py] = red_sum[1]
        for target in along_y[1:]:
            exchange(2, red_sum.at[1], red_y.at[py], target)
    attend_eval(1, 0, 3)
    if COMM:
        red_sum[2] = line_total(2, red_y, 4)
        red_z[z] = red_sum[2]
        for h in range(1, 8):
            exchange(3, red_sum.at[2], red_z.at[z], column_at[h, 0])
    first_norm(mixe_t, eval_rows, acc_e, norm_e, False)
    feed(0, norm_e, acc_e, False)
    feed(1, norm_e, acc_e, False)
    pair_wait(5)
    grad_out[pl.ds(1 - tp, 1)] = ig_recv[...].astype(F32)[None]
    if COMM:
        red_all[half_row, :] = line_total(3, red_z, 8)
        exchange(4, red_all.at[half_row], red_all.at[half_row], sibling)
    second_norm(acc_e, lambda at_row, value: eval_out.__setitem__(pl.ds(lax.div(at_row, HALF), 1), value[None]), False)
    if COMM:
        expect(4, red_all.at[pl.ds(pl.multiple_of((1 - core) * 8, 8), 8)])
    adapter_q[...] = red_all[0:8, :]
    adapter_v[...] = red_all[8:16, :]
    pair_wait(4)
    if COMM:
        for c in pairs:
            c.wait_send()
        for part in range(2):
            z_all(part).wait_send()
        for n in range(5):
            column_copy(n).wait_send()
            all_sent(n)
        everything = acc_e.at[pl.ds(0, 15 * 8)]
        remote(everything, everything, red_send.at[0], red_recv.at[0], partner).wait_send()


def scratches():
    vm, dma = pltpu.VMEM, pltpu.SemaphoreType.DMA
    return [
        *(vm(shape, BF16) for shape in SMALL),
        vm((2, 4, STAGED), BF16), vm((2, 4, FF), BF16), vm((12, D), F32),
        vm((16, 4, STAGED), BF16), vm((16, 4, FF), BF16), vm((BLOCK, 1536), F32),
        vm((D, 1280), BF16), vm((D, 1280), BF16), vm((D, D), BF16), vm((D, FF), BF16), vm((D, FF), BF16),
        vm((D, 3 * D), BF16), vm((128, 2 * D), BF16),
        vm((SEQ, D), BF16), vm((2, SEQ, D), BF16), vm((SEQ, D), BF16), vm((SEQ, 128), BF16), vm((2, SEQ, 128), BF16),
        vm((SEQ, D), BF16), vm((SEQ, D), BF16), vm((SEQ, D), BF16), vm((D, SEQ), BF16),
        vm((12, SEQ, SEQ), BF16), vm((12, 1, SEQ), F32), vm((2, SEQ, SEQ), F32), vm((2, SEQ, SEQ), BF16),
        vm((SEQ, FF), BF16), vm((2, SEQ, D), BF16), vm((SEQ, D), F32), vm((SEQ, 1), F32),
        vm((SEQ, D), BF16), vm((SEQ, D), F32), vm((SEQ, D), BF16), vm((SEQ, 3 * D), BF16),
        vm((SEQ, 2 * D), BF16), vm((SEQ, D), BF16), vm((D, SEQ), BF16), vm((4, SEQ, HALF), BF16), vm((4, 1, HALF), F32),
        vm((SEQ, D), BF16), vm((SEQ, D), F32), vm((HALF, D), BF16), vm((HALF, D), BF16),
        vm((16, D), F32), vm((8, D), F32), vm((4, 8, D), F32), vm((4, 8, D), F32), vm((8, 8, D), F32),
        vm((3, 8, D), F32), vm((16, D), F32),
        dma((2,)), dma((2,)), dma((5,)), dma((5,)), dma((19,)), dma((5,)), dma((5, 11)), dma((5,)), dma((5,)),
        dma((7,)), dma((7,)), dma((10,)), dma((1,)), dma((5,)),
    ]


def layer(*operands):
    shapes = ((2, HALF, D), BF16), ((2, HALF, D), F32), ((2, HALF, D), BF16), ((8, D), F32), ((8, D), F32)
    out = tuple(pltpu.VMEM(*shape) for shape in shapes)
    hbm, vmem = pl.BlockSpec(memory_space=pl.ANY), pl.BlockSpec(memory_space=pltpu.VMEM)
    params = dict(collective_id=0) if COMM else {}
    return pl.pallas_call(
        layer_kernel,
        out_shape=out,
        in_specs=[pl.BlockSpec(memory_space=pltpu.SMEM)] + [hbm] * 22,
        out_specs=[vmem] * 5,
        scratch_shapes=scratches(),
        compiler_params=pltpu.CompilerParams(has_side_effects=True, vmem_limit_bytes=LIMIT << 20, **params),
    )(*operands)


def shards(tokens, eval_tokens, cotangent, lengths, *rest):
    rest = (*rest[0:5], rest[5].T, *rest[6:])
    frozen, ups, (query_bias, value_bias, bias_out, bias_up, bias_down, *norms) = rest[0:8], rest[8:10], rest[10:]
    vectors = (query_bias, value_bias, bias_out, bias_down, *norms, bias_up)
    activations, input_grad, evaluated, grad_q, grad_v = layer(
        lengths, *frozen, *ups, *vectors, tokens, eval_tokens, cotangent
    )
    return activations, input_grad, grad_q, grad_v, evaluated


def solution(mesh):
    rows, frozen, whole = P("dp", "tp", None), P(("dp", "tp"), None), P()
    in_specs = (rows, rows, rows, P("dp"), frozen, frozen, frozen, frozen, P("dp", "tp"), P("tp", "dp"), frozen, frozen)
    in_specs += (whole,) * 11
    out_specs = (rows, rows, whole, whole, rows)
    return jax.shard_map(shards, mesh=mesh, in_specs=in_specs, out_specs=out_specs, check_vma=False)
```

```python
import functools

import jax
import jax.numpy as jnp
from jax import lax
from jax.experimental import pallas as pl
from jax.experimental.pallas import tpu as pltpu
from jax.sharding import PartitionSpec as P

EPSILON = 1e-05
D = 768
FF = 3072
SEQ = 512
HALF = 256
BLOCK = 48
PAIRS = 6
LIMIT = 60
ROWS = 256
SIDE = 384
WIDTHS = (640, 640, 384, 1536, 1536)
STARTS = (0, 640, 1280, 1664, 3200)
STAGED = 1664
DIRECT = (True, False, False, False, False)
SMALL = ((3, D),) * 4 + ((6, 1536), (6, 1536), (3, 8), (3, 8), (8, D), (8, D)) + ((D,),) * 8 + ((FF,),)
Z_PARTS = ((0, 640), (640, 1024))
MESH = pl.DeviceIdType.MESH
BF16 = jnp.bfloat16
F32 = jnp.float32
COMM = True


def dot(a, b):
    return jnp.dot(a, b, preferred_element_type=F32)


def dot_nt(a, b):
    return lax.dot_general(a, b, (((1,), (1,)), ((), ())), preferred_element_type=F32)


def dot_tn(a, b):
    return lax.dot_general(a, b, (((0,), (0,)), ((), ())), preferred_element_type=F32)


def place():
    dp, tp = lax.axis_index("dp"), lax.axis_index("tp")
    core = lax.rem(dp, 2)
    z = lax.rem(lax.div(dp, 2), 4) * 2 + tp
    y = lax.rem(lax.div(dp, 8), 4)
    x = lax.div(dp, 32)
    return x, y, z, core


def slot_of(z, core):
    return (lax.div(z, 2) * 2 + core) * 2 + lax.rem(z, 2)


def remote(src, dst, send, recv, target):
    return pltpu.make_async_remote_copy(
        src_ref=src, dst_ref=dst, send_sem=send, recv_sem=recv, device_id=target, device_id_type=MESH
    )


def by_rows(count, body, size=ROWS):
    def step(i, carry):
        body(pl.ds(pl.multiple_of(i * size, size), size), i * size)
        return carry

    lax.fori_loop(0, count // size, step, 0)


def layer_kernel(lengths, *refs):
    sources, small = refs[0:19], refs[27:46]
    tokens, eval_tokens, cotangent, act_out, grad_out, eval_out, adapter_q, adapter_v = refs[19:27]
    w_query, w_key, w_value, w_out, w_up, w_down, a_query, a_value, query_up, value_up = small[0:10]
    vec_q, vec_v, vec_o, vec_down, gain_a, shift_a, gain_b, shift_b, vec_up = small[10:19]
    (
        staged, staged_f, vec, arrived, arrived_f, packed, wa0, wa1, wo, f0, f1, mkv, umat, x, xe, cot, low, kb,
        q, k, v, mix_t, expo, inv, scores, ds, gates, hidden, xh1, rs1, norm_low, acc, y_low, dqkv,
        kv, qe, mixe_t, expo_e, inv_e, norm_e, acc_e, ig_send, ig_recv, red, red_sib, red_x, red_y, red_z, red_sum, red_all,
        z_send, z_recv, f_send, f_recv, small_sem, xy_send, xy_recv, sib_send, sib_recv, pair_send, pair_recv, local_sem, red_send, red_recv,
    ) = refs[46:]
    fetches = [pltpu.make_async_copy(a, b, small_sem.at[n]) for n, (a, b) in enumerate(zip(sources, small))]
    for c in fetches:
        c.start()
    if COMM:
        px, py, z, core = place()
    else:
        px = py = z = core = jnp.minimum(lengths[0], 0)
    tp = lax.rem(z, 2)
    first = core == 0
    u = jnp.where(first, px, py)
    w = jnp.where(first, py, px)
    mine_rows = pl.ds(pl.multiple_of(tp * HALF, HALF), HALF)
    other_rows = pl.ds(pl.multiple_of((1 - tp) * HALF, HALF), HALF)
    def send(copy):
        if COMM:
            copy.start()

    round_u = [lax.rem(u + h, 4) for h in range(4)]
    round_w = [lax.rem(w + h, 4) for h in range(4)]
    scale_u, scale_w = jnp.where(first, 4, 1), jnp.where(first, 1, 4)
    base_dp = lax.div(z, 2) * 2 + core
    rows_u = [a * scale_u * BLOCK for a in round_u]
    rows_w = [a * scale_w * BLOCK for a in round_w]
    towards_u = [((a * scale_u + w * scale_w) * 8 + base_dp, tp) for a in round_u]
    towards_w = [((u * scale_u + a * scale_w) * 8 + base_dp, tp) for a in round_w]
    block_rows = [[pl.multiple_of(a + b, BLOCK) for b in rows_w] for a in rows_u]
    column = [(dz, dc) for dz in (4, 3, 5, 2, 6, 1, 7, 0) for dc in range(2) if (dz, dc) != (0, 0)]
    cores = (core, 1 - core)
    plane = (px * 4 + py) * 8
    round_z = [lax.rem(z + h, 8) for h in range(8)]
    along_z = [(plane + lax.div(a, 2) * 2, lax.rem(a, 2)) for a in round_z]
    sibling, partner = (along_z[0][0] + 1 - core, tp), (along_z[0][0] + core, 1 - tp)
    column_at = {(dz, dc): (along_z[dz][0] + cores[dc], along_z[dz][1]) for dz, dc in column}

    if COMM:
        greet = [column_at[d] for d in column] + towards_u[1:] + towards_w[1:]
        barrier = pltpu.get_barrier_semaphore()
        for other in greet:
            pl.semaphore_signal(barrier, inc=1, device_id=other, device_id_type=MESH)

    staged[...] = jnp.zeros_like(staged)
    staged_f[...] = jnp.zeros_like(staged_f)
    for n in (0, 1, 2, 6, 7):
        fetches[n].wait()
    low_maps = [a_query[...].astype(F32), a_value[...].astype(F32), jnp.zeros((3, 112), F32)]
    staged[0, 0:3, 0:128] = jnp.concatenate(low_maps, axis=1).astype(BF16)
    for g in range(2):
        a, b = 640 * g, SIDE * g
        staged[0, 0:3, a + 128 : a + 512] = w_query[:, b : b + SIDE]
        staged[0, 0:3, a + 512 : a + 640] = w_key[:, b : b + 128]
        staged[1, 0:3, a : a + 256] = w_key[:, b + 128 : b + SIDE]
        staged[1, 0:3, a + 256 : a + 640] = w_value[:, b : b + SIDE]

    def stage_rest():
        for n in (3, 4, 5):
            fetches[n].wait()
        up, down = w_up[...].astype(F32), w_down[...].astype(F32)
        for c in range(2):
            staged[c, 0:3, STARTS[2] : STARTS[2] + SIDE] = w_out[:, SIDE * c : SIDE * c + SIDE]
            for half in range(2):
                for which, part in enumerate((up, down)):
                    lo = half * 1536 + which * D
                    staged_f[c, 0:3, lo : lo + D] = part[3 * half : 3 * half + 3, c * D : c * D + D].astype(BF16)

    lane = lax.broadcasted_iota(jnp.int32, (1, 128), 1)
    left = lane < 64

    def prepare():
        for n in range(8, 19):
            fetches[n].wait()
        zero_u = jnp.zeros((8, SIDE), F32)
        up_q, up_v = query_up[...].astype(F32) * 2.0, value_up[...].astype(F32) * 2.0
        top = [up_q[:, 0:SIDE], zero_u, up_q[:, SIDE:D], zero_u]
        bottom = [zero_u, up_v[:, 0:SIDE], zero_u, up_v[:, SIDE:D]]
        for n, ref in enumerate((vec_q, vec_v, vec_o, vec_down, gain_a, shift_a, gain_b, shift_b)):
            vec[n : n + 1, :] = ref[...].astype(F32).reshape(1, D)
        for n in range(4):
            vec[8 + n : 9 + n, :] = vec_up[n * D : n * D + D].astype(F32).reshape(1, D)
        umat[...] = jnp.concatenate(
            [jnp.concatenate(top, axis=1), jnp.concatenate(bottom, axis=1), jnp.zeros((112, 2 * D), F32)], axis=0
        ).astype(BF16)
        for item in range(2):
            position = lax.broadcasted_iota(jnp.int32, (SEQ, 128), 0)
            kb[item] = jnp.where(position < lengths[item], 0.0, -1e30).astype(BF16)

    if COMM:
        pl.semaphore_wait(barrier, len(greet))

    mine = slot_of(z, core)

    def z_copy(part, n):
        dz, dc = column[n]
        lo, width = Z_PARTS[part]
        return remote(
            staged.at[cores[dc], :, pl.ds(lo, width)], arrived.at[mine, :, pl.ds(lo, width)],
            z_send.at[part], z_recv.at[part], column_at[dz, dc],
        )

    def z_wait(part):
        if not COMM:
            return
        z_all(part).wait_recv()

    def z_all(part):
        lo, width = Z_PARTS[part]
        whole = arrived.at[pl.ds(0, 15), :, pl.ds(lo, width)]
        return remote(whole, whole, z_send.at[part], z_recv.at[part], partner)

    pair_at = lax.div(z, 2)
    ahead_z = (jnp.where(tp == 0, along_z[7][0], along_z[1][0]) + core, 1 - tp)
    pair_q = lax.rem(pair_at + jnp.where(tp == 0, 3, 1), 4)
    pair_p = lax.rem(pair_at + jnp.where(tp == 0, 1, 3), 4)
    pair_far = lax.rem(pair_at + 2, 4)

    def four(n):
        return arrived_f.at[pl.ds(pl.multiple_of(n * 4, 4), 4)]

    def two(zz):
        return arrived_f.at[pl.ds(pl.multiple_of(zz * 2, 2), 2)]

    def column_copy(n):
        if n == 0:
            src, dst = staged_f.at[1 - core], arrived_f.at[z * 2 + core]
        else:
            src = dst = (None, two(z), four(pair_at), four(pair_q), four(pair_p))[n]
        return remote(src, dst, f_send.at[n], f_recv.at[n], (sibling, partner, ahead_z, partner, ahead_z)[n])

    def column_send(n):
        if n == 0:
            arrived_f[pl.ds(z * 2 + core, 1)] = staged_f[pl.ds(core, 1)]
        send(column_copy(n))

    def column_take(n):
        far_z = z + 1 - 2 * tp
        dst = (arrived_f.at[z * 2 + 1 - core], two(far_z), four(pair_q), four(pair_p), four(pair_far))[n]
        if COMM:
            remote(dst, dst, f_send.at[n], f_recv.at[n], partner).wait_recv()

    def column_step(n):
        column_take(n - 1)
        column_send(n)

    groups = [(ref, width, pl.multiple_of(core * width, 128)) for ref, width in zip((wa0, wa1, wo, f0, f1), WIDTHS)]

    def region(g, uu, ww, part=None):
        ref, width, lo = groups[g]
        cut = (width // 128 + 1) // 2 * 128
        if part == 0:
            width = cut
        elif part == 1:
            lo, width = pl.multiple_of(lo + cut, 128), width - cut
        return ref.at[pl.ds(block_rows[uu][ww], BLOCK), pl.ds(lo, width)]

    steps = (0, 3, 1, 2)

    def xy(g, n, r, target):
        sem = n if n < 4 else (n - 4) // 4 * 2 + 3 + n % 4 // 2
        send(remote(r, r, xy_send.at[g], xy_recv.at[g, sem], target))

    def take(g, sem, blocks):
        if COMM:
            r = half_of(g, blocks * BLOCK)
            remote(r, r, xy_send.at[g], xy_recv.at[g, sem], partner).wait_recv()

    def to_sibling(g, j, i):
        r = region(g, steps[j], steps[i])
        send(remote(r, r, sib_send.at[g], sib_recv.at[g], sibling))

    def half_of(g, rows, other=False):
        ref, width, lo = groups[g]
        if other:
            lo = pl.multiple_of((1 - core) * width, 128)
        return ref.at[pl.ds(0, rows), pl.ds(lo, width)]

    def from_sibling(g):
        if COMM:
            r = half_of(g, D, True)
            remote(r, r, sib_send.at[g], sib_recv.at[g], partner).wait_recv()

    def all_sent(g):
        if COMM:
            r = half_of(g, 15 * BLOCK)
            remote(r, r, xy_send.at[g], xy_recv.at[g, 0], partner).wait_send()
            r = half_of(g, D)
            remote(r, r, sib_send.at[g], sib_recv.at[g], partner).wait_send()

    def line_send(g, base, uu, ww, ahead):
        r = region(g, uu, ww)
        xy(g, base, r, ahead(1))
        xy(g, base + 1, r, ahead(3))
        if DIRECT[g]:
            xy(g, base + 2, r, ahead(2))

    def along_u(h):
        return towards_u[h]

    def along_w(h):
        return towards_w[h]

    def first_send(g):
        r = region(g, 0, 0)
        for n, h in enumerate((1, 3, 2)[: 2 if g > 2 else 3]):
            xy(g, n, r, along_u(h))

    def second_send(g, j):
        line_send(g, 4 + 4 * j, steps[j], 0, along_w)
        to_sibling(g, j, 0)

    def second_forward(g, j):
        take(g, 2 * j + 3, 2)
        if not DIRECT[g]:
            xy(g, 6 + 4 * j, region(g, steps[j], 3, 0), along_w(1))
            xy(g, 7 + 4 * j, region(g, steps[j], 1, 1), along_w(3))
        to_sibling(g, j, 1)
        to_sibling(g, j, 2)

    def second_finish(g, j):
        take(g, 2 * j + 4, 1)
        to_sibling(g, j, 3)

    def begin(g):
        first_send(g)
        second_send(g, 0)

    def widen(g, js=(1, 2, 3)):
        for j in js:
            take(g, j - 1, 1)
            if g > 2 and j < 3:
                xy(g, 2, region(g, steps[j], 0, j - 1), along_u(steps[3 - j]))
            second_send(g, j)

    def relay(g, js=(0, 1, 2, 3)):
        for j in js:
            second_forward(g, j)

    def finish(g, js=(0, 1, 2, 3)):
        for j in js:
            second_finish(g, j)

    here = pl.ds(block_rows[0][0], BLOCK)

    def assemble(g):
        ref, width, lo = groups[g]
        for s in range(16):
            if g < 3:
                packed[3 * s : 3 * s + 3, 0:width] = arrived[s, 0:3, STARTS[g] : STARTS[g] + width].astype(F32)
            elif s // 2 % 2 == g - 3:
                for half in range(2):
                    row, src = (s // 4 * 2 + s % 2) * 6 + half * 3, half * 1536
                    packed[row : row + 3, :] = arrived_f[s, 0:3, src : src + 1536].astype(F32)
        ref[here, pl.ds(lo, width)] = packed[:, 0:width].astype(BF16)


    def row(n):
        return vec[n : n + 1, :]

    def project(g):
        wa = (wa0, wa1)[g]
        side = slice(SIDE * g, SIDE * g + SIDE)
        for half in range(2):
            r = slice(HALF * half, HALF * half + HALF)
            got = dot(x[r, :], wa[...])
            if g == 0:
                low[r, :] = got[:, 0:128].astype(BF16)
            more = dot(low[r, :], umat[:, D * g : D * g + D])
            q[r, side] = ((got[:, 128:512] + more[:, 0:SIDE] + row(0)[:, side]) * 0.125).astype(BF16)
            k[r, side] = got[:, 512:896].astype(BF16)
            v[r, side] = (got[:, 896:1280] + more[:, SIDE:D] + row(1)[:, side]).astype(BF16)

    def merge():
        for g, wa in enumerate((wa0, wa1)):
            more = dot(wa0[:, 0:128], umat[:, D * g : D * g + D])
            side = SIDE * g
            mkv[:, side : side + SIDE] = (wa[:, 128:512].astype(F32) + more[:, 0:SIDE]).astype(BF16)
            mkv[:, D + side : D + side + SIDE] = wa[:, 512:896]
            mkv[:, 2 * D + side : 2 * D + side + SIDE] = (wa[:, 896:1280].astype(F32) + more[:, SIDE:D]).astype(BF16)

    def project_eval(item):
        for half in range(2):
            r = slice(HALF * half, HALF * half + HALF)
            got = dot(xe[item, r, :], mkv[:, D : 3 * D])
            kv[r, 0:D] = got[:, 0:D].astype(BF16)
            kv[r, D : 2 * D] = (got[:, D:] + row(1)).astype(BF16)
        own = dot(xe[item, mine_rows, :], mkv[:, 0:D])
        qe[HALF * item : HALF * item + HALF, :] = ((own + row(0)) * 0.125).astype(BF16)

    def heads(k2, q2, bias):
        for h in range(2):
            keep = left if h == 0 else lane >= 64
            spare = lane == (64 if h == 0 else 0)
            kh = jnp.where(keep, k2, jnp.where(spare, bias, jnp.zeros_like(bias)))
            yield h, kh, jnp.where(spare, jnp.ones_like(q2), q2)

    def softmax(s_ref, queries, e_ref, inverse):
        for c in range(0, queries, 256):
            s = s_ref[:, c : c + 256]
            e = jnp.exp(s - jnp.max(s, axis=0, keepdims=True))
            inverse[:, c : c + 256] = 1.0 / jnp.sum(e, axis=0, keepdims=True)
            e_ref[:, c : c + 256] = e.astype(BF16)

    def attend(lo, hi):
        def pair(p, carry):
            s = pl.ds(pl.multiple_of(p * 128, 128), 128)
            v2t = jnp.transpose(v[:, s])
            for h, kh, qh in heads(k[:, s], q[:, s], kb[tp]):
                scores[h] = dot_nt(kh, qh)
            for h in range(2):
                n = 2 * p + h
                softmax(scores.at[h], SEQ, expo.at[n], inv.at[n])
                o = dot(v2t[64 * h : 64 * h + 64, :], expo[n]) * inv[n]
                mix_t[pl.ds(pl.multiple_of(p * 128 + 64 * h, 64), 64), :] = o.astype(BF16)
            return carry

        lax.fori_loop(lo, hi, pair, 0)

    def attend_eval(item, lo, hi):
        own = slice(HALF * item, HALF * item + HALF)

        def pairs_of(step, carry):
            turned = []
            for i in range(2):
                p = 2 * step + i
                s = pl.ds(pl.multiple_of(p * 128, 128), 128)
                ks = s
                vs = pl.ds(pl.multiple_of(D + p * 128, 128), 128)
                turned.append(jnp.transpose(kv[:, vs]))
                for h, kh, qh in heads(kv[:, ks], qe[own, s], kb[item]):
                    scores[i, :, HALF * h : HALF * h + HALF] = dot_nt(kh, qh)
            for i in range(2):
                p = 2 * step + i
                for h in range(2):
                    n = 2 * i + h
                    softmax(scores.at[i, :, pl.ds(HALF * h, HALF)], HALF, expo_e.at[n], inv_e.at[n])
                    o = dot(turned[i][64 * h : 64 * h + 64, :], expo_e[n]) * inv_e[n]
                    mixe_t[pl.ds(pl.multiple_of(p * 128 + 64 * h, 64), 64), own] = o.astype(BF16)
            return carry

        lax.fori_loop(lo, hi, pairs_of, 0)

    def mean(a):
        return jnp.sum(a, axis=-1, keepdims=True) * (1.0 / D)

    def normalise(a):
        centred = a - mean(a)
        scale = lax.rsqrt(mean(centred * centred) + EPSILON)
        return centred * scale, scale

    def first_norm(mixed, base, total, low_ref, keep):
        total[...] = dot_tn(mixed[...], wo[...])

        def body(r, at_row):
            xhat, scale = normalise(total[r, :] + base(at_row).astype(F32) + row(2))
            if keep:
                xh1[r, :] = xhat
                rs1[r, :] = scale
            normed = xhat * row(4) + row(5)
            low_ref[r, :] = normed.astype(BF16)
            total[r, :] = normed + row(3)

        by_rows(SEQ, body)

    def feed(part, low_ref, total, keep, between=None):
        f = (f0, f1)[part]

        def down(order, c, r):
            columns = pl.ds(pl.multiple_of(1536 * c + D, 128), D)
            total[r, :] += dot_nt(hidden[order, r, :], f[:, columns])

        ready = None
        for order, c in enumerate(cores):
            n = 2 * part + c
            if order and between:
                between()
            for half in range(2):
                r = slice(HALF * half, HALF * half + HALF)
                pre = dot(low_ref[r, :], f[:, pl.ds(pl.multiple_of(1536 * c, 128), D)]) + vec[pl.ds(8 + n, 1), :]
                if ready:
                    down(*ready)
                phi = 0.5 + 0.5 * lax.erf(pre * 0.7071067811865476)
                hidden[order, r, :] = (pre * phi).astype(BF16)
                if keep:
                    slope = phi + pre * (0.3989422804014327 * jnp.exp(pre * pre * -0.5))
                    gates[r, pl.ds(pl.multiple_of(D * n, 128), D)] = slope.astype(BF16)
                ready = (order, c, r)
        down(*ready)

    def feed_back():
        def up(n, r):
            f, c = (f0, f1)[n // 2], n % 2
            acc[r, :] += dot_nt(hidden[c, r, :], f[:, 1536 * c : 1536 * c + D])

        ready = None
        for n in range(4):
            f, c = (f0, f1)[n // 2], n % 2
            for half in range(2):
                r = slice(HALF * half, HALF * half + HALF)
                g = dot(norm_low[r, :], f[:, 1536 * c + D : 1536 * c + 2 * D])
                if ready:
                    up(*ready)
                hidden[c, r, :] = (g * gates[r, D * n : D * n + D].astype(F32)).astype(BF16)
                ready = (n, r)
        up(*ready)

    def second_norm(total, out, backward):
        def body(r, at_row):
            xhat, scale = normalise(total[r, :])
            out(at_row, (xhat * row(6) + row(7)).astype(BF16))
            if backward:
                position = lax.broadcasted_iota(jnp.int32, (ROWS, 1), 0) + at_row
                c = jnp.where(position < lengths[tp], cot[r, :].astype(F32), 0.0) * row(6)
                g = (c - mean(c) - xhat * mean(c * xhat)) * scale
                total[r, :] = g
                norm_low[r, :] = g.astype(BF16)

        by_rows(SEQ, body)

    def first_norm_back():
        def body(r, at_row):
            c = acc[r, :] * row(4)
            xhat = xh1[r, :]
            g = (c - mean(c) - xhat * mean(c * xhat)) * rs1[r, :]
            acc[r, :] = g
            norm_low[r, :] = g.astype(BF16)

        by_rows(SEQ, body)
        g = dot_nt(wo[...], norm_low[...])
        for n in range(12):
            mix_t[64 * n : 64 * n + 64, :] = (g[64 * n : 64 * n + 64, :] * inv[n]).astype(BF16)

    def attend_back():
        def triple(step, carry):
            jobs = [(i, h) for i in range(3) for h in range(2)]
            parts = {}

            def lanes(i, section):
                return pl.ds(pl.multiple_of(D * section + (3 * step + i) * 128, 128), 128)

            def load(i):
                if i not in parts:
                    s = lanes(i, 0)
                    g2t = mix_t[pl.ds(pl.multiple_of((3 * step + i) * 128, 128), 128), :]
                    parts[i] = (jnp.transpose(k[:, s]), q[:, s], v[:, s], g2t, [], [], [])
                return parts[i]

            def raw(m):
                i, h = jobs[m]
                v2, g2t = load(i)[2:4]
                scores[m % 2] = dot(jnp.where(left if h == 0 else lane >= 64, v2, jnp.zeros_like(v2)), g2t)

            def middle(m):
                i, h = jobs[m]
                n = 2 * (3 * step + i) + h
                load(i)[6].append(dot_nt(expo[n], load(i)[3]))
                for c in range(0, SEQ, 256):
                    e = expo[n, :, c : c + 256].astype(F32)
                    g = scores[m % 2, :, c : c + 256]
                    inner = jnp.sum(e * g, axis=0, keepdims=True) * inv[n, :, c : c + 256]
                    ds[m % 2, :, c : c + 256] = (e * (g - inner)).astype(BF16)

            def last(m):
                i, h = jobs[m]
                k2t, q2, _, _, dq, dk, dv = load(i)
                dq.append(dot(k2t[64 * h : 64 * h + 64, :], ds[m % 2]))
                dk.append(dot(ds[m % 2], q2))
                if h == 1:
                    dqkv[:, lanes(i, 0)] = (jnp.transpose(jnp.concatenate(dq, axis=0)) * 0.125).astype(BF16)
                    dqkv[:, lanes(i, 1)] = jnp.where(left, dk[0], dk[1]).astype(BF16)
                    dqkv[:, lanes(i, 2)] = jnp.where(left, dv[0], dv[1]).astype(BF16)

            raw(0)
            for m in range(6):
                if m < 5:
                    raw(m + 1)
                middle(m)
                if m:
                    last(m - 1)
            last(5)
            return carry

        lax.fori_loop(0, 2, triple, 0)

    def adapter_grads():
        red[0:8, :] = dot_tn(low[...], dqkv[:, 0:D])[0:8, :] * 2.0
        red[8:16, :] = dot_tn(low[...], dqkv[:, 2 * D :])[8:16, :] * 2.0

    def input_grads(r):
        return acc[r, :] + dot_nt(dqkv[r, :], mkv[...])


    along_x = [(jnp.where(first, a[0], b[0]), tp) for a, b in zip(towards_u, towards_w)]
    along_y = [(jnp.where(first, b[0], a[0]), tp) for a, b in zip(towards_u, towards_w)]

    half_row = pl.ds(pl.multiple_of(core * 8, 8), 8)

    def exchange(n, src, dst, target):
        send(remote(src, dst, red_send.at[0], red_recv.at[n], target))

    def expect(n, dst):
        if COMM:
            remote(dst, dst, red_send.at[0], red_recv.at[n], partner).wait_recv()

    def line_total(n, buffer, count):
        expect(n, buffer.at[pl.ds(0, count - 1)])
        total = buffer[0]
        for h in range(1, count):
            total = total + buffer[h]
        return total


    start = pl.multiple_of(tp * HALF, HALF)
    pairs = [
        remote(tokens.at[1 - tp, 0:128], x.at[pl.ds(start, 128)], pair_send.at[0], pair_recv.at[0], partner),
        remote(eval_tokens.at[0], xe.at[0, mine_rows], pair_send.at[1], pair_recv.at[1], partner),
        remote(eval_tokens.at[1], xe.at[1, mine_rows], pair_send.at[2], pair_recv.at[2], partner),
        remote(cotangent.at[1 - tp], cot.at[mine_rows], pair_send.at[3], pair_recv.at[3], partner),
        remote(y_low.at[other_rows], act_out.at[tp], pair_send.at[4], pair_recv.at[4], partner),
        remote(ig_send, ig_recv, pair_send.at[5], pair_recv.at[5], partner),
        remote(tokens.at[1 - tp, 128:HALF], x.at[pl.ds(start + 128, 128)], pair_send.at[6], pair_recv.at[6], partner),
    ]

    def pair_start(n):
        if COMM:
            pairs[n].start()

    def pair_wait(n):
        if COMM:
            pairs[n].wait_recv()

    own = [
        pltpu.make_async_copy(tokens.at[tp], x.at[mine_rows], local_sem.at[0]),
        pltpu.make_async_copy(eval_tokens, xe.at[:, mine_rows], local_sem.at[1]),
        pltpu.make_async_copy(cotangent.at[tp], cot.at[mine_rows], local_sem.at[2]),
    ]
    for c in own:
        c.start()

    def eval_rows(at_row):
        item = lax.div(at_row, HALF)
        start = pl.multiple_of(lax.rem(at_row, HALF) + tp * HALF, ROWS)
        return xe[item, pl.ds(start, ROWS), :]

    def z_start(part):
        for n in range(15):
            send(z_copy(part, n))

    z_start(0)
    stage_rest()
    column_send(0)
    arrived[pl.ds(mine, 1)] = staged[pl.ds(core, 1)]
    z_start(1)
    prepare()
    column_step(1)
    z_wait(0)
    assemble(0)
    begin(0)
    pair_start(0)
    column_step(2)
    z_wait(1)
    assemble(1)
    assemble(2)
    widen(0)
    begin(1)
    column_step(3)
    pair_start(6)
    pair_start(1)
    pair_start(2)
    pair_start(3)
    relay(0)
    widen(1)
    finish(0)
    relay(1, (0,))
    begin(2)
    column_step(4)
    from_sibling(0)
    pair_wait(0)
    pair_wait(6)
    own[0].wait()
    project(0)
    relay(1, (1, 2, 3))
    widen(2)
    column_take(4)
    assemble(3)
    begin(3)
    attend(0, 1)
    attend(1, 2)
    finish(1)
    relay(2)
    widen(3, (1, 2))
    assemble(4)
    begin(4)
    attend(2, 3)
    from_sibling(1)
    project(1)
    widen(3, (3,))
    finish(2)
    attend(3, 4)
    relay(3, (0,))
    attend(4, 5)
    widen(4, (1, 2))
    attend(5, 6)
    relay(3, (1,))
    merge()
    from_sibling(2)
    first_norm(mix_t, lambda at_row: x[pl.ds(pl.multiple_of(at_row, ROWS), ROWS), :], acc, norm_low, True)
    relay(3, (2, 3))
    widen(4, (3,))
    pair_wait(1)
    own[1].wait()
    project_eval(0)
    relay(4, (0, 1))
    finish(3, (0, 1))
    attend_eval(0, 0, 2)
    relay(4, (2,))
    finish(3, (2, 3))
    attend_eval(0, 2, 3)
    relay(4, (3,))

    def rest_of_groups():
        from_sibling(3)
        finish(4)

    feed(0, norm_low, acc, True, rest_of_groups)
    feed(1, norm_low, acc, True, lambda: from_sibling(4))
    pair_wait(2)
    pair_wait(3)
    own[2].wait()
    second_norm(acc, lambda at_row, value: y_low.__setitem__((pl.ds(at_row, ROWS), slice(None)), value), True)
    pair_start(4)
    act_out[pl.ds(tp, 1)] = y_low[mine_rows, :][None]
    feed_back()
    first_norm_back()
    attend_back()
    adapter_grads()
    exchange(0, red.at[pl.ds(pl.multiple_of((1 - core) * 8, 8), 8)], red_sib, sibling)
    ig_send[...] = input_grads(other_rows).astype(BF16)
    pair_start(5)
    expect(0, red_sib)
    red_sum[0] = red[half_row, :] + red_sib[...]
    if COMM:
        red_x[px] = red_sum[0]
        for target in along_x[1:]:
            exchange(1, red_sum.at[0], red_x.at[px], target)
    grad_out[pl.ds(tp, 1)] = input_grads(mine_rows)[None]

    project_eval(1)
    if COMM:
        red_sum[1] = line_total(1, red_x, 4)
        red_y[py] = red_sum[1]
        for target in along_y[1:]:
            exchange(2, red_sum.at[1], red_y.at[py], target)
    attend_eval(1, 0, 3)
    if COMM:
        red_sum[2] = line_total(2, red_y, 4)
        red_z[z] = red_sum[2]
        for h in range(1, 8):
            exchange(3, red_sum.at[2], red_z.at[z], column_at[h, 0])
    first_norm(mixe_t, eval_rows, acc_e, norm_e, False)
    feed(0, norm_e, acc_e, False)
    feed(1, norm_e, acc_e, False)
    pair_wait(5)
    grad_out[pl.ds(1 - tp, 1)] = ig_recv[...].astype(F32)[None]
    if COMM:
        red_all[half_row, :] = line_total(3, red_z, 8)
        exchange(4, red_all.at[half_row], red_all.at[half_row], sibling)
    second_norm(acc_e, lambda at_row, value: eval_out.__setitem__(pl.ds(lax.div(at_row, HALF), 1), value[None]), False)
    if COMM:
        expect(4, red_all.at[pl.ds(pl.multiple_of((1 - core) * 8, 8), 8)])
    adapter_q[...] = red_all[0:8, :]
    adapter_v[...] = red_all[8:16, :]
    pair_wait(4)
    if COMM:
        for c in pairs:
            c.wait_send()
        for part in range(2):
            z_all(part).wait_send()
        for n in range(5):
            column_copy(n).wait_send()
            all_sent(n)
        everything = acc_e.at[pl.ds(0, 15 * 8)]
        remote(everything, everything, red_send.at[0], red_recv.at[0], partner).wait_send()


def scratches():
    vm, dma = pltpu.VMEM, pltpu.SemaphoreType.DMA
    return [
        *(vm(shape, BF16) for shape in SMALL),
        vm((2, 4, STAGED), BF16), vm((2, 4, FF), BF16), vm((12, D), F32),
        vm((16, 4, STAGED), BF16), vm((16, 4, FF), BF16), vm((BLOCK, 1536), F32),
        vm((D, 1280), BF16), vm((D, 1280), BF16), vm((D, D), BF16), vm((D, FF), BF16), vm((D, FF), BF16),
        vm((D, 3 * D), BF16), vm((128, 2 * D), BF16),
        vm((SEQ, D), BF16), vm((2, SEQ, D), BF16), vm((SEQ, D), BF16), vm((SEQ, 128), BF16), vm((2, SEQ, 128), BF16),
        vm((SEQ, D), BF16), vm((SEQ, D), BF16), vm((SEQ, D), BF16), vm((D, SEQ), BF16),
        vm((12, SEQ, SEQ), BF16), vm((12, 1, SEQ), F32), vm((2, SEQ, SEQ), F32), vm((2, SEQ, SEQ), BF16),
        vm((SEQ, FF), BF16), vm((2, SEQ, D), BF16), vm((SEQ, D), F32), vm((SEQ, 1), F32),
        vm((SEQ, D), BF16), vm((SEQ, D), F32), vm((SEQ, D), BF16), vm((SEQ, 3 * D), BF16),
        vm((SEQ, 2 * D), BF16), vm((SEQ, D), BF16), vm((D, SEQ), BF16), vm((4, SEQ, HALF), BF16), vm((4, 1, HALF), F32),
        vm((SEQ, D), BF16), vm((SEQ, D), F32), vm((HALF, D), BF16), vm((HALF, D), BF16),
        vm((16, D), F32), vm((8, D), F32), vm((4, 8, D), F32), vm((4, 8, D), F32), vm((8, 8, D), F32),
        vm((3, 8, D), F32), vm((16, D), F32),
        dma((2,)), dma((2,)), dma((5,)), dma((5,)), dma((19,)), dma((5,)), dma((5, 11)), dma((5,)), dma((5,)),
        dma((7,)), dma((7,)), dma((10,)), dma((1,)), dma((5,)),
    ]


def layer(*operands):
    shapes = ((2, HALF, D), BF16), ((2, HALF, D), F32), ((2, HALF, D), BF16), ((8, D), F32), ((8, D), F32)
    out = tuple(pltpu.VMEM(*shape) for shape in shapes)
    hbm, vmem = pl.BlockSpec(memory_space=pl.ANY), pl.BlockSpec(memory_space=pltpu.VMEM)
    params = dict(collective_id=0) if COMM else {}
    return pl.pallas_call(
        layer_kernel,
        out_shape=out,
        in_specs=[pl.BlockSpec(memory_space=pltpu.SMEM)] + [hbm] * 22,
        out_specs=[vmem] * 5,
        scratch_shapes=scratches(),
        compiler_params=pltpu.CompilerParams(has_side_effects=True, vmem_limit_bytes=LIMIT << 20, **params),
    )(*operands)


def shards(tokens, eval_tokens, cotangent, lengths, *rest):
    rest = (*rest[0:5], rest[5].T, *rest[6:])
    frozen, ups, (query_bias, value_bias, bias_out, bias_up, bias_down, *norms) = rest[0:8], rest[8:10], rest[10:]
    vectors = (query_bias, value_bias, bias_out, bias_down, *norms, bias_up)
    activations, input_grad, evaluated, grad_q, grad_v = layer(
        lengths, *frozen, *ups, *vectors, tokens, eval_tokens, cotangent
    )
    return activations, input_grad, grad_q, grad_v, evaluated


def solution(mesh):
    rows, frozen, whole = P("dp", "tp", None), P(("dp", "tp"), None), P()
    in_specs = (rows, rows, rows, P("dp"), frozen, frozen, frozen, frozen, P("dp", "tp"), P("tp", "dp"), frozen, frozen)
    in_specs += (whole,) * 11
    out_specs = (rows, rows, whole, whole, rows)
    return jax.shard_map(shards, mesh=mesh, in_specs=in_specs, out_specs=out_specs, check_vma=False)
```

```python
import functools

import jax
import jax.numpy as jnp
from jax import lax
from jax.experimental import pallas as pl
from jax.experimental.pallas import tpu as pltpu
from jax.sharding import PartitionSpec as P

EPSILON = 1e-05
D = 768
FF = 3072
SEQ = 512
HALF = 256
BLOCK = 48
PAIRS = 6
LIMIT = 60
ROWS = 256
SIDE = 384
WIDTHS = (640, 640, 384, 1536, 1536)
STARTS = (0, 640, 1280, 1664, 3200)
STAGED = 1664
DIRECT = (True, False, False, False, False)
SMALL = ((3, D),) * 4 + ((6, 1536), (6, 1536), (3, 8), (3, 8), (8, D), (8, D)) + ((D,),) * 8 + ((FF,),)
Z_PARTS = ((0, 640), (640, 1024))
MESH = pl.DeviceIdType.MESH
BF16 = jnp.bfloat16
F32 = jnp.float32
COMM = True


def dot(a, b):
    return jnp.dot(a, b, preferred_element_type=F32)


def dot_nt(a, b):
    return lax.dot_general(a, b, (((1,), (1,)), ((), ())), preferred_element_type=F32)


def dot_tn(a, b):
    return lax.dot_general(a, b, (((0,), (0,)), ((), ())), preferred_element_type=F32)


def place():
    dp, tp = lax.axis_index("dp"), lax.axis_index("tp")
    core = lax.rem(dp, 2)
    z = lax.rem(lax.div(dp, 2), 4) * 2 + tp
    y = lax.rem(lax.div(dp, 8), 4)
    x = lax.div(dp, 32)
    return x, y, z, core


def slot_of(z, core):
    return (lax.div(z, 2) * 2 + core) * 2 + lax.rem(z, 2)


def remote(src, dst, send, recv, target):
    return pltpu.make_async_remote_copy(
        src_ref=src, dst_ref=dst, send_sem=send, recv_sem=recv, device_id=target, device_id_type=MESH
    )


def by_rows(count, body, size=ROWS):
    def step(i, carry):
        body(pl.ds(pl.multiple_of(i * size, size), size), i * size)
        return carry

    lax.fori_loop(0, count // size, step, 0)


def layer_kernel(lengths, *refs):
    sources, small = refs[0:19], refs[27:46]
    tokens, eval_tokens, cotangent, act_out, grad_out, eval_out, adapter_q, adapter_v = refs[19:27]
    w_query, w_key, w_value, w_out, w_up, w_down, a_query, a_value, query_up, value_up = small[0:10]
    vec_q, vec_v, vec_o, vec_down, gain_a, shift_a, gain_b, shift_b, vec_up = small[10:19]
    (
        staged, staged_f, vec, arrived, arrived_f, packed, wa0, wa1, wo, f0, f1, mkv, umat, x, xe, cot, low, kb,
        q, k, v, mix_t, expo, inv, scores, ds, gates, hidden, xh1, rs1, norm_low, acc, y_low, dqkv,
        kv, qe, mixe_t, expo_e, inv_e, norm_e, acc_e, ig_send, ig_recv, red, red_sib, red_x, red_y, red_z, red_sum, red_all,
        z_send, z_recv, f_send, f_recv, small_sem, xy_send, xy_recv, sib_send, sib_recv, pair_send, pair_recv, local_sem, red_send, red_recv,
    ) = refs[46:]
    fetches = [pltpu.make_async_copy(a, b, small_sem.at[n]) for n, (a, b) in enumerate(zip(sources, small))]
    for c in fetches:
        c.start()
    if COMM:
        px, py, z, core = place()
    else:
        px = py = z = core = jnp.minimum(lengths[0], 0)
    tp = lax.rem(z, 2)
    first = core == 0
    u = jnp.where(first, px, py)
    w = jnp.where(first, py, px)
    mine_rows = pl.ds(pl.multiple_of(tp * HALF, HALF), HALF)
    other_rows = pl.ds(pl.multiple_of((1 - tp) * HALF, HALF), HALF)
    def send(copy):
        if COMM:
            copy.start()

    round_u = [lax.rem(u + h, 4) for h in range(4)]
    round_w = [lax.rem(w + h, 4) for h in range(4)]
    scale_u, scale_w = jnp.where(first, 4, 1), jnp.where(first, 1, 4)
    base_dp = lax.div(z, 2) * 2 + core
    rows_u = [a * scale_u * BLOCK for a in round_u]
    rows_w = [a * scale_w * BLOCK for a in round_w]
    towards_u = [((a * scale_u + w * scale_w) * 8 + base_dp, tp) for a in round_u]
    towards_w = [((u * scale_u + a * scale_w) * 8 + base_dp, tp) for a in round_w]
    block_rows = [[pl.multiple_of(a + b, BLOCK) for b in rows_w] for a in rows_u]
    column = [(dz, dc) for dz in (4, 3, 5, 2, 6, 1, 7, 0) for dc in range(2) if (dz, dc) != (0, 0)]
    cores = (core, 1 - core)
    plane = (px * 4 + py) * 8
    round_z = [lax.rem(z + h, 8) for h in range(8)]
    along_z = [(plane + lax.div(a, 2) * 2, lax.rem(a, 2)) for a in round_z]
    sibling, partner = (along_z[0][0] + 1 - core, tp), (along_z[0][0] + core, 1 - tp)
    column_at = {(dz, dc): (along_z[dz][0] + cores[dc], along_z[dz][1]) for dz, dc in column}

    if COMM:
        greet = [column_at[d] for d in column] + towards_u[1:] + towards_w[1:]
        barrier = pltpu.get_barrier_semaphore()
        for other in greet:
            pl.semaphore_signal(barrier, inc=1, device_id=other, device_id_type=MESH)

    staged[...] = jnp.zeros_like(staged)
    staged_f[...] = jnp.zeros_like(staged_f)
    for n in (0, 1, 2, 6, 7):
        fetches[n].wait()
    low_maps = [a_query[...].astype(F32), a_value[...].astype(F32), jnp.zeros((3, 112), F32)]
    staged[0, 0:3, 0:128] = jnp.concatenate(low_maps, axis=1).astype(BF16)
    for g in range(2):
        a, b = 640 * g, SIDE * g
        staged[0, 0:3, a + 128 : a + 512] = w_query[:, b : b + SIDE]
        staged[0, 0:3, a + 512 : a + 640] = w_key[:, b : b + 128]
        staged[1, 0:3, a : a + 256] = w_key[:, b + 128 : b + SIDE]
        staged[1, 0:3, a + 256 : a + 640] = w_value[:, b : b + SIDE]

    def stage_rest():
        for n in (3, 4, 5):
            fetches[n].wait()
        up, down = w_up[...].astype(F32), w_down[...].astype(F32)
        for c in range(2):
            staged[c, 0:3, STARTS[2] : STARTS[2] + SIDE] = w_out[:, SIDE * c : SIDE * c + SIDE]
            for half in range(2):
                for which, part in enumerate((up, down)):
                    lo = half * 1536 + which * D
                    staged_f[c, 0:3, lo : lo + D] = part[3 * half : 3 * half + 3, c * D : c * D + D].astype(BF16)

    lane = lax.broadcasted_iota(jnp.int32, (1, 128), 1)
    left = lane < 64

    def prepare():
        for n in range(8, 19):
            fetches[n].wait()
        zero_u = jnp.zeros((8, SIDE), F32)
        up_q, up_v = query_up[...].astype(F32) * 2.0, value_up[...].astype(F32) * 2.0
        top = [up_q[:, 0:SIDE], zero_u, up_q[:, SIDE:D], zero_u]
        bottom = [zero_u, up_v[:, 0:SIDE], zero_u, up_v[:, SIDE:D]]
        for n, ref in enumerate((vec_q, vec_v, vec_o, vec_down, gain_a, shift_a, gain_b, shift_b)):
            vec[n : n + 1, :] = ref[...].astype(F32).reshape(1, D)
        for n in range(4):
            vec[8 + n : 9 + n, :] = vec_up[n * D : n * D + D].astype(F32).reshape(1, D)
        umat[...] = jnp.concatenate(
            [jnp.concatenate(top, axis=1), jnp.concatenate(bottom, axis=1), jnp.zeros((112, 2 * D), F32)], axis=0
        ).astype(BF16)
        for item in range(2):
            position = lax.broadcasted_iota(jnp.int32, (SEQ, 128), 0)
            kb[item] = jnp.where(position < lengths[item], 0.0, -1e30).astype(BF16)

    if COMM:
        pl.semaphore_wait(barrier, len(greet))

    mine = slot_of(z, core)

    def z_copy(part, n):
        dz, dc = column[n]
        lo, width = Z_PARTS[part]
        return remote(
            staged.at[cores[dc], :, pl.ds(lo, width)], arrived.at[mine, :, pl.ds(lo, width)],
            z_send.at[part], z_recv.at[part], column_at[dz, dc],
        )

    def z_wait(part):
        if not COMM:
            return
        z_all(part).wait_recv()

    def z_all(part):
        lo, width = Z_PARTS[part]
        whole = arrived.at[pl.ds(0, 15), :, pl.ds(lo, width)]
        return remote(whole, whole, z_send.at[part], z_recv.at[part], partner)

    pair_at = lax.div(z, 2)
    ahead_z = (jnp.where(tp == 0, along_z[7][0], along_z[1][0]) + core, 1 - tp)
    pair_q = lax.rem(pair_at + jnp.where(tp == 0, 3, 1), 4)
    pair_p = lax.rem(pair_at + jnp.where(tp == 0, 1, 3), 4)
    pair_far = lax.rem(pair_at + 2, 4)

    def four(n):
        return arrived_f.at[pl.ds(pl.multiple_of(n * 4, 4), 4)]

    def two(zz):
        return arrived_f.at[pl.ds(pl.multiple_of(zz * 2, 2), 2)]

    def column_copy(n):
        if n == 0:
            src, dst = staged_f.at[1 - core], arrived_f.at[z * 2 + core]
        else:
            src = dst = (None, two(z), four(pair_at), four(pair_q), four(pair_p))[n]
        return remote(src, dst, f_send.at[n], f_recv.at[n], (sibling, partner, ahead_z, partner, ahead_z)[n])

    def column_send(n):
        if n == 0:
            arrived_f[pl.ds(z * 2 + core, 1)] = staged_f[pl.ds(core, 1)]
        send(column_copy(n))

    def column_take(n):
        far_z = z + 1 - 2 * tp
        dst = (arrived_f.at[z * 2 + 1 - core], two(far_z), four(pair_q), four(pair_p), four(pair_far))[n]
        if COMM:
            remote(dst, dst, f_send.at[n], f_recv.at[n], partner).wait_recv()

    def column_step(n):
        column_take(n - 1)
        column_send(n)

    groups = [(ref, width, pl.multiple_of(core * width, 128)) for ref, width in zip((wa0, wa1, wo, f0, f1), WIDTHS)]

    def region(g, uu, ww, part=None):
        ref, width, lo = groups[g]
        cut = (width // 128 + 1) // 2 * 128
        if part == 0:
            width = cut
        elif part == 1:
            lo, width = pl.multiple_of(lo + cut, 128), width - cut
        return ref.at[pl.ds(block_rows[uu][ww], BLOCK), pl.ds(lo, width)]

    steps = (0, 3, 1, 2)

    def xy(g, n, r, target):
        sem = n if n < 4 else (n - 4) // 4 * 2 + 3 + n % 4 // 2
        send(remote(r, r, xy_send.at[g], xy_recv.at[g, sem], target))

    def take(g, sem, blocks):
        if COMM:
            r = half_of(g, blocks * BLOCK)
            remote(r, r, xy_send.at[g], xy_recv.at[g, sem], partner).wait_recv()

    def to_sibling(g, j, i):
        r = region(g, steps[j], steps[i])
        send(remote(r, r, sib_send.at[g], sib_recv.at[g], sibling))

    def half_of(g, rows, other=False):
        ref, width, lo = groups[g]
        if other:
            lo = pl.multiple_of((1 - core) * width, 128)
        return ref.at[pl.ds(0, rows), pl.ds(lo, width)]

    def from_sibling(g):
        if COMM:
            r = half_of(g, D, True)
            remote(r, r, sib_send.at[g], sib_recv.at[g], partner).wait_recv()

    def all_sent(g):
        if COMM:
            r = half_of(g, 15 * BLOCK)
            remote(r, r, xy_send.at[g], xy_recv.at[g, 0], partner).wait_send()
            r = half_of(g, D)
            remote(r, r, sib_send.at[g], sib_recv.at[g], partner).wait_send()

    def line_send(g, base, uu, ww, ahead):
        r = region(g, uu, ww)
        xy(g, base, r, ahead(1))
        xy(g, base + 1, r, ahead(3))
        if DIRECT[g]:
            xy(g, base + 2, r, ahead(2))

    def along_u(h):
        return towards_u[h]

    def along_w(h):
        return towards_w[h]

    def first_send(g):
        r = region(g, 0, 0)
        for n, h in enumerate((1, 3, 2)[: 2 if g > 2 else 3]):
            xy(g, n, r, along_u(h))

    def second_send(g, j):
        line_send(g, 4 + 4 * j, steps[j], 0, along_w)
        to_sibling(g, j, 0)

    def second_forward(g, j):
        take(g, 2 * j + 3, 2)
        if not DIRECT[g]:
            xy(g, 6 + 4 * j, region(g, steps[j], 3, 0), along_w(1))
            xy(g, 7 + 4 * j, region(g, steps[j], 1, 1), along_w(3))
        to_sibling(g, j, 1)
        to_sibling(g, j, 2)

    def second_finish(g, j):
        take(g, 2 * j + 4, 1)
        to_sibling(g, j, 3)

    def begin(g):
        first_send(g)
        second_send(g, 0)

    def widen(g, js=(1, 2, 3)):
        for j in js:
            take(g, j - 1, 1)
            if g > 2 and j < 3:
                xy(g, 2, region(g, steps[j], 0, j - 1), along_u(steps[3 - j]))
            second_send(g, j)

    def relay(g, js=(0, 1, 2, 3)):
        for j in js:
            second_forward(g, j)

    def finish(g, js=(0, 1, 2, 3)):
        for j in js:
            second_finish(g, j)

    here = pl.ds(block_rows[0][0], BLOCK)

    def assemble(g):
        ref, width, lo = groups[g]
        for s in range(16):
            if g < 3:
                packed[3 * s : 3 * s + 3, 0:width] = arrived[s, 0:3, STARTS[g] : STARTS[g] + width].astype(F32)
            elif s // 2 % 2 == g - 3:
                for half in range(2):
                    row, src = (s // 4 * 2 + s % 2) * 6 + half * 3, half * 1536
                    packed[row : row + 3, :] = arrived_f[s, 0:3, src : src + 1536].astype(F32)
        ref[here, pl.ds(lo, width)] = packed[:, 0:width].astype(BF16)


    def row(n):
        return vec[n : n + 1, :]

    def project(g):
        wa = (wa0, wa1)[g]
        side = slice(SIDE * g, SIDE * g + SIDE)
        for half in range(2):
            r = slice(HALF * half, HALF * half + HALF)
            got = dot(x[r, :], wa[...])
            if g == 0:
                low[r, :] = got[:, 0:128].astype(BF16)
            more = dot(low[r, :], umat[:, D * g : D * g + D])
            q[r, side] = ((got[:, 128:512] + more[:, 0:SIDE] + row(0)[:, side]) * 0.125).astype(BF16)
            k[r, side] = got[:, 512:896].astype(BF16)
            v[r, side] = (got[:, 896:1280] + more[:, SIDE:D] + row(1)[:, side]).astype(BF16)

    def merge():
        for g, wa in enumerate((wa0, wa1)):
            more = dot(wa0[:, 0:128], umat[:, D * g : D * g + D])
            side = SIDE * g
            mkv[:, side : side + SIDE] = (wa[:, 128:512].astype(F32) + more[:, 0:SIDE]).astype(BF16)
            mkv[:, D + side : D + side + SIDE] = wa[:, 512:896]
            mkv[:, 2 * D + side : 2 * D + side + SIDE] = (wa[:, 896:1280].astype(F32) + more[:, SIDE:D]).astype(BF16)

    def project_eval(item):
        for half in range(2):
            r = slice(HALF * half, HALF * half + HALF)
            got = dot(xe[item, r, :], mkv[:, D : 3 * D])
            kv[r, 0:D] = got[:, 0:D].astype(BF16)
            kv[r, D : 2 * D] = (got[:, D:] + row(1)).astype(BF16)
        own = dot(xe[item, mine_rows, :], mkv[:, 0:D])
        qe[HALF * item : HALF * item + HALF, :] = ((own + row(0)) * 0.125).astype(BF16)

    def heads(k2, q2, bias):
        for h in range(2):
            keep = left if h == 0 else lane >= 64
            spare = lane == (64 if h == 0 else 0)
            kh = jnp.where(keep, k2, jnp.where(spare, bias, jnp.zeros_like(bias)))
            yield h, kh, jnp.where(spare, jnp.ones_like(q2), q2)

    def softmax(s_ref, queries, e_ref, inverse):
        for c in range(0, queries, 256):
            s = s_ref[:, c : c + 256]
            e = jnp.exp(s - jnp.max(s, axis=0, keepdims=True))
            inverse[:, c : c + 256] = 1.0 / jnp.sum(e, axis=0, keepdims=True)
            e_ref[:, c : c + 256] = e.astype(BF16)

    def attend(lo, hi):
        def pair(p, carry):
            s = pl.ds(pl.multiple_of(p * 128, 128), 128)
            v2t = jnp.transpose(v[:, s])
            for h, kh, qh in heads(k[:, s], q[:, s], kb[tp]):
                scores[h] = dot_nt(kh, qh)
            for h in range(2):
                n = 2 * p + h
                softmax(scores.at[h], SEQ, expo.at[n], inv.at[n])
                o = dot(v2t[64 * h : 64 * h + 64, :], expo[n]) * inv[n]
                mix_t[pl.ds(pl.multiple_of(p * 128 + 64 * h, 64), 64), :] = o.astype(BF16)
            return carry

        lax.fori_loop(lo, hi, pair, 0)

    def attend_eval(item, lo, hi):
        own = slice(HALF * item, HALF * item + HALF)

        def pairs_of(step, carry):
            turned = []
            for i in range(2):
                p = 2 * step + i
                s = pl.ds(pl.multiple_of(p * 128, 128), 128)
                ks = s
                vs = pl.ds(pl.multiple_of(D + p * 128, 128), 128)
                turned.append(jnp.transpose(kv[:, vs]))
                for h, kh, qh in heads(kv[:, ks], qe[own, s], kb[item]):
                    scores[i, :, HALF * h : HALF * h + HALF] = dot_nt(kh, qh)
            for i in range(2):
                p = 2 * step + i
                for h in range(2):
                    n = 2 * i + h
                    softmax(scores.at[i, :, pl.ds(HALF * h, HALF)], HALF, expo_e.at[n], inv_e.at[n])
                    o = dot(turned[i][64 * h : 64 * h + 64, :], expo_e[n]) * inv_e[n]
                    mixe_t[pl.ds(pl.multiple_of(p * 128 + 64 * h, 64), 64), own] = o.astype(BF16)
            return carry

        lax.fori_loop(lo, hi, pairs_of, 0)

    def mean(a):
        return jnp.sum(a, axis=-1, keepdims=True) * (1.0 / D)

    def normalise(a):
        centred = a - mean(a)
        scale = lax.rsqrt(mean(centred * centred) + EPSILON)
        return centred * scale, scale

    def first_norm(mixed, base, total, low_ref, keep):
        total[...] = dot_tn(mixed[...], wo[...])

        def body(r, at_row):
            xhat, scale = normalise(total[r, :] + base(at_row).astype(F32) + row(2))
            if keep:
                xh1[r, :] = xhat
                rs1[r, :] = scale
            normed = xhat * row(4) + row(5)
            low_ref[r, :] = normed.astype(BF16)
            total[r, :] = normed + row(3)

        by_rows(SEQ, body)

    def feed(part, low_ref, total, keep, between=None):
        f = (f0, f1)[part]

        def down(order, c, r):
            columns = pl.ds(pl.multiple_of(1536 * c + D, 128), D)
            total[r, :] += dot_nt(hidden[order, r, :], f[:, columns])

        ready = None
        for order, c in enumerate(cores):
            n = 2 * part + c
            if order and between:
                between()
            for half in range(2):
                r = slice(HALF * half, HALF * half + HALF)
                pre = dot(low_ref[r, :], f[:, pl.ds(pl.multiple_of(1536 * c, 128), D)]) + vec[pl.ds(8 + n, 1), :]
                if ready:
                    down(*ready)
                phi = 0.5 + 0.5 * lax.erf(pre * 0.7071067811865476)
                hidden[order, r, :] = (pre * phi).astype(BF16)
                if keep:
                    slope = phi + pre * (0.3989422804014327 * jnp.exp(pre * pre * -0.5))
                    gates[r, pl.ds(pl.multiple_of(D * n, 128), D)] = slope.astype(BF16)
                ready = (order, c, r)
        down(*ready)

    def feed_back():
        def up(n, r):
            f, c = (f0, f1)[n // 2], n % 2
            acc[r, :] += dot_nt(hidden[c, r, :], f[:, 1536 * c : 1536 * c + D])

        ready = None
        for n in range(4):
            f, c = (f0, f1)[n // 2], n % 2
            for half in range(2):
                r = slice(HALF * half, HALF * half + HALF)
                g = dot(norm_low[r, :], f[:, 1536 * c + D : 1536 * c + 2 * D])
                if ready:
                    up(*ready)
                hidden[c, r, :] = (g * gates[r, D * n : D * n + D].astype(F32)).astype(BF16)
                ready = (n, r)
        up(*ready)

    def second_norm(total, out, backward):
        def body(r, at_row):
            xhat, scale = normalise(total[r, :])
            out(at_row, (xhat * row(6) + row(7)).astype(BF16))
            if backward:
                position = lax.broadcasted_iota(jnp.int32, (ROWS, 1), 0) + at_row
                c = jnp.where(position < lengths[tp], cot[r, :].astype(F32), 0.0) * row(6)
                g = (c - mean(c) - xhat * mean(c * xhat)) * scale
                total[r, :] = g
                norm_low[r, :] = g.astype(BF16)

        by_rows(SEQ, body)

    def first_norm_back():
        def body(r, at_row):
            c = acc[r, :] * row(4)
            xhat = xh1[r, :]
            g = (c - mean(c) - xhat * mean(c * xhat)) * rs1[r, :]
            acc[r, :] = g
            norm_low[r, :] = g.astype(BF16)

        by_rows(SEQ, body)
        g = dot_nt(wo[...], norm_low[...])
        for n in range(12):
            mix_t[64 * n : 64 * n + 64, :] = (g[64 * n : 64 * n + 64, :] * inv[n]).astype(BF16)

    def attend_back():
        def triple(step, carry):
            jobs = [(i, h) for i in range(3) for h in range(2)]
            parts = {}

            def lanes(i, section):
                return pl.ds(pl.multiple_of(D * section + (3 * step + i) * 128, 128), 128)

            def load(i):
                if i not in parts:
                    s = lanes(i, 0)
                    g2t = mix_t[pl.ds(pl.multiple_of((3 * step + i) * 128, 128), 128), :]
                    parts[i] = (jnp.transpose(k[:, s]), q[:, s], v[:, s], g2t, [], [], [])
                return parts[i]

            def raw(m):
                i, h = jobs[m]
                v2, g2t = load(i)[2:4]
                scores[m % 2] = dot(jnp.where(left if h == 0 else lane >= 64, v2, jnp.zeros_like(v2)), g2t)

            def middle(m):
                i, h = jobs[m]
                n = 2 * (3 * step + i) + h
                load(i)[6].append(dot_nt(expo[n], load(i)[3]))
                for c in range(0, SEQ, 256):
                    e = expo[n, :, c : c + 256].astype(F32)
                    g = scores[m % 2, :, c : c + 256]
                    inner = jnp.sum(e * g, axis=0, keepdims=True) * inv[n, :, c : c + 256]
                    ds[m % 2, :, c : c + 256] = (e * (g - inner)).astype(BF16)

            def last(m):
                i, h = jobs[m]
                k2t, q2, _, _, dq, dk, dv = load(i)
                dq.append(dot(k2t[64 * h : 64 * h + 64, :], ds[m % 2]))
                dk.append(dot(ds[m % 2], q2))
                if h == 1:
                    dqkv[:, lanes(i, 0)] = (jnp.transpose(jnp.concatenate(dq, axis=0)) * 0.125).astype(BF16)
                    dqkv[:, lanes(i, 1)] = jnp.where(left, dk[0], dk[1]).astype(BF16)
                    dqkv[:, lanes(i, 2)] = jnp.where(left, dv[0], dv[1]).astype(BF16)

            raw(0)
            for m in range(6):
                if m < 5:
                    raw(m + 1)
                middle(m)
                if m:
                    last(m - 1)
            last(5)
            return carry

        lax.fori_loop(0, 2, triple, 0)

    def adapter_grads():
        red[0:8, :] = dot_tn(low[...], dqkv[:, 0:D])[0:8, :] * 2.0
        red[8:16, :] = dot_tn(low[...], dqkv[:, 2 * D :])[8:16, :] * 2.0

    def input_grads(r):
        return acc[r, :] + dot_nt(dqkv[r, :], mkv[...])


    along_x = [(jnp.where(first, a[0], b[0]), tp) for a, b in zip(towards_u, towards_w)]
    along_y = [(jnp.where(first, b[0], a[0]), tp) for a, b in zip(towards_u, towards_w)]

    half_row = pl.ds(pl.multiple_of(core * 8, 8), 8)

    def exchange(n, src, dst, target):
        send(remote(src, dst, red_send.at[0], red_recv.at[n], target))

    def expect(n, dst):
        if COMM:
            remote(dst, dst, red_send.at[0], red_recv.at[n], partner).wait_recv()

    def line_total(n, buffer, count):
        expect(n, buffer.at[pl.ds(0, count - 1)])
        total = buffer[0]
        for h in range(1, count):
            total = total + buffer[h]
        return total


    start = pl.multiple_of(tp * HALF, HALF)
    pairs = [
        remote(tokens.at[1 - tp, 0:128], x.at[pl.ds(start, 128)], pair_send.at[0], pair_recv.at[0], partner),
        remote(eval_tokens.at[0], xe.at[0, mine_rows], pair_send.at[1], pair_recv.at[1], partner),
        remote(eval_tokens.at[1], xe.at[1, mine_rows], pair_send.at[2], pair_recv.at[2], partner),
        remote(cotangent.at[1 - tp], cot.at[mine_rows], pair_send.at[3], pair_recv.at[3], partner),
        remote(y_low.at[other_rows], act_out.at[tp], pair_send.at[4], pair_recv.at[4], partner),
        remote(ig_send, ig_recv, pair_send.at[5], pair_recv.at[5], partner),
        remote(tokens.at[1 - tp, 128:HALF], x.at[pl.ds(start + 128, 128)], pair_send.at[6], pair_recv.at[6], partner),
    ]

    def pair_start(n):
        if COMM:
            pairs[n].start()

    def pair_wait(n):
        if COMM:
            pairs[n].wait_recv()

    own = [
        pltpu.make_async_copy(tokens.at[tp], x.at[mine_rows], local_sem.at[0]),
        pltpu.make_async_copy(eval_tokens, xe.at[:, mine_rows], local_sem.at[1]),
        pltpu.make_async_copy(cotangent.at[tp], cot.at[mine_rows], local_sem.at[2]),
    ]
    for c in own:
        c.start()

    def eval_rows(at_row):
        item = lax.div(at_row, HALF)
        start = pl.multiple_of(lax.rem(at_row, HALF) + tp * HALF, ROWS)
        return xe[item, pl.ds(start, ROWS), :]

    def z_start(part):
        for n in range(15):
            send(z_copy(part, n))

    z_start(0)
    stage_rest()
    column_send(0)
    arrived[pl.ds(mine, 1)] = staged[pl.ds(core, 1)]
    z_start(1)
    prepare()
    column_step(1)
    z_wait(0)
    assemble(0)
    begin(0)
    pair_start(0)
    column_step(2)
    z_wait(1)
    assemble(1)
    assemble(2)
    widen(0)
    begin(1)
    column_step(3)
    pair_start(6)
    pair_start(1)
    pair_start(2)
    pair_start(3)
    relay(0)
    widen(1)
    finish(0)
    relay(1, (0,))
    begin(2)
    column_step(4)
    from_sibling(0)
    pair_wait(0)
    pair_wait(6)
    own[0].wait()
    project(0)
    relay(1, (1, 2, 3))
    widen(2)
    column_take(4)
    assemble(3)
    begin(3)
    attend(0, 1)
    attend(1, 2)
    finish(1)
    relay(2)
    widen(3, (1, 2))
    assemble(4)
    begin(4)
    attend(2, 3)
    from_sibling(1)
    project(1)
    widen(3, (3,))
    finish(2)
    attend(3, 4)
    relay(3, (0,))
    attend(4, 5)
    widen(4, (1, 2))
    attend(5, 6)
    relay(3, (1,))
    merge()
    from_sibling(2)
    first_norm(mix_t, lambda at_row: x[pl.ds(pl.multiple_of(at_row, ROWS), ROWS), :], acc, norm_low, True)
    relay(3, (2, 3))
    widen(4, (3,))
    pair_wait(1)
    own[1].wait()
    project_eval(0)
    relay(4, (0, 1))
    finish(3, (0, 1))
    attend_eval(0, 0, 2)
    relay(4, (2,))
    finish(3, (2, 3))
    attend_eval(0, 2, 3)
    relay(4, (3,))

    def rest_of_groups():
        from_sibling(3)
        finish(4)

    pair_wait(2)
    project_eval(1)
    feed(0, norm_low, acc, True, rest_of_groups)
    feed(1, norm_low, acc, True, lambda: from_sibling(4))
    pair_wait(3)
    own[2].wait()
    second_norm(acc, lambda at_row, value: y_low.__setitem__((pl.ds(at_row, ROWS), slice(None)), value), True)
    pair_start(4)
    act_out[pl.ds(tp, 1)] = y_low[mine_rows, :][None]
    feed_back()
    first_norm_back()
    attend_back()
    adapter_grads()
    exchange(0, red.at[pl.ds(pl.multiple_of((1 - core) * 8, 8), 8)], red_sib, sibling)
    ig_send[...] = input_grads(other_rows).astype(BF16)
    pair_start(5)
    expect(0, red_sib)
    red_sum[0] = red[half_row, :] + red_sib[...]
    if COMM:
        red_x[px] = red_sum[0]
        for target in along_x[1:]:
            exchange(1, red_sum.at[0], red_x.at[px], target)
    grad_out[pl.ds(tp, 1)] = input_grads(mine_rows)[None]

    if COMM:
        red_sum[1] = line_total(1, red_x, 4)
        red_y[py] = red_sum[1]
        for target in along_y[1:]:
            exchange(2, red_sum.at[1], red_y.at[py], target)
    attend_eval(1, 0, 3)
    if COMM:
        red_sum[2] = line_total(2, red_y, 4)
        red_z[z] = red_sum[2]
        for h in range(1, 8):
            exchange(3, red_sum.at[2], red_z.at[z], column_at[h, 0])
    first_norm(mixe_t, eval_rows, acc_e, norm_e, False)
    feed(0, norm_e, acc_e, False)
    feed(1, norm_e, acc_e, False)
    pair_wait(5)
    grad_out[pl.ds(1 - tp, 1)] = ig_recv[...].astype(F32)[None]
    if COMM:
        red_all[half_row, :] = line_total(3, red_z, 8)
        exchange(4, red_all.at[half_row], red_all.at[half_row], sibling)
    second_norm(acc_e, lambda at_row, value: eval_out.__setitem__(pl.ds(lax.div(at_row, HALF), 1), value[None]), False)
    if COMM:
        expect(4, red_all.at[pl.ds(pl.multiple_of((1 - core) * 8, 8), 8)])
    adapter_q[...] = red_all[0:8, :]
    adapter_v[...] = red_all[8:16, :]
    pair_wait(4)
    if COMM:
        for c in pairs:
            c.wait_send()
        for part in range(2):
            z_all(part).wait_send()
        for n in range(5):
            column_copy(n).wait_send()
            all_sent(n)
        everything = acc_e.at[pl.ds(0, 15 * 8)]
        remote(everything, everything, red_send.at[0], red_recv.at[0], partner).wait_send()


def scratches():
    vm, dma = pltpu.VMEM, pltpu.SemaphoreType.DMA
    return [
        *(vm(shape, BF16) for shape in SMALL),
        vm((2, 4, STAGED), BF16), vm((2, 4, FF), BF16), vm((12, D), F32),
        vm((16, 4, STAGED), BF16), vm((16, 4, FF), BF16), vm((BLOCK, 1536), F32),
        vm((D, 1280), BF16), vm((D, 1280), BF16), vm((D, D), BF16), vm((D, FF), BF16), vm((D, FF), BF16),
        vm((D, 3 * D), BF16), vm((128, 2 * D), BF16),
        vm((SEQ, D), BF16), vm((2, SEQ, D), BF16), vm((SEQ, D), BF16), vm((SEQ, 128), BF16), vm((2, SEQ, 128), BF16),
        vm((SEQ, D), BF16), vm((SEQ, D), BF16), vm((SEQ, D), BF16), vm((D, SEQ), BF16),
        vm((12, SEQ, SEQ), BF16), vm((12, 1, SEQ), F32), vm((2, SEQ, SEQ), F32), vm((2, SEQ, SEQ), BF16),
        vm((SEQ, FF), BF16), vm((2, SEQ, D), BF16), vm((SEQ, D), F32), vm((SEQ, 1), F32),
        vm((SEQ, D), BF16), vm((SEQ, D), F32), vm((SEQ, D), BF16), vm((SEQ, 3 * D), BF16),
        vm((SEQ, 2 * D), BF16), vm((SEQ, D), BF16), vm((D, SEQ), BF16), vm((4, SEQ, HALF), BF16), vm((4, 1, HALF), F32),
        vm((SEQ, D), BF16), vm((SEQ, D), F32), vm((HALF, D), BF16), vm((HALF, D), BF16),
        vm((16, D), F32), vm((8, D), F32), vm((4, 8, D), F32), vm((4, 8, D), F32), vm((8, 8, D), F32),
        vm((3, 8, D), F32), vm((16, D), F32),
        dma((2,)), dma((2,)), dma((5,)), dma((5,)), dma((19,)), dma((5,)), dma((5, 11)), dma((5,)), dma((5,)),
        dma((7,)), dma((7,)), dma((10,)), dma((1,)), dma((5,)),
    ]


def layer(*operands):
    shapes = ((2, HALF, D), BF16), ((2, HALF, D), F32), ((2, HALF, D), BF16), ((8, D), F32), ((8, D), F32)
    out = tuple(pltpu.VMEM(*shape) for shape in shapes)
    hbm, vmem = pl.BlockSpec(memory_space=pl.ANY), pl.BlockSpec(memory_space=pltpu.VMEM)
    params = dict(collective_id=0) if COMM else {}
    return pl.pallas_call(
        layer_kernel,
        out_shape=out,
        in_specs=[pl.BlockSpec(memory_space=pltpu.SMEM)] + [hbm] * 22,
        out_specs=[vmem] * 5,
        scratch_shapes=scratches(),
        compiler_params=pltpu.CompilerParams(has_side_effects=True, vmem_limit_bytes=LIMIT << 20, **params),
    )(*operands)


def shards(tokens, eval_tokens, cotangent, lengths, *rest):
    rest = (*rest[0:5], rest[5].T, *rest[6:])
    frozen, ups, (query_bias, value_bias, bias_out, bias_up, bias_down, *norms) = rest[0:8], rest[8:10], rest[10:]
    vectors = (query_bias, value_bias, bias_out, bias_down, *norms, bias_up)
    activations, input_grad, evaluated, grad_q, grad_v = layer(
        lengths, *frozen, *ups, *vectors, tokens, eval_tokens, cotangent
    )
    return activations, input_grad, grad_q, grad_v, evaluated


def solution(mesh):
    rows, frozen, whole = P("dp", "tp", None), P(("dp", "tp"), None), P()
    in_specs = (rows, rows, rows, P("dp"), frozen, frozen, frozen, frozen, P("dp", "tp"), P("tp", "dp"), frozen, frozen)
    in_specs += (whole,) * 11
    out_specs = (rows, rows, whole, whole, rows)
    return jax.shard_map(shards, mesh=mesh, in_specs=in_specs, out_specs=out_specs, check_vma=False)
```
